32 devices in a mesh: dp: 2 (over y), expert: 16 (over z, x, core).
Axes of the slice: x: 2, y: 2, z: 4, core: 2. Of those that a mesh axis runs over, the one named last changes fastest.
Arguments:
- tokens: bfloat16 [1024, 2048], P(('dp', 'expert')), may hold values from -6 to 6
- cotangent: bfloat16 [1024, 2048], P(('dp', 'expert')), may hold values from -0.29882812 to 0.29882812
- routes: int32 [1024, 8], P(('dp', 'expert')), may hold values from 0 to 15, all different within a row; in each aligned block of 32 rows (0 to 31, 32 to 63, ...) at most 32 rows name the same one
- combine: float32 [1024, 8], P(('dp', 'expert')), may hold values from 0.05 to 0.5
- w_in: bfloat16 [16, 2, 512, 2048], P('expert', None, 'dp'), may hold values from -0.125 to 0.125
- w_out: bfloat16 [16, 512, 2048], P('expert', 'dp'), may hold values from -0.25 to 0.25
- v_in: bfloat16 [16, 2, 512, 2048], P('expert', None, 'dp'), may hold values from -0.125 to 0.125
Outputs:
- hvp: float32 [16, 2, 512, 2048], P('expert', None, 'dp')
The draws below stay inside these ranges and needn't reach their ends.
Inputs may be any that keep to these rules, and one draw needn't show every extreme that they name: `routes`: each token names 8 different experts. Among the tokens of one device no expert is named more than 32 times, and on some device an expert is named exactly 32 times.
All inputs are finite; a program needn't handle non-finite values.
Results may differ from the reference program's by a relative error of at most 0.015.
Values may be sent and summed in bfloat16 or wider, within the bound.
No kernel may reach another device: no remote copies, remote signals or barrier semaphores. Data moves between devices by JAX's collectives and lax.ppermute only.
A program may use at most 128 MiB of HBM per device.

```python
import math
import jax
import jax.numpy as jnp
import numpy as np
from jax import lax

D = 2048
TOP = 8
FF_W = 512
TOK_DEV = 32
EXPERTS = 16
TOKENS = 1024
CAP = 32
N_DP = 2
N_EXPERT = 16


def steps_of(rng, dims, shards, smallest, top_value):
    level = 1.0
    for dim, blocks in shards:
        steps = jax.random.uniform(jax.random.fold_in(jax.random.fold_in(rng, 6), dim), (blocks,), jnp.float32, smallest / len(shards), top_value / len(shards))
        level = level * jnp.repeat(jnp.exp(steps), dims[dim] // blocks).reshape((-1,) + (1,) * (len(dims) - 1 - dim))
    return level


def deal_out(key, own, number, rows, count, top, bound, slope):
    order = jax.random.permutation(key, count)
    crowded, common = shares(count, rows * top, bound, slope, True), shares(count, rows * top, bound, slope, False)
    places = jnp.arange(count)

    def named(sizes, offset_by):
        used = int((sizes > 0).sum())
        fixed = max(1, used // 4)
        moved = fixed + (places - fixed + offset_by * (used - fixed)) % max(1, count - fixed)
        return jnp.zeros((count,), jnp.int32).at[order[jnp.where(places < fixed, places, moved)]].set(jnp.asarray(sizes, jnp.int32))

    sizes = jnp.where(number % 4 == 0, named(crowded, number // 4), named(common, number - number // 4 - 1))
    mixed = jax.random.permutation(jax.random.fold_in(own, 3), count)
    giver, taker = mixed[0:count // 2 * 2:2], mixed[1:count // 2 * 2:2]
    room = jnp.minimum(sizes[giver] - 1, bound - sizes[taker]) // 2
    room = jnp.where((giver == order[0]) | (taker == order[0]) | (sizes[taker] == 0), 0, jnp.maximum(room, 0))
    moved = jax.random.randint(jax.random.fold_in(own, 4), (count // 2,), 0, 1 << 20) % (room + 1)
    sizes = sizes.at[giver].add(-moved).at[taker].add(moved)
    members = jnp.searchsorted(jnp.cumsum(sizes), jnp.arange(rows * top), side="right").astype(jnp.int32)
    listing = members.reshape(top, rows).T
    listing = listing[jax.random.permutation(jax.random.fold_in(own, 1), rows)]
    offset_by = jax.random.randint(jax.random.fold_in(own, 2), (rows, 1), 0, top)
    return jnp.take_along_axis(listing, (jnp.arange(top)[None, :] + offset_by) % top, axis=1)


def shares(amount, total, reach, skew, full):
    portions = [(1 << 20) // math.isqrt(rank ** skew) + 1 for rank in range(1, amount + 1)]
    largest = reach if full else min(reach, max(-(-total // amount), total * portions[0] // sum(portions)))
    least = 1 if total - largest >= amount - 1 else 0
    counts, surplus = [largest] + [least] * (amount - 1), total - largest - least * (amount - 1)
    while surplus > 0:
        movable = [i for i in range(1, amount) if counts[i] < largest] or [i for i in range(1, amount) if counts[i] < reach]
        whole, budget = sum([portions[i] for i in movable]), surplus
        for i in movable:
            addition = min(reach - counts[i], max(1, budget * portions[i] // whole), surplus)
            counts[i] = counts[i] + addition
            surplus = surplus - addition
    return np.array(counts)


def noise(rng, shape, width, most, cuts=(), kind=jnp.bfloat16):
    loudness = steps_of(rng, shape, cuts, -0.22, 0.18) if cuts else 1.0
    values = jax.random.normal(rng, shape, jnp.float32) * width * loudness
    return jnp.minimum(jnp.maximum(values, -most), most).astype(kind)


def setup_inputs(seed: int = 0) -> dict:
    streams_of = jax.random.split(jax.random.key(seed), 8)
    tokens = noise(streams_of[0], (TOKENS, D), 1.0, 6.0, ((0, 32),))
    cotangent = noise(streams_of[1], (TOKENS, D), 0.05, 0.29882812, ((0, 32),))
    routes_keys = jax.random.split(jax.random.fold_in(streams_of[2], 1), TOKENS // TOK_DEV)
    routes_turns = jax.random.permutation(jax.random.fold_in(streams_of[2], 3), TOKENS // TOK_DEV)
    routes = jax.vmap(lambda own, number: deal_out(jax.random.fold_in(streams_of[2], 2), own, number, TOK_DEV, EXPERTS, TOP, CAP, 2))(routes_keys, routes_turns).reshape((TOKENS, TOP))
    combine = jnp.clip(jnp.exp(math.log(0.5) - 2.3025851 * jax.random.uniform(streams_of[3], (TOKENS, TOP), jnp.float32) ** steps_of(streams_of[3], (TOKENS, TOP), ((0, 32),), -0.2, 0.2)), 0.05, 0.5)
    w_in = noise(streams_of[4], (EXPERTS, 2, FF_W, D), D ** -0.5, 0.125, ((0, 16), (2, 2)))
    w_out = noise(streams_of[5], (EXPERTS, FF_W, D), FF_W ** -0.5, 0.25, ((0, 16), (1, 2)))
    v_in = noise(streams_of[6], (EXPERTS, 2, FF_W, D), D ** -0.5, 0.125, ((0, 16), (2, 2)))
    return {"tokens": tokens, "cotangent": cotangent, "routes": routes, "combine": combine, "w_in": w_in, "w_out": w_out, "v_in": v_in}


def expert_terms(slot_rows, slot_grads, w_pair, v_pair, w_down):
    hidden_width = w_pair.shape[1]
    model_dim = w_pair.shape[2]
    stacked = jnp.concatenate([w_pair, v_pair], axis=0).reshape(4 * hidden_width, model_dim)
    projected = lax.dot_general(slot_rows, stacked, (((1,), (1,)), ((), ())), preferred_element_type=jnp.float32)
    pre_gate = projected[:, :hidden_width]
    pre_up = projected[:, hidden_width:2 * hidden_width]
    tan_gate = projected[:, 2 * hidden_width:3 * hidden_width]
    tan_up = projected[:, 3 * hidden_width:]
    back_grad = lax.dot_general(slot_grads, w_down, (((1,), (1,)), ((), ())), preferred_element_type=jnp.float32)
    gate_sig = jax.nn.sigmoid(pre_gate)
    first_deriv = gate_sig * (1.0 + pre_gate * (1.0 - gate_sig))
    second_deriv = gate_sig * (1.0 - gate_sig) * (2.0 + pre_gate * (1.0 - 2.0 * gate_sig))
    gate_dir = (back_grad * (tan_up * first_deriv + pre_up * second_deriv * tan_gate)).astype(jnp.bfloat16)
    up_dir = (back_grad * first_deriv * tan_gate).astype(jnp.bfloat16)
    gate_term = lax.dot_general(gate_dir, slot_rows, (((0,), (0,)), ((), ())), preferred_element_type=jnp.float32)
    up_term = lax.dot_general(up_dir, slot_rows, (((0,), (0,)), ((), ())), preferred_element_type=jnp.float32)
    return jnp.stack([gate_term, up_term], axis=0)


def reference(tokens, cotangent, routes, combine, w_in, w_out, v_in):
    pair_count = TOK_DEV * TOP
    per_group = N_EXPERT * TOK_DEV
    slot_count = N_EXPERT * CAP
    grouped = routes.reshape(N_DP, N_EXPERT, pair_count)
    onehot = (grouped[..., None] == jnp.arange(EXPERTS, dtype=jnp.int32)).astype(jnp.int32)
    earlier = jnp.cumsum(onehot, axis=2) - onehot
    slot_rank = jnp.sum(earlier * onehot, axis=3)
    source = jnp.arange(N_EXPERT, dtype=jnp.int32)[None, :, None]
    position = (grouped * slot_count + source * CAP + slot_rank).astype(jnp.int32)
    pair_id = jnp.broadcast_to(source * pair_count + jnp.arange(pair_count, dtype=jnp.int32)[None, None, :], position.shape).astype(jnp.int32)
    group_id = jnp.broadcast_to(jnp.arange(N_DP, dtype=jnp.int32)[:, None, None], position.shape)
    slot_table = jnp.full((N_DP, EXPERTS * slot_count), per_group * TOP, jnp.int32)
    slot_table = slot_table.at[group_id, position].set(pair_id)
    slot_table = slot_table.reshape(N_DP, EXPERTS, slot_count)
    tok_pad = jnp.concatenate([tokens.reshape(N_DP, per_group, D), jnp.zeros((N_DP, 1, D), tokens.dtype)], axis=1)
    cot_pad = jnp.concatenate([cotangent.reshape(N_DP, per_group, D), jnp.zeros((N_DP, 1, D), cotangent.dtype)], axis=1)
    comb_pad = jnp.concatenate([combine.reshape(N_DP, per_group, TOP), jnp.zeros((N_DP, 1, TOP), combine.dtype)], axis=1)

    def one_expert(expert):
        def one_group(running_sum, group):
            entries = slot_table[group, expert]
            token_index = entries // TOP
            choice_index = entries % TOP
            slot_rows = tok_pad[group][token_index]
            weight_col = comb_pad[group][token_index, choice_index]
            slot_grads = (weight_col[:, None] * cot_pad[group][token_index].astype(jnp.float32)).astype(jnp.bfloat16)
            partial_value = expert_terms(slot_rows, slot_grads, w_in[expert], v_in[expert], w_out[expert])
            rounded = lax.optimization_barrier(partial_value.astype(jnp.bfloat16))
            return running_sum + rounded.astype(jnp.float32), None

        zero_start = jnp.zeros((2, FF_W, D), jnp.float32)
        result, _ = lax.scan(one_group, zero_start, jnp.arange(N_DP, dtype=jnp.int32))
        return result

    return lax.map(one_expert, jnp.arange(EXPERTS, dtype=jnp.int32))
```

```python
import jax
import jax.numpy as jnp
from jax import lax
from jax.experimental import pallas as pl
from jax.experimental.pallas import tpu as pltpu
from jax.sharding import PartitionSpec as P

NT = (((1,), (1,)), ((), ()))
NN = (((1,), (0,)), ((), ()))


def expert_terms(slot_rows, slot_grads, w_pair, v_pair, w_down):
    hidden_width = w_pair.shape[1]
    model_dim = w_pair.shape[2]
    stacked = jnp.concatenate([w_pair, v_pair], axis=0).reshape(4 * hidden_width, model_dim)
    projected = lax.dot_general(slot_rows, stacked, NT, preferred_element_type=jnp.float32)
    pre_gate = projected[:, :hidden_width]
    pre_up = projected[:, hidden_width : 2 * hidden_width]
    tan_gate = projected[:, 2 * hidden_width : 3 * hidden_width]
    tan_up = projected[:, 3 * hidden_width :]
    back_grad = lax.dot_general(slot_grads, w_down, NT, preferred_element_type=jnp.float32)
    gate_dir, up_dir = directions(pre_gate, pre_up, tan_gate, tan_up, back_grad)
    gate_term = lax.dot_general(
        gate_dir, slot_rows, (((0,), (0,)), ((), ())), preferred_element_type=jnp.float32
    )
    up_term = lax.dot_general(
        up_dir, slot_rows, (((0,), (0,)), ((), ())), preferred_element_type=jnp.float32
    )
    return jnp.stack([gate_term, up_term], axis=0)


def directions(pre_gate, pre_up, tan_gate, tan_up, back_grad):
    gate_sig = jax.nn.sigmoid(pre_gate)
    first_deriv = gate_sig * (1.0 + pre_gate * (1.0 - gate_sig))
    second_deriv = gate_sig * (1.0 - gate_sig) * (2.0 + pre_gate * (1.0 - 2.0 * gate_sig))
    gate_dir = back_grad * (tan_up * first_deriv + pre_up * second_deriv * tan_gate)
    up_dir = back_grad * first_deriv * tan_gate
    return gate_dir.astype(jnp.bfloat16), up_dir.astype(jnp.bfloat16)


def dispatched(tokens, cotangent, routes, combine, w_in, w_out, v_in):
    n_expert = lax.axis_size("expert")
    exp_dev = w_in.shape[0]
    experts = n_expert * exp_dev
    tok_dev, top_k = routes.shape
    model_dim = tokens.shape[1]
    capacity = 2 * tok_dev * top_k // experts
    pair_count = tok_dev * top_k
    slot_count = n_expert * capacity
    flat_routes = routes.reshape(pair_count)
    onehot = (flat_routes[:, None] == jnp.arange(experts, dtype=jnp.int32)[None, :]).astype(
        jnp.int32
    )
    earlier = jnp.cumsum(onehot, axis=0) - onehot
    slot_rank = jnp.sum(earlier * onehot, axis=1)
    position = flat_routes * capacity + slot_rank
    slot_table = jnp.full((experts * capacity,), pair_count, jnp.int32)
    slot_table = slot_table.at[position].set(jnp.arange(pair_count, dtype=jnp.int32))
    token_index = slot_table // top_k
    padded_tokens = jnp.concatenate([tokens, jnp.zeros((1, model_dim), jnp.bfloat16)], axis=0)
    scaled = (combine[:, :, None] * cotangent[:, None, :].astype(jnp.float32)).astype(jnp.bfloat16)
    padded_scaled = jnp.concatenate(
        [scaled.reshape(pair_count, model_dim), jnp.zeros((1, model_dim), jnp.bfloat16)], axis=0
    )
    send_rows = padded_tokens[token_index].reshape(n_expert, exp_dev * capacity, model_dim)
    send_grads = padded_scaled[slot_table].reshape(n_expert, exp_dev * capacity, model_dim)
    recv_rows = lax.all_to_all(send_rows, "expert", split_axis=0, concat_axis=0, tiled=True)
    recv_grads = lax.all_to_all(send_grads, "expert", split_axis=0, concat_axis=0, tiled=True)

    def regroup(received):
        shaped = received.reshape(n_expert, exp_dev, capacity, model_dim)
        return jnp.transpose(shaped, (1, 0, 2, 3)).reshape(exp_dev, slot_count, model_dim)

    local_rows = regroup(recv_rows)
    local_grads = regroup(recv_grads)
    batched_terms = jax.vmap(expert_terms)
    pair_piece, probe_piece, down_piece = lax.all_gather(
        (w_in, v_in, w_out[:, None]), "dp", axis=2, tiled=True
    )
    partials = batched_terms(local_rows, local_grads, pair_piece, probe_piece, down_piece[:, 0])
    return lax.psum_scatter(
        partials.astype(jnp.bfloat16), "dp", scatter_dimension=2, tiled=True
    ).astype(jnp.float32)


def dense_kernel(x_ref, c_ref, wt_ref, w_ref, v_ref, wo_ref, out_ref):
    half = w_ref.shape[0] // 2
    x = x_ref[...]
    pre = lax.dot_general(w_ref[...], x, NT, preferred_element_type=jnp.float32)
    tan = lax.dot_general(v_ref[...], x, NT, preferred_element_type=jnp.float32)
    back = lax.dot_general(wo_ref[...], c_ref[...], NT, preferred_element_type=jnp.float32)
    back = back * wt_ref[...]
    gate_dir, up_dir = directions(pre[:half], pre[half:], tan[:half], tan[half:], back)
    gate = lax.dot_general(gate_dir, x, NN, preferred_element_type=jnp.float32)
    up = lax.dot_general(up_dir, x, NN, preferred_element_type=jnp.float32)

    @pl.when(pl.program_id(0) == 0)
    def _():
        out_ref[0:half, :] = gate
        out_ref[half:, :] = up

    @pl.when(pl.program_id(0) != 0)
    def _():
        out_ref[0:half, :] += gate
        out_ref[half:, :] += up


def dense(tokens, cotangent, routes, combine, w_in, w_out, v_in):
    axes = ("dp", "expert")
    experts = lax.axis_size("expert")
    model_dim = tokens.shape[1]
    half = w_in.shape[2]
    named = routes[:, :, None] == jnp.arange(experts, dtype=jnp.int32)[None, None, :]
    weights = jnp.sum(jnp.where(named, combine[:, :, None], 0.0), axis=1)
    weights = lax.all_gather(weights, axes, axis=0, tiled=True)
    x = lax.all_gather(tokens, axes, axis=0, tiled=True)
    c = lax.all_gather(cotangent, axes, axis=0, tiled=True)
    mine = jnp.arange(experts, dtype=jnp.int32)[None, :] == lax.axis_index("expert")
    column = jnp.sum(jnp.where(mine, weights, 0.0), axis=1)[None, :]
    rows = x.shape[0]
    chunk = 256
    out = pl.pallas_call(
        dense_kernel,
        grid=(rows // chunk,),
        in_specs=[
            pl.BlockSpec((chunk, model_dim), lambda i: (i, 0)),
            pl.BlockSpec((chunk, model_dim), lambda i: (i, 0)),
            pl.BlockSpec((1, chunk), lambda i: (0, i)),
            pl.BlockSpec((2 * half, model_dim), lambda i: (0, 0)),
            pl.BlockSpec((2 * half, model_dim), lambda i: (0, 0)),
            pl.BlockSpec((half, model_dim), lambda i: (0, 0)),
        ],
        out_specs=pl.BlockSpec((2 * half, model_dim), lambda i: (0, 0)),
        out_shape=jax.ShapeDtypeStruct((2 * half, model_dim), jnp.float32),
        compiler_params=pltpu.CompilerParams(vmem_limit_bytes=48 * 2**20),
        cost_estimate=pl.CostEstimate(
            flops=2 * rows * model_dim * 7 * half, bytes_accessed=17 * 2**20, transcendentals=rows * half
        ),
    )(
        x,
        c,
        column,
        w_in.reshape(2 * half, model_dim),
        v_in.reshape(2 * half, model_dim),
        w_out.reshape(half, model_dim),
    )
    return out.reshape(1, 2, half, model_dim)


def local(tokens, cotangent, routes, combine, w_in, w_out, v_in):
    experts = lax.axis_size("expert") * w_in.shape[0]
    tok_dev, top_k = routes.shape
    if w_in.shape[0] == 1 and 2 * tok_dev * top_k // experts >= tok_dev:
        return dense(tokens, cotangent, routes, combine, w_in, w_out, v_in)
    return dispatched(tokens, cotangent, routes, combine, w_in, w_out, v_in)


def solution(mesh):
    in_specs = (
        P(("dp", "expert"), None),
        P(("dp", "expert"), None),
        P(("dp", "expert"), None),
        P(("dp", "expert"), None),
        P("expert", None, "dp", None),
        P("expert", "dp", None),
        P("expert", None, "dp", None),
    )
    out_specs = P("expert", None, "dp", None)
    return jax.shard_map(local, mesh=mesh, in_specs=in_specs, out_specs=out_specs, check_vma=False)
```

```python
import functools

import jax
import jax.numpy as jnp
from jax import lax
from jax.experimental import pallas as pl
from jax.experimental.pallas import tpu as pltpu
from jax.sharding import PartitionSpec as P

NT = (((1,), (1,)), ((), ()))
NN = (((1,), (0,)), ((), ()))


def expert_terms(slot_rows, slot_grads, w_pair, v_pair, w_down):
    hidden_width = w_pair.shape[1]
    model_dim = w_pair.shape[2]
    stacked = jnp.concatenate([w_pair, v_pair], axis=0).reshape(4 * hidden_width, model_dim)
    projected = lax.dot_general(slot_rows, stacked, NT, preferred_element_type=jnp.float32)
    pre_gate = projected[:, :hidden_width]
    pre_up = projected[:, hidden_width : 2 * hidden_width]
    tan_gate = projected[:, 2 * hidden_width : 3 * hidden_width]
    tan_up = projected[:, 3 * hidden_width :]
    back_grad = lax.dot_general(slot_grads, w_down, NT, preferred_element_type=jnp.float32)
    gate_dir, up_dir = directions(pre_gate, pre_up, tan_gate, tan_up, back_grad)
    gate_term = lax.dot_general(
        gate_dir, slot_rows, (((0,), (0,)), ((), ())), preferred_element_type=jnp.float32
    )
    up_term = lax.dot_general(
        up_dir, slot_rows, (((0,), (0,)), ((), ())), preferred_element_type=jnp.float32
    )
    return jnp.stack([gate_term, up_term], axis=0)


def directions(pre_gate, pre_up, tan_gate, tan_up, back_grad):
    gate_sig = jax.nn.sigmoid(pre_gate)
    first_deriv = gate_sig * (1.0 + pre_gate * (1.0 - gate_sig))
    second_deriv = gate_sig * (1.0 - gate_sig) * (2.0 + pre_gate * (1.0 - 2.0 * gate_sig))
    gate_dir = back_grad * (tan_up * first_deriv + pre_up * second_deriv * tan_gate)
    up_dir = back_grad * first_deriv * tan_gate
    return gate_dir.astype(jnp.bfloat16), up_dir.astype(jnp.bfloat16)


def dispatched(tokens, cotangent, routes, combine, w_in, w_out, v_in):
    n_expert = lax.axis_size("expert")
    exp_dev = w_in.shape[0]
    experts = n_expert * exp_dev
    tok_dev, top_k = routes.shape
    model_dim = tokens.shape[1]
    capacity = 2 * tok_dev * top_k // experts
    pair_count = tok_dev * top_k
    slot_count = n_expert * capacity
    flat_routes = routes.reshape(pair_count)
    onehot = (flat_routes[:, None] == jnp.arange(experts, dtype=jnp.int32)[None, :]).astype(
        jnp.int32
    )
    earlier = jnp.cumsum(onehot, axis=0) - onehot
    slot_rank = jnp.sum(earlier * onehot, axis=1)
    position = flat_routes * capacity + slot_rank
    slot_table = jnp.full((experts * capacity,), pair_count, jnp.int32)
    slot_table = slot_table.at[position].set(jnp.arange(pair_count, dtype=jnp.int32))
    token_index = slot_table // top_k
    padded_tokens = jnp.concatenate([tokens, jnp.zeros((1, model_dim), jnp.bfloat16)], axis=0)
    scaled = (combine[:, :, None] * cotangent[:, None, :].astype(jnp.float32)).astype(jnp.bfloat16)
    padded_scaled = jnp.concatenate(
        [scaled.reshape(pair_count, model_dim), jnp.zeros((1, model_dim), jnp.bfloat16)], axis=0
    )
    send_rows = padded_tokens[token_index].reshape(n_expert, exp_dev * capacity, model_dim)
    send_grads = padded_scaled[slot_table].reshape(n_expert, exp_dev * capacity, model_dim)
    recv_rows = lax.all_to_all(send_rows, "expert", split_axis=0, concat_axis=0, tiled=True)
    recv_grads = lax.all_to_all(send_grads, "expert", split_axis=0, concat_axis=0, tiled=True)

    def regroup(received):
        shaped = received.reshape(n_expert, exp_dev, capacity, model_dim)
        return jnp.transpose(shaped, (1, 0, 2, 3)).reshape(exp_dev, slot_count, model_dim)

    local_rows = regroup(recv_rows)
    local_grads = regroup(recv_grads)
    batched_terms = jax.vmap(expert_terms)
    pair_piece, probe_piece, down_piece = lax.all_gather(
        (w_in, v_in, w_out[:, None]), "dp", axis=2, tiled=True
    )
    partials = batched_terms(local_rows, local_grads, pair_piece, probe_piece, down_piece[:, 0])
    return lax.psum_scatter(
        partials.astype(jnp.bfloat16), "dp", scatter_dimension=2, tiled=True
    ).astype(jnp.float32)


def dense_kernel(*refs, blocks, tok_dev):
    count = len(blocks)
    sources = refs[:count]
    wt_ref, w_ref, v_ref, wo_ref, out_ref, x_s, c_s, sems = refs[count:]
    half = w_ref.shape[0] // 2
    chunk = 8 * tok_dev
    copies = []
    for n, (kind, slot, first, rows) in enumerate(blocks):
        dst = (x_s if kind == 0 else c_s).at[pl.ds(slot * tok_dev, tok_dev)]
        src = sources[n] if rows == tok_dev else sources[n].at[pl.ds(first, tok_dev)]
        copy = pltpu.make_async_copy(src, dst, sems.at[n])
        copy.start()
        copies.append((slot * tok_dev // chunk, copy))
    for step in range(x_s.shape[0] // chunk):
        for owner, copy in copies:
            if owner == step:
                copy.wait()
        x = x_s[step * chunk : (step + 1) * chunk]
        c = c_s[step * chunk : (step + 1) * chunk]
        pre = lax.dot_general(w_ref[...], x, NT, preferred_element_type=jnp.float32)
        tan = lax.dot_general(v_ref[...], x, NT, preferred_element_type=jnp.float32)
        back = lax.dot_general(wo_ref[...], c, NT, preferred_element_type=jnp.float32)
        back = back * wt_ref[:, step * chunk : (step + 1) * chunk]
        gate_dir, up_dir = directions(pre[:half], pre[half:], tan[:half], tan[half:], back)
        gate = lax.dot_general(gate_dir, x, NN, preferred_element_type=jnp.float32)
        up = lax.dot_general(up_dir, x, NN, preferred_element_type=jnp.float32)
        if step == 0:
            out_ref[0:half, :] = gate
            out_ref[half:, :] = up
        else:
            out_ref[0:half, :] += gate
            out_ref[half:, :] += up


CORE, X, Y = 1, 2, 16
Z_NEAR, Z_FAR = 4, 8


def swap(value, mask):
    axes = ("dp", "expert")
    count = lax.axis_size("dp") * lax.axis_size("expert")
    return lax.ppermute(value, axes, [(i, i ^ mask) for i in range(count)])


def everyone(value, masks):
    order, held = [0], value[None]
    for mask in masks:
        held = jnp.concatenate([held, swap(held, mask)], axis=0)
        order = order + [m ^ mask for m in order]
    return held, order


def dense(tokens, cotangent, routes, combine, w_in, w_out, v_in):
    experts = lax.axis_size("expert")
    tok_dev, model_dim = tokens.shape
    half = w_in.shape[2]
    named = routes[:, None, :] == jnp.arange(experts, dtype=jnp.int32)[None, :, None]
    weights = jnp.sum(jnp.where(named, combine[:, None, :], 0.0), axis=2).T
    weights, order = everyone(weights, (Z_FAR, Z_NEAR, Y, X, CORE))
    mine = jnp.arange(experts, dtype=jnp.int32)[None, :, None] == lax.axis_index("expert")
    weights = jnp.sum(jnp.where(mine, weights, 0.0), axis=1)

    own = jnp.concatenate([tokens, cotangent], axis=0)
    slices = [(0, own)] + [(m, swap(own, m)) for m in (Z_NEAR, Z_NEAR ^ Z_FAR, Z_FAR)]
    operands, blocks, sources = [], [], []

    def hold(array, kinds, mask):
        if mask not in sources:
            sources.append(mask)
        slot = sources.index(mask)
        for n, kind in enumerate(kinds):
            operands.append(array)
            blocks.append((kind, slot, n * tok_dev, len(kinds) * tok_dev))

    for mask, block in slices:
        by_x, by_y = swap(block, X), swap(block, Y)
        diag_x = swap(by_y[:tok_dev], X)
        diag_c = swap(by_x[tok_dev:], Y)
        parts = [(block, (0, 1), mask), (by_x, (0, 1), mask ^ X), (by_y, (0, 1), mask ^ Y)]
        parts += [(diag_x, (0,), mask ^ X ^ Y), (diag_c, (1,), mask ^ X ^ Y)]
        for array, kinds, source in parts:
            hold(array, kinds, source)
        for array, kinds, source in parts:
            hold(swap(array, CORE), kinds, source ^ CORE)

    column = jnp.stack([weights[order.index(m)] for m in sources], axis=0).reshape(1, -1)
    rows = len(sources) * tok_dev
    whole = pl.BlockSpec(memory_space=pltpu.VMEM)
    out = pl.pallas_call(
        functools.partial(dense_kernel, blocks=blocks, tok_dev=tok_dev),
        in_specs=[pl.BlockSpec(memory_space=pl.ANY)] * len(operands) + [whole] * 4,
        out_specs=whole,
        out_shape=jax.ShapeDtypeStruct((2 * half, model_dim), jnp.float32),
        scratch_shapes=[
            pltpu.VMEM((rows, model_dim), jnp.bfloat16),
            pltpu.VMEM((rows, model_dim), jnp.bfloat16),
            pltpu.SemaphoreType.DMA((len(blocks),)),
        ],
        compiler_params=pltpu.CompilerParams(vmem_limit_bytes=48 * 2**20),
        cost_estimate=pl.CostEstimate(
            flops=2 * rows * model_dim * 7 * half,
            bytes_accessed=17 * 2**20,
            transcendentals=rows * half,
        ),
    )(
        *operands,
        column,
        w_in.reshape(2 * half, model_dim),
        v_in.reshape(2 * half, model_dim),
        w_out.reshape(half, model_dim),
    )
    return out.reshape(1, 2, half, model_dim)


def local(tokens, cotangent, routes, combine, w_in, w_out, v_in):
    experts = lax.axis_size("expert") * w_in.shape[0]
    tok_dev, top_k = routes.shape
    sizes = (lax.axis_size("dp"), lax.axis_size("expert"))
    if sizes == (2, 16) and w_in.shape[0] == 1 and 2 * tok_dev * top_k // experts >= tok_dev:
        return dense(tokens, cotangent, routes, combine, w_in, w_out, v_in)
    return dispatched(tokens, cotangent, routes, combine, w_in, w_out, v_in)


def solution(mesh):
    in_specs = (
        P(("dp", "expert"), None),
        P(("dp", "expert"), None),
        P(("dp", "expert"), None),
        P(("dp", "expert"), None),
        P("expert", None, "dp", None),
        P("expert", "dp", None),
        P("expert", None, "dp", None),
    )
    out_specs = P("expert", None, "dp", None)
    return jax.shard_map(local, mesh=mesh, in_specs=in_specs, out_specs=out_specs, check_vma=False)
```

```python
import functools

import jax
import jax.numpy as jnp
from jax import lax
from jax.experimental import pallas as pl
from jax.experimental.pallas import tpu as pltpu
from jax.sharding import PartitionSpec as P

NT = (((1,), (1,)), ((), ()))
NN = (((1,), (0,)), ((), ()))


def expert_terms(slot_rows, slot_grads, w_pair, v_pair, w_down):
    hidden_width = w_pair.shape[1]
    model_dim = w_pair.shape[2]
    stacked = jnp.concatenate([w_pair, v_pair], axis=0).reshape(4 * hidden_width, model_dim)
    projected = lax.dot_general(slot_rows, stacked, NT, preferred_element_type=jnp.float32)
    pre_gate = projected[:, :hidden_width]
    pre_up = projected[:, hidden_width : 2 * hidden_width]
    tan_gate = projected[:, 2 * hidden_width : 3 * hidden_width]
    tan_up = projected[:, 3 * hidden_width :]
    back_grad = lax.dot_general(slot_grads, w_down, NT, preferred_element_type=jnp.float32)
    gate_dir, up_dir = directions(pre_gate, pre_up, tan_gate, tan_up, back_grad)
    gate_term = lax.dot_general(
        gate_dir, slot_rows, (((0,), (0,)), ((), ())), preferred_element_type=jnp.float32
    )
    up_term = lax.dot_general(
        up_dir, slot_rows, (((0,), (0,)), ((), ())), preferred_element_type=jnp.float32
    )
    return jnp.stack([gate_term, up_term], axis=0)


def directions(pre_gate, pre_up, tan_gate, tan_up, back_grad):
    gate_sig = jax.nn.sigmoid(pre_gate)
    first_deriv = gate_sig * (1.0 + pre_gate * (1.0 - gate_sig))
    second_deriv = gate_sig * (1.0 - gate_sig) * (2.0 + pre_gate * (1.0 - 2.0 * gate_sig))
    gate_dir = back_grad * (tan_up * first_deriv + pre_up * second_deriv * tan_gate)
    up_dir = back_grad * first_deriv * tan_gate
    return gate_dir.astype(jnp.bfloat16), up_dir.astype(jnp.bfloat16)


def dispatched(tokens, cotangent, routes, combine, w_in, w_out, v_in):
    n_expert = lax.axis_size("expert")
    exp_dev = w_in.shape[0]
    experts = n_expert * exp_dev
    tok_dev, top_k = routes.shape
    model_dim = tokens.shape[1]
    capacity = 2 * tok_dev * top_k // experts
    pair_count = tok_dev * top_k
    slot_count = n_expert * capacity
    flat_routes = routes.reshape(pair_count)
    onehot = (flat_routes[:, None] == jnp.arange(experts, dtype=jnp.int32)[None, :]).astype(
        jnp.int32
    )
    earlier = jnp.cumsum(onehot, axis=0) - onehot
    slot_rank = jnp.sum(earlier * onehot, axis=1)
    position = flat_routes * capacity + slot_rank
    slot_table = jnp.full((experts * capacity,), pair_count, jnp.int32)
    slot_table = slot_table.at[position].set(jnp.arange(pair_count, dtype=jnp.int32))
    token_index = slot_table // top_k
    padded_tokens = jnp.concatenate([tokens, jnp.zeros((1, model_dim), jnp.bfloat16)], axis=0)
    scaled = (combine[:, :, None] * cotangent[:, None, :].astype(jnp.float32)).astype(jnp.bfloat16)
    padded_scaled = jnp.concatenate(
        [scaled.reshape(pair_count, model_dim), jnp.zeros((1, model_dim), jnp.bfloat16)], axis=0
    )
    send_rows = padded_tokens[token_index].reshape(n_expert, exp_dev * capacity, model_dim)
    send_grads = padded_scaled[slot_table].reshape(n_expert, exp_dev * capacity, model_dim)
    recv_rows = lax.all_to_all(send_rows, "expert", split_axis=0, concat_axis=0, tiled=True)
    recv_grads = lax.all_to_all(send_grads, "expert", split_axis=0, concat_axis=0, tiled=True)

    def regroup(received):
        shaped = received.reshape(n_expert, exp_dev, capacity, model_dim)
        return jnp.transpose(shaped, (1, 0, 2, 3)).reshape(exp_dev, slot_count, model_dim)

    local_rows = regroup(recv_rows)
    local_grads = regroup(recv_grads)
    batched_terms = jax.vmap(expert_terms)
    pair_piece, probe_piece, down_piece = lax.all_gather(
        (w_in, v_in, w_out[:, None]), "dp", axis=2, tiled=True
    )
    partials = batched_terms(local_rows, local_grads, pair_piece, probe_piece, down_piece[:, 0])
    return lax.psum_scatter(
        partials.astype(jnp.bfloat16), "dp", scatter_dimension=2, tiled=True
    ).astype(jnp.float32)


CORE, X, Y = 1, 2, 16
Z_NEAR, Z_FAR = 4, 8
LANES = 128


def pack_kernel(tok_ref, cot_ref, route_ref, comb_ref, out_ref, *, experts):
    tok_dev, model_dim = tok_ref.shape
    out_ref[0:tok_dev, 0:model_dim] = tok_ref[...]
    out_ref[tok_dev:, 0:model_dim] = cot_ref[...]
    lane = lax.broadcasted_iota(jnp.int32, (tok_dev, LANES), 1)
    weight = jnp.zeros((tok_dev, LANES), jnp.float32)
    for k in range(route_ref.shape[1]):
        named = route_ref[:, k : k + 1] == lane % experts
        weight = jnp.where(named, comb_ref[:, k : k + 1], weight)
    high = weight.astype(jnp.bfloat16).astype(jnp.float32)
    middle = (weight - high).astype(jnp.bfloat16).astype(jnp.float32)
    low = weight - high - middle
    part = lane // experts
    zero = jnp.zeros_like(weight)
    value = jnp.where(part == 0, high, jnp.where(part == 1, middle, jnp.where(part == 2, low, zero)))
    out_ref[0:tok_dev, model_dim:] = value.astype(jnp.bfloat16)
    out_ref[tok_dev:, model_dim:] = zero.astype(jnp.bfloat16)


def slice_dirs(pieces, pick_ref, w_ref, v_ref, wo_ref, x_ref, c_ref, wt_ref, tok_dev):
    model_dim = x_ref.shape[1]
    half = wo_ref.shape[0]
    row = 0
    for piece in pieces:
        for first in range(0, piece.shape[0], 2 * tok_dev):
            at = pl.ds(row, tok_dev)
            x_ref[at, :] = piece[first : first + tok_dev, 0:model_dim]
            wt_ref[at, :] = piece[first : first + tok_dev, model_dim:]
            c_ref[at, :] = piece[first + tok_dev : first + 2 * tok_dev, 0:model_dim]
            row += tok_dev
    x = x_ref[...]
    weight = lax.dot_general(pick_ref[...], wt_ref[...], NT, preferred_element_type=jnp.float32)
    pre = lax.dot_general(w_ref[...], x, NT, preferred_element_type=jnp.float32)
    tan = lax.dot_general(v_ref[...], x, NT, preferred_element_type=jnp.float32)
    back = lax.dot_general(wo_ref[...], c_ref[...], NT, preferred_element_type=jnp.float32)
    back = back * weight[0:1, :]
    return directions(pre[:half], pre[half:], tan[:half], tan[half:], back)


def slice_kernel(*refs, count, tok_dev):
    pieces = refs[:count]
    pick_ref, w_ref, v_ref, wo_ref, x_ref, dir_ref, c_ref, wt_ref = refs[count:]
    half = wo_ref.shape[0]
    gate_dir, up_dir = slice_dirs(
        pieces, pick_ref, w_ref, v_ref, wo_ref, x_ref, c_ref, wt_ref, tok_dev
    )
    dir_ref[0:half, :] = gate_dir
    dir_ref[half:, :] = up_dir


def last_kernel(*refs, count, earlier, tok_dev):
    pieces = refs[:count]
    held = refs[count : count + 2 * earlier]
    pick_ref, w_ref, v_ref, wo_ref, out_ref, x_ref, c_ref, wt_ref, dir_ref, sum_ref, sems = refs[
        count + 2 * earlier :
    ]
    half = wo_ref.shape[0]
    gate_dir, up_dir = slice_dirs(
        pieces, pick_ref, w_ref, v_ref, wo_ref, x_ref, c_ref, wt_ref, tok_dev
    )
    dir_ref[0:half, :] = gate_dir
    dir_ref[half:, :] = up_dir
    pairs = [(held[2 * n], held[2 * n + 1]) for n in range(earlier)] + [(x_ref, dir_ref)]
    columns = 512
    copies = []
    for n in range(out_ref.shape[1] // columns):
        at = pl.ds(n * columns, columns)
        total = None
        for rows, dirs in pairs:
            term = lax.dot_general(dirs[...], rows[:, at], NN, preferred_element_type=jnp.float32)
            total = term if total is None else total + term
        sum_ref[:, at] = total
        copy = pltpu.make_async_copy(sum_ref.at[:, at], out_ref.at[:, at], sems.at[n])
        copy.start()
        copies.append(copy)
    for copy in copies:
        copy.wait()


def swap(value, masks):
    axes = ("dp", "expert")
    count = lax.axis_size("dp") * lax.axis_size("expert")
    return lax.ppermute(value, axes, [(i, i ^ masks[i & CORE]) for i in range(count)])


def dense(tokens, cotangent, routes, combine, w_in, w_out, v_in):
    experts = lax.axis_size("expert")
    tok_dev, model_dim = tokens.shape
    half = w_in.shape[2]
    wide = model_dim + LANES
    inside = pl.BlockSpec(memory_space=pltpu.VMEM)
    own = pl.pallas_call(
        functools.partial(pack_kernel, experts=experts),
        in_specs=[inside] * 4,
        out_specs=inside,
        out_shape=jax.ShapeDtypeStruct((2 * tok_dev, wide), jnp.bfloat16),
    )(tokens, cotangent, routes, combine)

    lane = jnp.arange(LANES, dtype=jnp.int32)
    mine = (lane % experts == lax.axis_index("expert")) & (lane < 3 * experts)
    pick = jnp.broadcast_to(mine.astype(jnp.bfloat16)[None, :], (16, LANES))

    slices = [own] + [swap(own, (m, m)) for m in (Z_NEAR, Z_NEAR ^ Z_FAR, Z_FAR)]
    weights = (
        w_in.reshape(2 * half, model_dim),
        v_in.reshape(2 * half, model_dim),
        w_out.reshape(half, model_dim),
    )
    held = []
    for n, block in enumerate(slices):
        chip = jnp.concatenate([block, swap(block, (CORE, CORE))], axis=0)
        beside = swap(chip, (X, Y))
        across = swap(beside[: 2 * tok_dev], (Y, X))
        got = jnp.concatenate([beside, across], axis=0)
        pieces = [chip, got, swap(got, (CORE, CORE))]
        rows = sum(p.shape[0] for p in pieces) // 2
        last = n == len(slices) - 1
        scratch = [
            pltpu.VMEM((rows, model_dim), jnp.bfloat16),
            pltpu.VMEM((rows, LANES), jnp.bfloat16),
        ]
        params = pltpu.CompilerParams(vmem_limit_bytes=28 * 2**20)
        if not last:
            held += pl.pallas_call(
                functools.partial(slice_kernel, count=len(pieces), tok_dev=tok_dev),
                in_specs=[inside] * (len(pieces) + 4),
                out_specs=[inside] * 2,
                out_shape=[
                    jax.ShapeDtypeStruct((rows, model_dim), jnp.bfloat16),
                    jax.ShapeDtypeStruct((2 * half, rows), jnp.bfloat16),
                ],
                scratch_shapes=scratch,
                compiler_params=params,
                cost_estimate=pl.CostEstimate(
                    flops=2 * rows * model_dim * 5 * half,
                    bytes_accessed=8 * 2**20,
                    transcendentals=rows * half,
                ),
            )(*pieces, pick, *weights)
    out = pl.pallas_call(
        functools.partial(
            last_kernel, count=len(pieces), earlier=len(held) // 2, tok_dev=tok_dev
        ),
        in_specs=[inside] * (len(pieces) + len(held) + 4),
        out_specs=pl.BlockSpec(memory_space=pl.ANY),
        out_shape=jax.ShapeDtypeStruct((2 * half, model_dim), jnp.float32),
        scratch_shapes=[pltpu.VMEM((rows, model_dim), jnp.bfloat16)]
        + scratch
        + [
            pltpu.VMEM((2 * half, rows), jnp.bfloat16),
            pltpu.VMEM((2 * half, model_dim), jnp.float32),
            pltpu.SemaphoreType.DMA((model_dim // 512,)),
        ],
        compiler_params=params,
        cost_estimate=pl.CostEstimate(
            flops=2 * rows * model_dim * 13 * half,
            bytes_accessed=16 * 2**20,
            transcendentals=rows * half,
        ),
    )(*pieces, *held, pick, *weights)
    return out.reshape(1, 2, half, model_dim)


def local(tokens, cotangent, routes, combine, w_in, w_out, v_in):
    experts = lax.axis_size("expert") * w_in.shape[0]
    tok_dev, top_k = routes.shape
    sizes = (lax.axis_size("dp"), lax.axis_size("expert"))
    if sizes == (2, 16) and w_in.shape[0] == 1 and 2 * tok_dev * top_k // experts >= tok_dev:
        return dense(tokens, cotangent, routes, combine, w_in, w_out, v_in)
    return dispatched(tokens, cotangent, routes, combine, w_in, w_out, v_in)


def solution(mesh):
    in_specs = (
        P(("dp", "expert"), None),
        P(("dp", "expert"), None),
        P(("dp", "expert"), None),
        P(("dp", "expert"), None),
        P("expert", None, "dp", None),
        P("expert", "dp", None),
        P("expert", None, "dp", None),
    )
    out_specs = P("expert", None, "dp", None)
    return jax.shard_map(local, mesh=mesh, in_specs=in_specs, out_specs=out_specs, check_vma=False)
```

```python
import functools

import jax
import jax.numpy as jnp
from jax import lax
from jax.experimental import pallas as pl
from jax.experimental.pallas import tpu as pltpu
from jax.sharding import PartitionSpec as P

NT = (((1,), (1,)), ((), ()))
NN = (((1,), (0,)), ((), ()))


def expert_terms(slot_rows, slot_grads, w_pair, v_pair, w_down):
    hidden_width = w_pair.shape[1]
    model_dim = w_pair.shape[2]
    stacked = jnp.concatenate([w_pair, v_pair], axis=0).reshape(4 * hidden_width, model_dim)
    projected = lax.dot_general(slot_rows, stacked, NT, preferred_element_type=jnp.float32)
    pre_gate = projected[:, :hidden_width]
    pre_up = projected[:, hidden_width : 2 * hidden_width]
    tan_gate = projected[:, 2 * hidden_width : 3 * hidden_width]
    tan_up = projected[:, 3 * hidden_width :]
    back_grad = lax.dot_general(slot_grads, w_down, NT, preferred_element_type=jnp.float32)
    gate_dir, up_dir = directions(pre_gate, pre_up, tan_gate, tan_up, back_grad)
    gate_term = lax.dot_general(
        gate_dir, slot_rows, (((0,), (0,)), ((), ())), preferred_element_type=jnp.float32
    )
    up_term = lax.dot_general(
        up_dir, slot_rows, (((0,), (0,)), ((), ())), preferred_element_type=jnp.float32
    )
    return jnp.stack([gate_term, up_term], axis=0)


def directions(pre_gate, pre_up, tan_gate, tan_up, back_grad):
    gate_sig = jax.nn.sigmoid(pre_gate)
    first_deriv = gate_sig * (1.0 + pre_gate * (1.0 - gate_sig))
    second_deriv = gate_sig * (1.0 - gate_sig) * (2.0 + pre_gate * (1.0 - 2.0 * gate_sig))
    gate_dir = back_grad * (tan_up * first_deriv + pre_up * second_deriv * tan_gate)
    up_dir = back_grad * first_deriv * tan_gate
    return gate_dir.astype(jnp.bfloat16), up_dir.astype(jnp.bfloat16)


def dispatched(tokens, cotangent, routes, combine, w_in, w_out, v_in):
    n_expert = lax.axis_size("expert")
    exp_dev = w_in.shape[0]
    experts = n_expert * exp_dev
    tok_dev, top_k = routes.shape
    model_dim = tokens.shape[1]
    capacity = 2 * tok_dev * top_k // experts
    pair_count = tok_dev * top_k
    slot_count = n_expert * capacity
    flat_routes = routes.reshape(pair_count)
    onehot = (flat_routes[:, None] == jnp.arange(experts, dtype=jnp.int32)[None, :]).astype(
        jnp.int32
    )
    earlier = jnp.cumsum(onehot, axis=0) - onehot
    slot_rank = jnp.sum(earlier * onehot, axis=1)
    position = flat_routes * capacity + slot_rank
    slot_table = jnp.full((experts * capacity,), pair_count, jnp.int32)
    slot_table = slot_table.at[position].set(jnp.arange(pair_count, dtype=jnp.int32))
    token_index = slot_table // top_k
    padded_tokens = jnp.concatenate([tokens, jnp.zeros((1, model_dim), jnp.bfloat16)], axis=0)
    scaled = (combine[:, :, None] * cotangent[:, None, :].astype(jnp.float32)).astype(jnp.bfloat16)
    padded_scaled = jnp.concatenate(
        [scaled.reshape(pair_count, model_dim), jnp.zeros((1, model_dim), jnp.bfloat16)], axis=0
    )
    send_rows = padded_tokens[token_index].reshape(n_expert, exp_dev * capacity, model_dim)
    send_grads = padded_scaled[slot_table].reshape(n_expert, exp_dev * capacity, model_dim)
    recv_rows = lax.all_to_all(send_rows, "expert", split_axis=0, concat_axis=0, tiled=True)
    recv_grads = lax.all_to_all(send_grads, "expert", split_axis=0, concat_axis=0, tiled=True)

    def regroup(received):
        shaped = received.reshape(n_expert, exp_dev, capacity, model_dim)
        return jnp.transpose(shaped, (1, 0, 2, 3)).reshape(exp_dev, slot_count, model_dim)

    local_rows = regroup(recv_rows)
    local_grads = regroup(recv_grads)
    batched_terms = jax.vmap(expert_terms)
    pair_piece, probe_piece, down_piece = lax.all_gather(
        (w_in, v_in, w_out[:, None]), "dp", axis=2, tiled=True
    )
    partials = batched_terms(local_rows, local_grads, pair_piece, probe_piece, down_piece[:, 0])
    return lax.psum_scatter(
        partials.astype(jnp.bfloat16), "dp", scatter_dimension=2, tiled=True
    ).astype(jnp.float32)


CORE, X, Y = 1, 2, 16
Z_NEAR, Z_FAR = 4, 8
LANES = 128


def pack_kernel(tok_ref, cot_ref, route_ref, comb_ref, out_ref, *, experts):
    tok_dev, model_dim = tok_ref.shape
    out_ref[0:tok_dev, 0:model_dim] = tok_ref[...]
    out_ref[tok_dev:, 0:model_dim] = cot_ref[...]
    line = lax.broadcasted_iota(jnp.int32, (LANES, tok_dev), 0)
    weight = jnp.zeros((LANES, tok_dev), jnp.float32)
    for k in range(route_ref.shape[0]):
        named = route_ref[k : k + 1, :] == line % experts
        weight = jnp.where(named, comb_ref[k : k + 1, :], weight)
    high = weight.astype(jnp.bfloat16).astype(jnp.float32)
    middle = (weight - high).astype(jnp.bfloat16).astype(jnp.float32)
    low = weight - high - middle
    part = line // experts
    zero = jnp.zeros_like(weight)
    value = jnp.where(part == 0, high, jnp.where(part == 1, middle, jnp.where(part == 2, low, zero)))
    row = lax.broadcasted_iota(jnp.int32, (tok_dev, tok_dev), 0)
    column = lax.broadcasted_iota(jnp.int32, (tok_dev, tok_dev), 1)
    same = (row == column).astype(jnp.float32).astype(jnp.bfloat16)
    turned = lax.dot_general(
        same, value.astype(jnp.bfloat16), NT, preferred_element_type=jnp.float32
    )
    out_ref[0:tok_dev, model_dim:] = turned.astype(jnp.bfloat16)
    out_ref[tok_dev:, model_dim:] = jnp.zeros((tok_dev, LANES), jnp.bfloat16)


def slice_dirs(pieces, pick_ref, w_ref, v_ref, wo_ref, x_ref, c_ref, wt_ref, tok_dev):
    model_dim = x_ref.shape[1]
    half = wo_ref.shape[0]
    row = 0
    for piece in pieces:
        for first in range(0, piece.shape[0], 2 * tok_dev):
            at = pl.ds(row, tok_dev)
            x_ref[at, :] = piece[first : first + tok_dev, 0:model_dim]
            wt_ref[at, :] = piece[first : first + tok_dev, model_dim:]
            c_ref[at, :] = piece[first + tok_dev : first + 2 * tok_dev, 0:model_dim]
            row += tok_dev
    x = x_ref[...]
    weight = lax.dot_general(pick_ref[...], wt_ref[...], NT, preferred_element_type=jnp.float32)
    both = jnp.concatenate([w_ref[...], v_ref[...]], axis=0)
    seen = lax.dot_general(both, x, NT, preferred_element_type=jnp.float32)
    back = lax.dot_general(wo_ref[...], c_ref[...], NT, preferred_element_type=jnp.float32)
    back = back * weight[0:1, :]
    parts = [seen[n * half : (n + 1) * half] for n in range(4)]
    return directions(*parts, back)


def slice_kernel(*refs, count, tok_dev):
    pieces = refs[:count]
    pick_ref, w_ref, v_ref, wo_ref, x_ref, dir_ref, c_ref, wt_ref = refs[count:]
    half = wo_ref.shape[0]
    gate_dir, up_dir = slice_dirs(
        pieces, pick_ref, w_ref, v_ref, wo_ref, x_ref, c_ref, wt_ref, tok_dev
    )
    dir_ref[0:half, :] = gate_dir
    dir_ref[half:, :] = up_dir


def last_kernel(*refs, count, earlier, tok_dev):
    pieces = refs[:count]
    held = refs[count : count + 2 * earlier]
    pick_ref, w_ref, v_ref, wo_ref, out_ref, x_ref, c_ref, wt_ref, dir_ref, sum_ref, sems = refs[
        count + 2 * earlier :
    ]
    half = wo_ref.shape[0]
    gate_dir, up_dir = slice_dirs(
        pieces, pick_ref, w_ref, v_ref, wo_ref, x_ref, c_ref, wt_ref, tok_dev
    )
    dir_ref[0:half, :] = gate_dir
    dir_ref[half:, :] = up_dir
    pairs = [(held[2 * n], held[2 * n + 1]) for n in range(earlier)] + [(x_ref, dir_ref)]
    columns = 512
    copies = []
    for n in range(out_ref.shape[1] // columns):
        at = pl.ds(n * columns, columns)
        rows = jnp.concatenate([r[:, at] for r, _ in pairs], axis=0)
        dirs = jnp.concatenate([d[...] for _, d in pairs], axis=1)
        sum_ref[:, at] = lax.dot_general(dirs, rows, NN, preferred_element_type=jnp.float32)
        copy = pltpu.make_async_copy(sum_ref.at[:, at], out_ref.at[:, at], sems.at[n])
        copy.start()
        copies.append(copy)
    for copy in copies:
        copy.wait()


def swap(value, masks):
    axes = ("dp", "expert")
    count = lax.axis_size("dp") * lax.axis_size("expert")
    return lax.ppermute(value, axes, [(i, i ^ masks[i & CORE]) for i in range(count)])


def after(value, *others):
    return lax.optimization_barrier((value, *others))[0]


def dense(tokens, cotangent, routes, combine, w_in, w_out, v_in):
    experts = lax.axis_size("expert")
    tok_dev, model_dim = tokens.shape
    half = w_in.shape[2]
    wide = model_dim + LANES
    inside = pl.BlockSpec(memory_space=pltpu.VMEM)
    own = pl.pallas_call(
        functools.partial(pack_kernel, experts=experts),
        in_specs=[inside] * 4,
        out_specs=inside,
        out_shape=jax.ShapeDtypeStruct((2 * tok_dev, wide), jnp.bfloat16),
    )(tokens, cotangent, routes.T, combine.T)

    lane = jnp.arange(LANES, dtype=jnp.int32)
    mine = (lane % experts == lax.axis_index("expert")) & (lane < 3 * experts)
    pick = jnp.broadcast_to(mine.astype(jnp.bfloat16)[None, :], (16, LANES))

    slices = [own]
    for mask in (Z_NEAR, Z_NEAR ^ Z_FAR, Z_FAR):
        sent = own if len(slices) == 1 else after(own, slices[-1])
        slices.append(swap(sent, (mask, mask)))
    weights = (
        w_in.reshape(2 * half, model_dim),
        v_in.reshape(2 * half, model_dim),
        w_out.reshape(half, model_dim),
    )
    held = []
    for n, block in enumerate(slices):
        chip = jnp.concatenate([block, swap(block, (CORE, CORE))], axis=0)
        beside = swap(chip, (X, Y))
        across = swap(beside[: 2 * tok_dev], (Y, X))
        pieces = [chip, beside, across]
        pieces += [swap(got, (CORE, CORE)) for got in (beside, across)]
        rows = sum(p.shape[0] for p in pieces) // 2
        last = n == len(slices) - 1
        scratch = [
            pltpu.VMEM((rows, model_dim), jnp.bfloat16),
            pltpu.VMEM((rows, LANES), jnp.bfloat16),
        ]
        params = pltpu.CompilerParams(vmem_limit_bytes=28 * 2**20)
        if not last:
            held += pl.pallas_call(
                functools.partial(slice_kernel, count=len(pieces), tok_dev=tok_dev),
                in_specs=[inside] * (len(pieces) + 4),
                out_specs=[inside] * 2,
                out_shape=[
                    jax.ShapeDtypeStruct((rows, model_dim), jnp.bfloat16),
                    jax.ShapeDtypeStruct((2 * half, rows), jnp.bfloat16),
                ],
                scratch_shapes=scratch,
                compiler_params=params,
                cost_estimate=pl.CostEstimate(
                    flops=2 * rows * model_dim * 5 * half,
                    bytes_accessed=8 * 2**20,
                    transcendentals=rows * half,
                ),
            )(*pieces, pick, *weights)
    out = pl.pallas_call(
        functools.partial(
            last_kernel, count=len(pieces), earlier=len(held) // 2, tok_dev=tok_dev
        ),
        in_specs=[inside] * (len(pieces) + len(held) + 4),
        out_specs=pl.BlockSpec(memory_space=pl.ANY),
        out_shape=jax.ShapeDtypeStruct((2 * half, model_dim), jnp.float32),
        scratch_shapes=[pltpu.VMEM((rows, model_dim), jnp.bfloat16)]
        + scratch
        + [
            pltpu.VMEM((2 * half, rows), jnp.bfloat16),
            pltpu.VMEM((2 * half, model_dim), jnp.float32),
            pltpu.SemaphoreType.DMA((model_dim // 512,)),
        ],
        compiler_params=params,
        cost_estimate=pl.CostEstimate(
            flops=2 * rows * model_dim * 13 * half,
            bytes_accessed=16 * 2**20,
            transcendentals=rows * half,
        ),
    )(*pieces, *held, pick, *weights)
    return out.reshape(1, 2, half, model_dim)


def local(tokens, cotangent, routes, combine, w_in, w_out, v_in):
    experts = lax.axis_size("expert") * w_in.shape[0]
    tok_dev, top_k = routes.shape
    sizes = (lax.axis_size("dp"), lax.axis_size("expert"))
    if sizes == (2, 16) and w_in.shape[0] == 1 and 2 * tok_dev * top_k // experts >= tok_dev:
        return dense(tokens, cotangent, routes, combine, w_in, w_out, v_in)
    return dispatched(tokens, cotangent, routes, combine, w_in, w_out, v_in)


def solution(mesh):
    in_specs = (
        P(("dp", "expert"), None),
        P(("dp", "expert"), None),
        P(("dp", "expert"), None),
        P(("dp", "expert"), None),
        P("expert", None, "dp", None),
        P("expert", "dp", None),
        P("expert", None, "dp", None),
    )
    out_specs = P("expert", None, "dp", None)
    return jax.shard_map(local, mesh=mesh, in_specs=in_specs, out_specs=out_specs, check_vma=False)
```

```python
import functools

import jax
import jax.numpy as jnp
from jax import lax
from jax.experimental import pallas as pl
from jax.experimental.pallas import tpu as pltpu
from jax.sharding import PartitionSpec as P

NT = (((1,), (1,)), ((), ()))
NN = (((1,), (0,)), ((), ()))


def expert_terms(slot_rows, slot_grads, w_pair, v_pair, w_down):
    hidden_width = w_pair.shape[1]
    model_dim = w_pair.shape[2]
    stacked = jnp.concatenate([w_pair, v_pair], axis=0).reshape(4 * hidden_width, model_dim)
    projected = lax.dot_general(slot_rows, stacked, NT, preferred_element_type=jnp.float32)
    pre_gate = projected[:, :hidden_width]
    pre_up = projected[:, hidden_width : 2 * hidden_width]
    tan_gate = projected[:, 2 * hidden_width : 3 * hidden_width]
    tan_up = projected[:, 3 * hidden_width :]
    back_grad = lax.dot_general(slot_grads, w_down, NT, preferred_element_type=jnp.float32)
    gate_dir, up_dir = directions(pre_gate, pre_up, tan_gate, tan_up, back_grad)
    gate_term = lax.dot_general(
        gate_dir, slot_rows, (((0,), (0,)), ((), ())), preferred_element_type=jnp.float32
    )
    up_term = lax.dot_general(
        up_dir, slot_rows, (((0,), (0,)), ((), ())), preferred_element_type=jnp.float32
    )
    return jnp.stack([gate_term, up_term], axis=0)


def directions(pre_gate, pre_up, tan_gate, tan_up, back_grad):
    gate_sig = jax.nn.sigmoid(pre_gate)
    first_deriv = gate_sig * (1.0 + pre_gate * (1.0 - gate_sig))
    second_deriv = gate_sig * (1.0 - gate_sig) * (2.0 + pre_gate * (1.0 - 2.0 * gate_sig))
    gate_dir = back_grad * (tan_up * first_deriv + pre_up * second_deriv * tan_gate)
    up_dir = back_grad * first_deriv * tan_gate
    return gate_dir.astype(jnp.bfloat16), up_dir.astype(jnp.bfloat16)


def dispatched(tokens, cotangent, routes, combine, w_in, w_out, v_in):
    n_expert = lax.axis_size("expert")
    exp_dev = w_in.shape[0]
    experts = n_expert * exp_dev
    tok_dev, top_k = routes.shape
    model_dim = tokens.shape[1]
    capacity = 2 * tok_dev * top_k // experts
    pair_count = tok_dev * top_k
    slot_count = n_expert * capacity
    flat_routes = routes.reshape(pair_count)
    onehot = (flat_routes[:, None] == jnp.arange(experts, dtype=jnp.int32)[None, :]).astype(
        jnp.int32
    )
    earlier = jnp.cumsum(onehot, axis=0) - onehot
    slot_rank = jnp.sum(earlier * onehot, axis=1)
    position = flat_routes * capacity + slot_rank
    slot_table = jnp.full((experts * capacity,), pair_count, jnp.int32)
    slot_table = slot_table.at[position].set(jnp.arange(pair_count, dtype=jnp.int32))
    token_index = slot_table // top_k
    padded_tokens = jnp.concatenate([tokens, jnp.zeros((1, model_dim), jnp.bfloat16)], axis=0)
    scaled = (combine[:, :, None] * cotangent[:, None, :].astype(jnp.float32)).astype(jnp.bfloat16)
    padded_scaled = jnp.concatenate(
        [scaled.reshape(pair_count, model_dim), jnp.zeros((1, model_dim), jnp.bfloat16)], axis=0
    )
    send_rows = padded_tokens[token_index].reshape(n_expert, exp_dev * capacity, model_dim)
    send_grads = padded_scaled[slot_table].reshape(n_expert, exp_dev * capacity, model_dim)
    recv_rows = lax.all_to_all(send_rows, "expert", split_axis=0, concat_axis=0, tiled=True)
    recv_grads = lax.all_to_all(send_grads, "expert", split_axis=0, concat_axis=0, tiled=True)

    def regroup(received):
        shaped = received.reshape(n_expert, exp_dev, capacity, model_dim)
        return jnp.transpose(shaped, (1, 0, 2, 3)).reshape(exp_dev, slot_count, model_dim)

    local_rows = regroup(recv_rows)
    local_grads = regroup(recv_grads)
    batched_terms = jax.vmap(expert_terms)
    pair_piece, probe_piece, down_piece = lax.all_gather(
        (w_in, v_in, w_out[:, None]), "dp", axis=2, tiled=True
    )
    partials = batched_terms(local_rows, local_grads, pair_piece, probe_piece, down_piece[:, 0])
    return lax.psum_scatter(
        partials.astype(jnp.bfloat16), "dp", scatter_dimension=2, tiled=True
    ).astype(jnp.float32)


CORE, X, Y = 1, 2, 16
Z_NEAR, Z_FAR = 4, 8
LANES = 128


def pack_kernel(tok_ref, cot_ref, route_ref, comb_ref, out_ref, *, experts):
    tok_dev, model_dim = tok_ref.shape
    out_ref[0:tok_dev, 0:model_dim] = tok_ref[...]
    out_ref[tok_dev:, 0:model_dim] = cot_ref[...]
    line = lax.broadcasted_iota(jnp.int32, (LANES, tok_dev), 0)
    weight = jnp.zeros((LANES, tok_dev), jnp.float32)
    for k in range(route_ref.shape[0]):
        named = route_ref[k : k + 1, :] == line % experts
        weight = jnp.where(named, comb_ref[k : k + 1, :], weight)
    high = weight.astype(jnp.bfloat16).astype(jnp.float32)
    middle = (weight - high).astype(jnp.bfloat16).astype(jnp.float32)
    low = weight - high - middle
    part = line // experts
    zero = jnp.zeros_like(weight)
    value = jnp.where(part == 0, high, jnp.where(part == 1, middle, jnp.where(part == 2, low, zero)))
    row = lax.broadcasted_iota(jnp.int32, (tok_dev, tok_dev), 0)
    column = lax.broadcasted_iota(jnp.int32, (tok_dev, tok_dev), 1)
    same = (row == column).astype(jnp.float32).astype(jnp.bfloat16)
    turned = lax.dot_general(
        same, value.astype(jnp.bfloat16), NT, preferred_element_type=jnp.float32
    )
    out_ref[0:tok_dev, model_dim:] = turned.astype(jnp.bfloat16)
    out_ref[tok_dev:, model_dim:] = jnp.zeros((tok_dev, LANES), jnp.bfloat16)


def slice_dirs(pieces, pick_ref, w_ref, v_ref, wo_ref, x_ref, c_ref, wt_ref, tok_dev):
    model_dim = x_ref.shape[1]
    half = wo_ref.shape[0]
    row = 0
    for piece in pieces:
        for first in range(0, piece.shape[0], 2 * tok_dev):
            at = pl.ds(row, tok_dev)
            x_ref[at, :] = piece[first : first + tok_dev, 0:model_dim]
            wt_ref[at, :] = piece[first : first + tok_dev, model_dim:]
            c_ref[at, :] = piece[first + tok_dev : first + 2 * tok_dev, 0:model_dim]
            row += tok_dev
    x = x_ref[...]
    weight = lax.dot_general(pick_ref[...], wt_ref[...], NT, preferred_element_type=jnp.float32)
    both = jnp.concatenate([w_ref[...], v_ref[...]], axis=0)
    seen = lax.dot_general(both, x, NT, preferred_element_type=jnp.float32)
    back = lax.dot_general(wo_ref[...], c_ref[...], NT, preferred_element_type=jnp.float32)
    back = back * weight[0:1, :]
    parts = [seen[n * half : (n + 1) * half] for n in range(4)]
    return directions(*parts, back)


def slice_kernel(*refs, count, tok_dev):
    pieces = refs[:count]
    pick_ref, w_ref, v_ref, wo_ref, x_ref, dir_ref, c_ref, wt_ref = refs[count:]
    half = wo_ref.shape[0]
    gate_dir, up_dir = slice_dirs(
        pieces, pick_ref, w_ref, v_ref, wo_ref, x_ref, c_ref, wt_ref, tok_dev
    )
    dir_ref[0:half, :] = gate_dir
    dir_ref[half:, :] = up_dir


def last_kernel(*refs, count, earlier, tok_dev):
    pieces = refs[:count]
    held = refs[count : count + 2 * earlier]
    pick_ref, w_ref, v_ref, wo_ref, out_ref, x_ref, c_ref, wt_ref, dir_ref, sum_ref, sems = refs[
        count + 2 * earlier :
    ]
    half = wo_ref.shape[0]
    gate_dir, up_dir = slice_dirs(
        pieces, pick_ref, w_ref, v_ref, wo_ref, x_ref, c_ref, wt_ref, tok_dev
    )
    dir_ref[0:half, :] = gate_dir
    dir_ref[half:, :] = up_dir
    pairs = [(held[2 * n], held[2 * n + 1]) for n in range(earlier)] + [(x_ref, dir_ref)]
    columns = 512
    copies = []
    for n in range(out_ref.shape[1] // columns):
        at = pl.ds(n * columns, columns)
        rows = jnp.concatenate([r[:, at] for r, _ in pairs], axis=0)
        dirs = jnp.concatenate([d[...] for _, d in pairs], axis=1)
        sum_ref[:, at] = lax.dot_general(dirs, rows, NN, preferred_element_type=jnp.float32)
        copy = pltpu.make_async_copy(sum_ref.at[:, at], out_ref.at[:, at], sems.at[n])
        copy.start()
        copies.append(copy)
    for copy in copies:
        copy.wait()


def swap(value, masks):
    axes = ("dp", "expert")
    count = lax.axis_size("dp") * lax.axis_size("expert")
    return lax.ppermute(value, axes, [(i, i ^ masks[i & CORE]) for i in range(count)])


def after(value, *others):
    return lax.optimization_barrier((value, *others))[0]


def dense(tokens, cotangent, routes, combine, w_in, w_out, v_in):
    experts = lax.axis_size("expert")
    tok_dev, model_dim = tokens.shape
    half = w_in.shape[2]
    wide = model_dim + LANES
    inside = pl.BlockSpec(memory_space=pltpu.VMEM)
    own = pl.pallas_call(
        functools.partial(pack_kernel, experts=experts),
        in_specs=[inside] * 4,
        out_specs=inside,
        out_shape=jax.ShapeDtypeStruct((2 * tok_dev, wide), jnp.bfloat16),
    )(tokens, cotangent, routes.T, combine.T)

    lane = jnp.arange(LANES, dtype=jnp.int32)
    mine = (lane % experts == lax.axis_index("expert")) & (lane < 3 * experts)
    pick = jnp.broadcast_to(mine.astype(jnp.bfloat16)[None, :], (16, LANES))

    weights = (
        w_in.reshape(2 * half, model_dim),
        v_in.reshape(2 * half, model_dim),
        w_out.reshape(half, model_dim),
    )

    def share(blocks, *first):
        others = [swap(b, (CORE, CORE)) for b in blocks]
        others[0] = after(others[0], *first)
        return jnp.concatenate(blocks + others, axis=0)

    def cross(chip, *first):
        beside = after(swap(chip, (X, Y)), *first)
        onward = beside[: chip.shape[0] // 2]
        across = swap(onward, (Y, X))
        pieces = [chip, beside, across]
        return pieces + [swap(got, (CORE, CORE)) for got in (beside, across)], onward

    def call(pieces, held, last):
        rows = sum(p.shape[0] for p in pieces) // 2
        total = rows + sum(h.shape[0] for h in held[0::2])
        scratch = [
            pltpu.VMEM((rows, model_dim), jnp.bfloat16),
            pltpu.VMEM((rows, LANES), jnp.bfloat16),
        ]
        kinds = dict(
            in_specs=[inside] * (len(pieces) + len(held) + 4),
            compiler_params=pltpu.CompilerParams(vmem_limit_bytes=20 * 2**20),
            cost_estimate=pl.CostEstimate(
                flops=2 * model_dim * half * (5 * rows + 2 * total * last),
                bytes_accessed=8 * 2**20,
                transcendentals=rows * half,
            ),
        )
        if not last:
            return pl.pallas_call(
                functools.partial(slice_kernel, count=len(pieces), tok_dev=tok_dev),
                out_specs=[inside] * 2,
                out_shape=[
                    jax.ShapeDtypeStruct((rows, model_dim), jnp.bfloat16),
                    jax.ShapeDtypeStruct((2 * half, rows), jnp.bfloat16),
                ],
                scratch_shapes=scratch,
                **kinds,
            )(*pieces, pick, *weights)
        return pl.pallas_call(
            functools.partial(
                last_kernel, count=len(pieces), earlier=len(held) // 2, tok_dev=tok_dev
            ),
            out_specs=pl.BlockSpec(memory_space=pl.ANY),
            out_shape=jax.ShapeDtypeStruct((2 * half, model_dim), jnp.float32),
            scratch_shapes=[pltpu.VMEM((rows, model_dim), jnp.bfloat16)]
            + scratch
            + [
                pltpu.VMEM((2 * half, rows), jnp.bfloat16),
                pltpu.VMEM((2 * half, model_dim), jnp.float32),
                pltpu.SemaphoreType.DMA((model_dim // 512,)),
            ],
            **kinds,
        )(*pieces, *held, pick, *weights)

    near = swap(own, (Z_NEAR, Z_NEAR))
    middle = swap(own, (Z_NEAR ^ Z_FAR, Z_NEAR ^ Z_FAR))
    chip_a = share([own])
    pieces_a, onward_a = cross(chip_a)
    near, middle, _ = lax.optimization_barrier((near, middle, onward_a))
    far = swap(after(own, near), (Z_FAR, Z_FAR))
    chip_b = share([near, middle], pieces_a[2])
    pieces_a[0] = after(pieces_a[0], chip_b)
    held_a = call(pieces_a, [], False)
    chip_c = share([after(far, held_a[1])])
    pieces_b, onward_b = cross(chip_b, chip_c)
    pieces_c, onward_c = cross(chip_c, onward_b)
    pieces_b[0] = after(pieces_b[0], onward_c)
    held_b = call(pieces_b, [], False)
    out = call(pieces_c, [*held_a, *held_b], True)
    return out.reshape(1, 2, half, model_dim)


def local(tokens, cotangent, routes, combine, w_in, w_out, v_in):
    experts = lax.axis_size("expert") * w_in.shape[0]
    tok_dev, top_k = routes.shape
    sizes = (lax.axis_size("dp"), lax.axis_size("expert"))
    if sizes == (2, 16) and w_in.shape[0] == 1 and 2 * tok_dev * top_k // experts >= tok_dev:
        return dense(tokens, cotangent, routes, combine, w_in, w_out, v_in)
    return dispatched(tokens, cotangent, routes, combine, w_in, w_out, v_in)


def solution(mesh):
    in_specs = (
        P(("dp", "expert"), None),
        P(("dp", "expert"), None),
        P(("dp", "expert"), None),
        P(("dp", "expert"), None),
        P("expert", None, "dp", None),
        P("expert", "dp", None),
        P("expert", None, "dp", None),
    )
    out_specs = P("expert", None, "dp", None)
    return jax.shard_map(local, mesh=mesh, in_specs=in_specs, out_specs=out_specs, check_vma=False)
```

```python
import functools

import jax
import jax.numpy as jnp
from jax import lax
from jax.experimental import pallas as pl
from jax.experimental.pallas import tpu as pltpu
from jax.sharding import PartitionSpec as P

NT = (((1,), (1,)), ((), ()))
NN = (((1,), (0,)), ((), ()))


def expert_terms(slot_rows, slot_grads, w_pair, v_pair, w_down):
    hidden_width = w_pair.shape[1]
    model_dim = w_pair.shape[2]
    stacked = jnp.concatenate([w_pair, v_pair], axis=0).reshape(4 * hidden_width, model_dim)
    projected = lax.dot_general(slot_rows, stacked, NT, preferred_element_type=jnp.float32)
    pre_gate = projected[:, :hidden_width]
    pre_up = projected[:, hidden_width : 2 * hidden_width]
    tan_gate = projected[:, 2 * hidden_width : 3 * hidden_width]
    tan_up = projected[:, 3 * hidden_width :]
    back_grad = lax.dot_general(slot_grads, w_down, NT, preferred_element_type=jnp.float32)
    gate_dir, up_dir = directions(pre_gate, pre_up, tan_gate, tan_up, back_grad)
    gate_term = lax.dot_general(
        gate_dir, slot_rows, (((0,), (0,)), ((), ())), preferred_element_type=jnp.float32
    )
    up_term = lax.dot_general(
        up_dir, slot_rows, (((0,), (0,)), ((), ())), preferred_element_type=jnp.float32
    )
    return jnp.stack([gate_term, up_term], axis=0)


def directions(pre_gate, pre_up, tan_gate, tan_up, back_grad):
    gate_sig = jax.nn.sigmoid(pre_gate)
    first_deriv = gate_sig * (1.0 + pre_gate * (1.0 - gate_sig))
    second_deriv = gate_sig * (1.0 - gate_sig) * (2.0 + pre_gate * (1.0 - 2.0 * gate_sig))
    gate_dir = back_grad * (tan_up * first_deriv + pre_up * second_deriv * tan_gate)
    up_dir = back_grad * first_deriv * tan_gate
    return gate_dir.astype(jnp.bfloat16), up_dir.astype(jnp.bfloat16)


def dispatched(tokens, cotangent, routes, combine, w_in, w_out, v_in):
    n_expert = lax.axis_size("expert")
    exp_dev = w_in.shape[0]
    experts = n_expert * exp_dev
    tok_dev, top_k = routes.shape
    model_dim = tokens.shape[1]
    capacity = 2 * tok_dev * top_k // experts
    pair_count = tok_dev * top_k
    slot_count = n_expert * capacity
    flat_routes = routes.reshape(pair_count)
    onehot = (flat_routes[:, None] == jnp.arange(experts, dtype=jnp.int32)[None, :]).astype(
        jnp.int32
    )
    earlier = jnp.cumsum(onehot, axis=0) - onehot
    slot_rank = jnp.sum(earlier * onehot, axis=1)
    position = flat_routes * capacity + slot_rank
    slot_table = jnp.full((experts * capacity,), pair_count, jnp.int32)
    slot_table = slot_table.at[position].set(jnp.arange(pair_count, dtype=jnp.int32))
    token_index = slot_table // top_k
    padded_tokens = jnp.concatenate([tokens, jnp.zeros((1, model_dim), jnp.bfloat16)], axis=0)
    scaled = (combine[:, :, None] * cotangent[:, None, :].astype(jnp.float32)).astype(jnp.bfloat16)
    padded_scaled = jnp.concatenate(
        [scaled.reshape(pair_count, model_dim), jnp.zeros((1, model_dim), jnp.bfloat16)], axis=0
    )
    send_rows = padded_tokens[token_index].reshape(n_expert, exp_dev * capacity, model_dim)
    send_grads = padded_scaled[slot_table].reshape(n_expert, exp_dev * capacity, model_dim)
    recv_rows = lax.all_to_all(send_rows, "expert", split_axis=0, concat_axis=0, tiled=True)
    recv_grads = lax.all_to_all(send_grads, "expert", split_axis=0, concat_axis=0, tiled=True)

    def regroup(received):
        shaped = received.reshape(n_expert, exp_dev, capacity, model_dim)
        return jnp.transpose(shaped, (1, 0, 2, 3)).reshape(exp_dev, slot_count, model_dim)

    local_rows = regroup(recv_rows)
    local_grads = regroup(recv_grads)
    batched_terms = jax.vmap(expert_terms)
    pair_piece, probe_piece, down_piece = lax.all_gather(
        (w_in, v_in, w_out[:, None]), "dp", axis=2, tiled=True
    )
    partials = batched_terms(local_rows, local_grads, pair_piece, probe_piece, down_piece[:, 0])
    return lax.psum_scatter(
        partials.astype(jnp.bfloat16), "dp", scatter_dimension=2, tiled=True
    ).astype(jnp.float32)


CORE, X, Y = 1, 2, 16
Z_NEAR, Z_FAR = 4, 8
LANES = 128


def pack_kernel(tok_ref, cot_ref, route_ref, comb_ref, out_ref, *, experts):
    tok_dev, model_dim = tok_ref.shape
    out_ref[0:tok_dev, 0:model_dim] = tok_ref[...]
    out_ref[tok_dev:, 0:model_dim] = cot_ref[...]
    line = lax.broadcasted_iota(jnp.int32, (LANES, tok_dev), 0)
    weight = jnp.zeros((LANES, tok_dev), jnp.float32)
    for k in range(route_ref.shape[0]):
        named = route_ref[k : k + 1, :] == line % experts
        weight = jnp.where(named, comb_ref[k : k + 1, :], weight)
    high = weight.astype(jnp.bfloat16).astype(jnp.float32)
    middle = (weight - high).astype(jnp.bfloat16).astype(jnp.float32)
    low = weight - high - middle
    part = line // experts
    zero = jnp.zeros_like(weight)
    value = jnp.where(part == 0, high, jnp.where(part == 1, middle, jnp.where(part == 2, low, zero)))
    row = lax.broadcasted_iota(jnp.int32, (tok_dev, tok_dev), 0)
    column = lax.broadcasted_iota(jnp.int32, (tok_dev, tok_dev), 1)
    same = (row == column).astype(jnp.float32).astype(jnp.bfloat16)
    turned = lax.dot_general(
        same, value.astype(jnp.bfloat16), NT, preferred_element_type=jnp.float32
    )
    out_ref[0:tok_dev, model_dim:] = turned.astype(jnp.bfloat16)
    out_ref[tok_dev:, model_dim:] = jnp.zeros((tok_dev, LANES), jnp.bfloat16)


def unpack(pieces, x_ref, c_ref, wt_ref, tok_dev):
    model_dim = x_ref.shape[1]
    row = 0
    for piece in pieces:
        for first in range(0, piece.shape[0], 2 * tok_dev):
            at = pl.ds(row, tok_dev)
            x_ref[at, :] = piece[first : first + tok_dev, 0:model_dim]
            wt_ref[at, :] = piece[first : first + tok_dev, model_dim:]
            c_ref[at, :] = piece[first + tok_dev : first + 2 * tok_dev, 0:model_dim]
            row += tok_dev


def gather_kernel(*refs):
    *parts, out_ref, sems = refs
    row, copies = 0, []
    for n, part in enumerate(parts):
        copies.append(
            pltpu.make_async_copy(part, out_ref.at[pl.ds(row, part.shape[0])], sems.at[n])
        )
        row += part.shape[0]
    for copy in copies:
        copy.start()
    for copy in copies:
        copy.wait()


def unit_dirs(weight, all_ref, x_ref, c_ref, dir_ref):
    half = all_ref.shape[0] // 5
    seen = lax.dot_general(
        all_ref[0 : 4 * half], x_ref[...], NT, preferred_element_type=jnp.float32
    )
    back = lax.dot_general(
        all_ref[4 * half :], c_ref[...], NT, preferred_element_type=jnp.float32
    )
    parts = [seen[n * half : (n + 1) * half] for n in range(4)]
    gate_dir, up_dir = directions(*parts, back * weight)
    dir_ref[0:half, :] = gate_dir
    dir_ref[half:, :] = up_dir


def route_weights(pick_ref, wt_ref):
    return lax.dot_general(pick_ref[...], wt_ref[...], NT, preferred_element_type=jnp.float32)


def both_kernel(*refs, count, tok_dev):
    pieces = refs[:count]
    pick_ref, mine, other, x_ref, dir_ref, sum_ref, c_ref, wt_ref, other_ref = refs[count:]
    unpack(pieces, x_ref, c_ref, wt_ref, tok_dev)
    weight = route_weights(pick_ref, wt_ref)
    unit_dirs(weight[8:9], other, x_ref, c_ref, other_ref)
    columns = 512
    for n in range(x_ref.shape[1] // columns):
        at = pl.ds(n * columns, columns)
        sum_ref[:, at] = lax.dot_general(
            other_ref[...], x_ref[:, at], NN, preferred_element_type=jnp.float32
        ).astype(jnp.bfloat16)
    unit_dirs(weight[0:1], mine, x_ref, c_ref, dir_ref)


def last_kernel(*refs, count, tok_dev):
    pieces = refs[:count]
    early_x, early_dir, add_ref, pick_ref, mine, out_ref = refs[count : count + 6]
    x_ref, c_ref, wt_ref, dir_ref, sum_ref, sems = refs[count + 6 :]
    unpack(pieces, x_ref, c_ref, wt_ref, tok_dev)
    weight = route_weights(pick_ref, wt_ref)
    unit_dirs(weight[0:1], mine, x_ref, c_ref, dir_ref)
    columns = 512
    copies = []
    for n in range(out_ref.shape[1] // columns):
        at = pl.ds(n * columns, columns)
        rows = jnp.concatenate([early_x[:, at], x_ref[:, at]], axis=0)
        dirs = jnp.concatenate([early_dir[...], dir_ref[...]], axis=1)
        total = lax.dot_general(dirs, rows, NN, preferred_element_type=jnp.float32)
        sum_ref[:, at] = total + add_ref[:, at].astype(jnp.float32)
        copy = pltpu.make_async_copy(sum_ref.at[:, at], out_ref.at[:, at], sems.at[n])
        copy.start()
        copies.append(copy)
    for copy in copies:
        copy.wait()


def swap(value, mask):
    axes = ("dp", "expert")
    count = lax.axis_size("dp") * lax.axis_size("expert")
    return lax.ppermute(value, axes, [(i, i ^ mask) for i in range(count)])


def after(value, *others):
    return lax.optimization_barrier((value, *others))[0]


def tied(values, *others):
    return list(lax.optimization_barrier((*values, *others)))[: len(values)]


def dense(tokens, cotangent, routes, combine, w_in, w_out, v_in):
    experts = lax.axis_size("expert")
    tok_dev, model_dim = tokens.shape
    half = w_in.shape[2]
    wide = model_dim + LANES
    inside = pl.BlockSpec(memory_space=pltpu.VMEM)
    own = pl.pallas_call(
        functools.partial(pack_kernel, experts=experts),
        in_specs=[inside] * 4,
        out_specs=inside,
        out_shape=jax.ShapeDtypeStruct((2 * tok_dev, wide), jnp.bfloat16),
    )(tokens, cotangent, routes.T, combine.T)

    lane = jnp.arange(LANES, dtype=jnp.int32)[None, :]
    line = jnp.arange(16, dtype=jnp.int32)[:, None]
    expert = lax.axis_index("expert")
    wanted = jnp.where(line < 8, expert, expert ^ CORE)
    pick = ((lane % experts == wanted) & (lane < 3 * experts)).astype(jnp.bfloat16)
    shards = (
        w_in.reshape(2 * half, model_dim),
        v_in.reshape(2 * half, model_dim),
        w_out.reshape(half, model_dim),
    )
    outside = pl.BlockSpec(memory_space=pl.ANY)
    mine = pl.pallas_call(
        gather_kernel,
        in_specs=[outside] * 3,
        out_specs=outside,
        out_shape=jax.ShapeDtypeStruct((5 * half, model_dim), jnp.bfloat16),
        scratch_shapes=[pltpu.SemaphoreType.DMA((3,))],
        cost_estimate=pl.CostEstimate(flops=0, bytes_accessed=10 * 2**20, transcendentals=0),
    )(*shards)

    first = [swap(own, m) for m in (Z_NEAR, X, Y, Z_NEAR ^ Z_FAR, X ^ Y)]
    near, beside_x, beside_y, middle, across, again, mine = tied([*first, own, mine])

    pair = jnp.concatenate([near, middle], axis=0)
    second = [swap(again, Z_FAR), swap(pair, X), swap(pair, Y), swap(across, Z_NEAR)]
    far, pair_x, pair_y, near_across, other = tied([*second, swap(mine, CORE)])

    third = [swap(far, m) for m in (X, Y, X ^ Y)] + [swap(after(across, far), Z_NEAR ^ Z_FAR)]
    pieces = [own, beside_x, beside_y, across, pair, pair_x, pair_y, near_across, far]
    rows = sum(p.shape[0] for p in pieces) // 2
    early_x, early_dir, partial = pl.pallas_call(
        functools.partial(both_kernel, count=len(pieces), tok_dev=tok_dev),
        in_specs=[inside] * (len(pieces) + 3),
        out_specs=[inside] * 3,
        out_shape=[
            jax.ShapeDtypeStruct((rows, model_dim), jnp.bfloat16),
            jax.ShapeDtypeStruct((2 * half, rows), jnp.bfloat16),
            jax.ShapeDtypeStruct((2 * half, model_dim), jnp.bfloat16),
        ],
        scratch_shapes=[
            pltpu.VMEM((rows, model_dim), jnp.bfloat16),
            pltpu.VMEM((rows, LANES), jnp.bfloat16),
            pltpu.VMEM((2 * half, rows), jnp.bfloat16),
        ],
        compiler_params=pltpu.CompilerParams(vmem_limit_bytes=14 * 2**20),
        cost_estimate=pl.CostEstimate(
            flops=2 * rows * model_dim * 12 * half,
            bytes_accessed=16 * 2**20,
            transcendentals=2 * rows * half,
        ),
    )(*pieces, pick, mine, other)
    partial = swap(after(partial, *third), CORE)

    blocks = third + [swap(after(block, early_dir), CORE) for block in third]
    rows = sum(p.shape[0] for p in blocks) // 2
    out = pl.pallas_call(
        functools.partial(last_kernel, count=len(blocks), tok_dev=tok_dev),
        in_specs=[inside] * (len(blocks) + 5),
        out_specs=pl.BlockSpec(memory_space=pl.ANY),
        out_shape=jax.ShapeDtypeStruct((2 * half, model_dim), jnp.float32),
        scratch_shapes=[
            pltpu.VMEM((rows, model_dim), jnp.bfloat16),
            pltpu.VMEM((rows, model_dim), jnp.bfloat16),
            pltpu.VMEM((rows, LANES), jnp.bfloat16),
            pltpu.VMEM((2 * half, rows), jnp.bfloat16),
            pltpu.VMEM((2 * half, model_dim), jnp.float32),
            pltpu.SemaphoreType.DMA((model_dim // 512,)),
        ],
        compiler_params=pltpu.CompilerParams(vmem_limit_bytes=14 * 2**20),
        cost_estimate=pl.CostEstimate(
            flops=2 * rows * model_dim * 10 * half,
            bytes_accessed=16 * 2**20,
            transcendentals=rows * half,
        ),
    )(*blocks, early_x, early_dir, partial, pick, mine)
    return out.reshape(1, 2, half, model_dim)


def local(tokens, cotangent, routes, combine, w_in, w_out, v_in):
    experts = lax.axis_size("expert") * w_in.shape[0]
    tok_dev, top_k = routes.shape
    sizes = (lax.axis_size("dp"), lax.axis_size("expert"))
    if sizes == (2, 16) and w_in.shape[0] == 1 and 2 * tok_dev * top_k // experts >= tok_dev:
        return dense(tokens, cotangent, routes, combine, w_in, w_out, v_in)
    return dispatched(tokens, cotangent, routes, combine, w_in, w_out, v_in)


def solution(mesh):
    in_specs = (
        P(("dp", "expert"), None),
        P(("dp", "expert"), None),
        P(("dp", "expert"), None),
        P(("dp", "expert"), None),
        P("expert", None, "dp", None),
        P("expert", "dp", None),
        P("expert", None, "dp", None),
    )
    out_specs = P("expert", None, "dp", None)
    return jax.shard_map(local, mesh=mesh, in_specs=in_specs, out_specs=out_specs, check_vma=False)
```

```python
import functools

import jax
import jax.numpy as jnp
from jax import lax
from jax.experimental import pallas as pl
from jax.experimental.pallas import tpu as pltpu
from jax.sharding import PartitionSpec as P

NT = (((1,), (1,)), ((), ()))
NN = (((1,), (0,)), ((), ()))


def expert_terms(slot_rows, slot_grads, w_pair, v_pair, w_down):
    hidden_width = w_pair.shape[1]
    model_dim = w_pair.shape[2]
    stacked = jnp.concatenate([w_pair, v_pair], axis=0).reshape(4 * hidden_width, model_dim)
    projected = lax.dot_general(slot_rows, stacked, NT, preferred_element_type=jnp.float32)
    pre_gate = projected[:, :hidden_width]
    pre_up = projected[:, hidden_width : 2 * hidden_width]
    tan_gate = projected[:, 2 * hidden_width : 3 * hidden_width]
    tan_up = projected[:, 3 * hidden_width :]
    back_grad = lax.dot_general(slot_grads, w_down, NT, preferred_element_type=jnp.float32)
    gate_dir, up_dir = directions(pre_gate, pre_up, tan_gate, tan_up, back_grad)
    gate_term = lax.dot_general(
        gate_dir, slot_rows, (((0,), (0,)), ((), ())), preferred_element_type=jnp.float32
    )
    up_term = lax.dot_general(
        up_dir, slot_rows, (((0,), (0,)), ((), ())), preferred_element_type=jnp.float32
    )
    return jnp.stack([gate_term, up_term], axis=0)


def directions(pre_gate, pre_up, tan_gate, tan_up, back_grad):
    gate_sig = jax.nn.sigmoid(pre_gate)
    first_deriv = gate_sig * (1.0 + pre_gate * (1.0 - gate_sig))
    second_deriv = gate_sig * (1.0 - gate_sig) * (2.0 + pre_gate * (1.0 - 2.0 * gate_sig))
    gate_dir = back_grad * (tan_up * first_deriv + pre_up * second_deriv * tan_gate)
    up_dir = back_grad * first_deriv * tan_gate
    return gate_dir.astype(jnp.bfloat16), up_dir.astype(jnp.bfloat16)


def dispatched(tokens, cotangent, routes, combine, w_in, w_out, v_in):
    n_expert = lax.axis_size("expert")
    exp_dev = w_in.shape[0]
    experts = n_expert * exp_dev
    tok_dev, top_k = routes.shape
    model_dim = tokens.shape[1]
    capacity = 2 * tok_dev * top_k // experts
    pair_count = tok_dev * top_k
    slot_count = n_expert * capacity
    flat_routes = routes.reshape(pair_count)
    onehot = (flat_routes[:, None] == jnp.arange(experts, dtype=jnp.int32)[None, :]).astype(
        jnp.int32
    )
    earlier = jnp.cumsum(onehot, axis=0) - onehot
    slot_rank = jnp.sum(earlier * onehot, axis=1)
    position = flat_routes * capacity + slot_rank
    slot_table = jnp.full((experts * capacity,), pair_count, jnp.int32)
    slot_table = slot_table.at[position].set(jnp.arange(pair_count, dtype=jnp.int32))
    token_index = slot_table // top_k
    padded_tokens = jnp.concatenate([tokens, jnp.zeros((1, model_dim), jnp.bfloat16)], axis=0)
    scaled = (combine[:, :, None] * cotangent[:, None, :].astype(jnp.float32)).astype(jnp.bfloat16)
    padded_scaled = jnp.concatenate(
        [scaled.reshape(pair_count, model_dim), jnp.zeros((1, model_dim), jnp.bfloat16)], axis=0
    )
    send_rows = padded_tokens[token_index].reshape(n_expert, exp_dev * capacity, model_dim)
    send_grads = padded_scaled[slot_table].reshape(n_expert, exp_dev * capacity, model_dim)
    recv_rows = lax.all_to_all(send_rows, "expert", split_axis=0, concat_axis=0, tiled=True)
    recv_grads = lax.all_to_all(send_grads, "expert", split_axis=0, concat_axis=0, tiled=True)

    def regroup(received):
        shaped = received.reshape(n_expert, exp_dev, capacity, model_dim)
        return jnp.transpose(shaped, (1, 0, 2, 3)).reshape(exp_dev, slot_count, model_dim)

    local_rows = regroup(recv_rows)
    local_grads = regroup(recv_grads)
    batched_terms = jax.vmap(expert_terms)
    pair_piece, probe_piece, down_piece = lax.all_gather(
        (w_in, v_in, w_out[:, None]), "dp", axis=2, tiled=True
    )
    partials = batched_terms(local_rows, local_grads, pair_piece, probe_piece, down_piece[:, 0])
    return lax.psum_scatter(
        partials.astype(jnp.bfloat16), "dp", scatter_dimension=2, tiled=True
    ).astype(jnp.float32)


CORE, X, Y = 1, 2, 16
Z_NEAR, Z_FAR = 4, 8
LANES = 128


def pack_kernel(tok_ref, cot_ref, route_ref, comb_ref, out_ref, *, experts):
    tok_dev, model_dim = tok_ref.shape
    out_ref[0:tok_dev, 0:model_dim] = tok_ref[...]
    out_ref[tok_dev:, 0:model_dim] = cot_ref[...]
    line = lax.broadcasted_iota(jnp.int32, (LANES, tok_dev), 0)
    weight = jnp.zeros((LANES, tok_dev), jnp.float32)
    for k in range(route_ref.shape[0]):
        named = route_ref[k : k + 1, :] == line % experts
        weight = jnp.where(named, comb_ref[k : k + 1, :], weight)
    high = weight.astype(jnp.bfloat16).astype(jnp.float32)
    middle = (weight - high).astype(jnp.bfloat16).astype(jnp.float32)
    low = weight - high - middle
    part = line // experts
    zero = jnp.zeros_like(weight)
    value = jnp.where(part == 0, high, jnp.where(part == 1, middle, jnp.where(part == 2, low, zero)))
    row = lax.broadcasted_iota(jnp.int32, (tok_dev, tok_dev), 0)
    column = lax.broadcasted_iota(jnp.int32, (tok_dev, tok_dev), 1)
    same = (row == column).astype(jnp.float32).astype(jnp.bfloat16)
    turned = lax.dot_general(
        same, value.astype(jnp.bfloat16), NT, preferred_element_type=jnp.float32
    )
    out_ref[0:tok_dev, model_dim:] = turned.astype(jnp.bfloat16)
    out_ref[tok_dev:, model_dim:] = jnp.zeros((tok_dev, LANES), jnp.bfloat16)


def unpack(pieces, x_ref, c_ref, wt_ref, tok_dev):
    model_dim = x_ref.shape[1]
    row = 0
    for piece in pieces:
        for first in range(0, piece.shape[0], 2 * tok_dev):
            at = pl.ds(row, tok_dev)
            x_ref[at, :] = piece[first : first + tok_dev, 0:model_dim]
            wt_ref[at, :] = piece[first : first + tok_dev, model_dim:]
            c_ref[at, :] = piece[first + tok_dev : first + 2 * tok_dev, 0:model_dim]
            row += tok_dev


def unit_dirs(weight, w_ref, v_ref, wo_ref, x_ref, c_ref, dir_ref):
    half = wo_ref.shape[0]
    both = jnp.concatenate([w_ref[...], v_ref[...]], axis=0)
    seen = lax.dot_general(both, x_ref[...], NT, preferred_element_type=jnp.float32)
    back = lax.dot_general(wo_ref[...], c_ref[...], NT, preferred_element_type=jnp.float32)
    parts = [seen[n * half : (n + 1) * half] for n in range(4)]
    gate_dir, up_dir = directions(*parts, back * weight)
    dir_ref[0:half, :] = gate_dir
    dir_ref[half:, :] = up_dir


def rows_to_dirs(stacks, pick_ref, shards, x_ref, c_ref, wt_ref, dir_ref, tok_dev):
    unpack(stacks, x_ref, c_ref, wt_ref, tok_dev)
    weight = lax.dot_general(pick_ref[...], wt_ref[...], NT, preferred_element_type=jnp.float32)
    unit_dirs(weight[0:1], *shards, x_ref, c_ref, dir_ref)


def first_kernel(mine, theirs, pick_ref, w, v, wo, x_ref, dir_ref, c_ref, wt_ref, *, tok_dev):
    rows_to_dirs((mine, theirs), pick_ref, (w, v, wo), x_ref, c_ref, wt_ref, dir_ref, tok_dev)


COLUMNS = 512


def second_kernel(
    mine, theirs, pick_ref, w, v, wo, early_x, early_dir, sum_ref, x_ref, dir_ref, c_ref, wt_ref,
    *, tok_dev
):
    rows_to_dirs((mine, theirs), pick_ref, (w, v, wo), x_ref, c_ref, wt_ref, dir_ref, tok_dev)
    dirs = jnp.concatenate([early_dir[...], dir_ref[...]], axis=1)
    for n in range(sum_ref.shape[1] // COLUMNS):
        at = pl.ds(n * COLUMNS, COLUMNS)
        rows = jnp.concatenate([early_x[:, at], x_ref[:, at]], axis=0)
        sum_ref[:, at] = lax.dot_general(dirs, rows, NN, preferred_element_type=jnp.float32)


def last_kernel(
    mine, theirs, pick_ref, w, v, wo, add_ref, out_ref, x_ref, dir_ref, c_ref, wt_ref, sum_ref, sems,
    *, tok_dev
):
    rows_to_dirs((mine, theirs), pick_ref, (w, v, wo), x_ref, c_ref, wt_ref, dir_ref, tok_dev)
    copies = []
    for n in range(out_ref.shape[1] // COLUMNS):
        at = pl.ds(n * COLUMNS, COLUMNS)
        total = lax.dot_general(
            dir_ref[...], x_ref[:, at], NN, preferred_element_type=jnp.float32
        )
        sum_ref[:, at] = total + add_ref[:, at]
        copy = pltpu.make_async_copy(sum_ref.at[:, at], out_ref.at[:, at], sems.at[n])
        copy.start()
        copies.append(copy)
    for copy in copies:
        copy.wait()


def swap(value, mask, sender=None):
    axes = ("dp", "expert")
    count = lax.axis_size("dp") * lax.axis_size("expert")
    pairs = [(i, i ^ mask) for i in range(count) if sender is None or sender(i)]
    return lax.ppermute(value, axes, pairs)


def inner(place):
    return (place & Z_NEAR) // Z_NEAR != (place & Z_FAR) // Z_FAR


def after(value, *others):
    return lax.optimization_barrier((value, *others))[0]


def tied(values, *others):
    return list(lax.optimization_barrier((*values, *others)))[: len(values)]


def dense(tokens, cotangent, routes, combine, w_in, w_out, v_in):
    experts = lax.axis_size("expert")
    tok_dev, model_dim = tokens.shape
    half = w_in.shape[2]
    wide = model_dim + LANES
    inside = pl.BlockSpec(memory_space=pltpu.VMEM)
    own = pl.pallas_call(
        functools.partial(pack_kernel, experts=experts),
        in_specs=[inside] * 4,
        out_specs=inside,
        out_shape=jax.ShapeDtypeStruct((2 * tok_dev, wide), jnp.bfloat16),
    )(tokens, cotangent, routes.T, combine.T)

    lane = jnp.arange(LANES, dtype=jnp.int32)[None, :]
    expert = lax.axis_index("expert")
    pick = ((lane % experts == expert) & (lane < 3 * experts)).astype(jnp.bfloat16)
    pick = jnp.broadcast_to(pick, (16, LANES))
    is_inner = inner(expert)
    shards = (
        w_in.reshape(2 * half, model_dim),
        v_in.reshape(2 * half, model_dim),
        w_out.reshape(half, model_dim),
    )

    def call(kernel, stack, theirs, more, outs, scratch):
        rows = stack.shape[0]
        operands = (stack, theirs, pick, *shards, *more)
        held = [
            ((rows, model_dim), jnp.bfloat16),
            ((2 * half, rows), jnp.bfloat16),
            ((rows, model_dim), jnp.bfloat16),
            ((rows, LANES), jnp.bfloat16),
        ]
        if outs is None:
            outs, held = held[:2], held[2:]
            out_specs = [inside] * 2
        else:
            out_specs = [inside if outs[1] else pl.BlockSpec(memory_space=pl.ANY)]
            outs = [((2 * half, model_dim), jnp.float32)]
        return pl.pallas_call(
            functools.partial(kernel, tok_dev=tok_dev),
            in_specs=[inside] * len(operands),
            out_specs=out_specs,
            out_shape=[jax.ShapeDtypeStruct(*o) for o in outs],
            scratch_shapes=[pltpu.VMEM(*h) for h in held] + scratch,
            compiler_params=pltpu.CompilerParams(vmem_limit_bytes=14 * 2**20),
            cost_estimate=pl.CostEstimate(
                flops=2 * rows * model_dim * 7 * half,
                bytes_accessed=12 * 2**20,
                transcendentals=rows * half,
            ),
        )(*operands)

    stacked = functools.partial(jnp.concatenate, axis=0)
    block = 2 * tok_dev
    first = [swap(own, m) for m in (Z_NEAR, X, Y, Z_NEAR ^ Z_FAR, X ^ Y)]
    near, beside_x, beside_y, middle, across = tied(first)

    pair = stacked([near, middle])
    stack_a = stacked([own, beside_x, beside_y, across])
    outward = swap(stacked([middle, across]), Z_NEAR)
    through = swap(stacked([near, across]), Z_NEAR ^ Z_FAR, inner)
    pair_x, pair_y = swap(pair, X), swap(pair, Y)
    early = call(first_kernel, stack_a, swap(stack_a, CORE), (), None, [])
    outward, through, pair_x, pair_y, *early = tied([outward, through, pair_x, pair_y, *early])

    far = jnp.where(is_inner, through[:block], outward[:block])
    stack_b = stacked([pair, pair_x, pair_y, outward[block:], far])
    third = [swap(far, X), swap(far, Y), swap(jnp.where(is_inner, far, middle), X ^ Y)]
    relayed = swap(through[block:], Z_NEAR, inner)
    (total,) = call(second_kernel, stack_b, swap(stack_b, CORE), early, (0, True), [])
    *third, relayed, total = tied([*third, relayed, total])

    stack_c = stacked([*third, jnp.where(is_inner, through[block:], relayed)])
    scratch = [
        pltpu.VMEM((2 * half, model_dim), jnp.float32),
        pltpu.SemaphoreType.DMA((model_dim // COLUMNS,)),
    ]
    (out,) = call(last_kernel, stack_c, swap(stack_c, CORE), (total,), (0, False), scratch)
    return out.reshape(1, 2, half, model_dim)


def local(tokens, cotangent, routes, combine, w_in, w_out, v_in):
    experts = lax.axis_size("expert") * w_in.shape[0]
    tok_dev, top_k = routes.shape
    sizes = (lax.axis_size("dp"), lax.axis_size("expert"))
    if sizes == (2, 16) and w_in.shape[0] == 1 and 2 * tok_dev * top_k // experts >= tok_dev:
        return dense(tokens, cotangent, routes, combine, w_in, w_out, v_in)
    return dispatched(tokens, cotangent, routes, combine, w_in, w_out, v_in)


def solution(mesh):
    in_specs = (
        P(("dp", "expert"), None),
        P(("dp", "expert"), None),
        P(("dp", "expert"), None),
        P(("dp", "expert"), None),
        P("expert", None, "dp", None),
        P("expert", "dp", None),
        P("expert", None, "dp", None),
    )
    out_specs = P("expert", None, "dp", None)
    return jax.shard_map(local, mesh=mesh, in_specs=in_specs, out_specs=out_specs, check_vma=False)
```

```python
import functools

import jax
import jax.numpy as jnp
from jax import lax
from jax.experimental import pallas as pl
from jax.experimental.pallas import tpu as pltpu
from jax.sharding import PartitionSpec as P

NT = (((1,), (1,)), ((), ()))
NN = (((1,), (0,)), ((), ()))


def expert_terms(slot_rows, slot_grads, w_pair, v_pair, w_down):
    hidden_width = w_pair.shape[1]
    model_dim = w_pair.shape[2]
    stacked = jnp.concatenate([w_pair, v_pair], axis=0).reshape(4 * hidden_width, model_dim)
    projected = lax.dot_general(slot_rows, stacked, NT, preferred_element_type=jnp.float32)
    pre_gate = projected[:, :hidden_width]
    pre_up = projected[:, hidden_width : 2 * hidden_width]
    tan_gate = projected[:, 2 * hidden_width : 3 * hidden_width]
    tan_up = projected[:, 3 * hidden_width :]
    back_grad = lax.dot_general(slot_grads, w_down, NT, preferred_element_type=jnp.float32)
    gate_dir, up_dir = directions(pre_gate, pre_up, tan_gate, tan_up, back_grad)
    gate_term = lax.dot_general(
        gate_dir, slot_rows, (((0,), (0,)), ((), ())), preferred_element_type=jnp.float32
    )
    up_term = lax.dot_general(
        up_dir, slot_rows, (((0,), (0,)), ((), ())), preferred_element_type=jnp.float32
    )
    return jnp.stack([gate_term, up_term], axis=0)


def directions(pre_gate, pre_up, tan_gate, tan_up, back_grad):
    gate_sig = jax.nn.sigmoid(pre_gate)
    first_deriv = gate_sig * (1.0 + pre_gate * (1.0 - gate_sig))
    second_deriv = gate_sig * (1.0 - gate_sig) * (2.0 + pre_gate * (1.0 - 2.0 * gate_sig))
    gate_dir = back_grad * (tan_up * first_deriv + pre_up * second_deriv * tan_gate)
    up_dir = back_grad * first_deriv * tan_gate
    return gate_dir.astype(jnp.bfloat16), up_dir.astype(jnp.bfloat16)


def dispatched(tokens, cotangent, routes, combine, w_in, w_out, v_in):
    n_expert = lax.axis_size("expert")
    exp_dev = w_in.shape[0]
    experts = n_expert * exp_dev
    tok_dev, top_k = routes.shape
    model_dim = tokens.shape[1]
    capacity = 2 * tok_dev * top_k // experts
    pair_count = tok_dev * top_k
    slot_count = n_expert * capacity
    flat_routes = routes.reshape(pair_count)
    onehot = (flat_routes[:, None] == jnp.arange(experts, dtype=jnp.int32)[None, :]).astype(
        jnp.int32
    )
    earlier = jnp.cumsum(onehot, axis=0) - onehot
    slot_rank = jnp.sum(earlier * onehot, axis=1)
    position = flat_routes * capacity + slot_rank
    slot_table = jnp.full((experts * capacity,), pair_count, jnp.int32)
    slot_table = slot_table.at[position].set(jnp.arange(pair_count, dtype=jnp.int32))
    token_index = slot_table // top_k
    padded_tokens = jnp.concatenate([tokens, jnp.zeros((1, model_dim), jnp.bfloat16)], axis=0)
    scaled = (combine[:, :, None] * cotangent[:, None, :].astype(jnp.float32)).astype(jnp.bfloat16)
    padded_scaled = jnp.concatenate(
        [scaled.reshape(pair_count, model_dim), jnp.zeros((1, model_dim), jnp.bfloat16)], axis=0
    )
    send_rows = padded_tokens[token_index].reshape(n_expert, exp_dev * capacity, model_dim)
    send_grads = padded_scaled[slot_table].reshape(n_expert, exp_dev * capacity, model_dim)
    recv_rows = lax.all_to_all(send_rows, "expert", split_axis=0, concat_axis=0, tiled=True)
    recv_grads = lax.all_to_all(send_grads, "expert", split_axis=0, concat_axis=0, tiled=True)

    def regroup(received):
        shaped = received.reshape(n_expert, exp_dev, capacity, model_dim)
        return jnp.transpose(shaped, (1, 0, 2, 3)).reshape(exp_dev, slot_count, model_dim)

    local_rows = regroup(recv_rows)
    local_grads = regroup(recv_grads)
    batched_terms = jax.vmap(expert_terms)
    pair_piece, probe_piece, down_piece = lax.all_gather(
        (w_in, v_in, w_out[:, None]), "dp", axis=2, tiled=True
    )
    partials = batched_terms(local_rows, local_grads, pair_piece, probe_piece, down_piece[:, 0])
    return lax.psum_scatter(
        partials.astype(jnp.bfloat16), "dp", scatter_dimension=2, tiled=True
    ).astype(jnp.float32)


CORE, X, Y = 1, 2, 16
Z_NEAR, Z_FAR = 4, 8
LANES = 128


def pack_kernel(tok_ref, cot_ref, route_ref, comb_ref, out_ref, *, experts):
    tok_dev, model_dim = tok_ref.shape
    out_ref[0:tok_dev, 0:model_dim] = tok_ref[...]
    out_ref[tok_dev:, 0:model_dim] = cot_ref[...]
    line = lax.broadcasted_iota(jnp.int32, (LANES, tok_dev), 0)
    weight = jnp.zeros((LANES, tok_dev), jnp.float32)
    for k in range(route_ref.shape[0]):
        named = route_ref[k : k + 1, :] == line % experts
        weight = jnp.where(named, comb_ref[k : k + 1, :], weight)
    high = weight.astype(jnp.bfloat16).astype(jnp.float32)
    middle = (weight - high).astype(jnp.bfloat16).astype(jnp.float32)
    low = weight - high - middle
    part = line // experts
    zero = jnp.zeros_like(weight)
    value = jnp.where(part == 0, high, jnp.where(part == 1, middle, jnp.where(part == 2, low, zero)))
    row = lax.broadcasted_iota(jnp.int32, (tok_dev, tok_dev), 0)
    column = lax.broadcasted_iota(jnp.int32, (tok_dev, tok_dev), 1)
    same = (row == column).astype(jnp.float32).astype(jnp.bfloat16)
    turned = lax.dot_general(
        same, value.astype(jnp.bfloat16), NT, preferred_element_type=jnp.float32
    )
    out_ref[0:tok_dev, model_dim:] = turned.astype(jnp.bfloat16)
    out_ref[tok_dev:, model_dim:] = jnp.zeros((tok_dev, LANES), jnp.bfloat16)


def stack_kernel(flag_ref, *refs, count, layouts):
    for out_ref, parts in zip(refs[count:], layouts):
        row = 0
        for part in parts:
            at = pl.ds(row, part[0][2] if isinstance(part[0], tuple) else part[2])
            if isinstance(part[0], tuple):
                for taken, (n, first, rows) in zip((1, 0), part):

                    @pl.when(flag_ref[0] == taken)
                    def _(n=n, first=first, rows=rows, at=at, out_ref=out_ref):
                        out_ref[at, :] = refs[n][first : first + rows]

            else:
                n, first, rows = part
                out_ref[at, :] = refs[n][first : first + rows]
            row += at.size


def unpack(pieces, x_ref, c_ref, wt_ref, tok_dev):
    model_dim = x_ref.shape[1]
    row = 0
    for piece in pieces:
        for first in range(0, piece.shape[0], 2 * tok_dev):
            at = pl.ds(row, tok_dev)
            x_ref[at, :] = piece[first : first + tok_dev, 0:model_dim]
            wt_ref[at, :] = piece[first : first + tok_dev, model_dim:]
            c_ref[at, :] = piece[first + tok_dev : first + 2 * tok_dev, 0:model_dim]
            row += tok_dev


def unit_dirs(weight, w_ref, v_ref, wo_ref, x_ref, c_ref, dir_ref):
    half = wo_ref.shape[0]
    both = jnp.concatenate([w_ref[...], v_ref[...]], axis=0)
    seen = lax.dot_general(both, x_ref[...], NT, preferred_element_type=jnp.float32)
    back = lax.dot_general(wo_ref[...], c_ref[...], NT, preferred_element_type=jnp.float32)
    parts = [seen[n * half : (n + 1) * half] for n in range(4)]
    gate_dir, up_dir = directions(*parts, back * weight)
    dir_ref[0:half, :] = gate_dir
    dir_ref[half:, :] = up_dir


def rows_to_dirs(stacks, pick_ref, shards, x_ref, c_ref, wt_ref, dir_ref, tok_dev):
    unpack(stacks, x_ref, c_ref, wt_ref, tok_dev)
    weight = lax.dot_general(pick_ref[...], wt_ref[...], NT, preferred_element_type=jnp.float32)
    unit_dirs(weight[0:1], *shards, x_ref, c_ref, dir_ref)


def first_kernel(mine, theirs, pick_ref, w, v, wo, x_ref, dir_ref, c_ref, wt_ref, *, tok_dev):
    rows_to_dirs((mine, theirs), pick_ref, (w, v, wo), x_ref, c_ref, wt_ref, dir_ref, tok_dev)


COLUMNS = 512


def second_kernel(
    mine, theirs, pick_ref, w, v, wo, early_x, early_dir, sum_ref, x_ref, dir_ref, c_ref, wt_ref,
    *, tok_dev
):
    rows_to_dirs((mine, theirs), pick_ref, (w, v, wo), x_ref, c_ref, wt_ref, dir_ref, tok_dev)
    dirs = jnp.concatenate([early_dir[...], dir_ref[...]], axis=1)
    for n in range(sum_ref.shape[1] // COLUMNS):
        at = pl.ds(n * COLUMNS, COLUMNS)
        rows = jnp.concatenate([early_x[:, at], x_ref[:, at]], axis=0)
        sum_ref[:, at] = lax.dot_general(dirs, rows, NN, preferred_element_type=jnp.float32)


def last_kernel(
    mine, theirs, pick_ref, w, v, wo, add_ref, out_ref, x_ref, dir_ref, c_ref, wt_ref, sum_ref, sems,
    *, tok_dev
):
    rows_to_dirs((mine, theirs), pick_ref, (w, v, wo), x_ref, c_ref, wt_ref, dir_ref, tok_dev)
    copies = []
    for n in range(out_ref.shape[1] // COLUMNS):
        at = pl.ds(n * COLUMNS, COLUMNS)
        total = lax.dot_general(
            dir_ref[...], x_ref[:, at], NN, preferred_element_type=jnp.float32
        )
        sum_ref[:, at] = total + add_ref[:, at]
        copy = pltpu.make_async_copy(sum_ref.at[:, at], out_ref.at[:, at], sems.at[n])
        copy.start()
        copies.append(copy)
    for copy in copies:
        copy.wait()


def swap(value, mask, sender=None):
    axes = ("dp", "expert")
    count = lax.axis_size("dp") * lax.axis_size("expert")
    pairs = [(i, i ^ mask) for i in range(count) if sender is None or sender(i)]
    return lax.ppermute(value, axes, pairs)


def inner(place):
    return (place & Z_NEAR) // Z_NEAR != (place & Z_FAR) // Z_FAR


def after(value, *others):
    return lax.optimization_barrier((value, *others))[0]


def tied(values, *others):
    return list(lax.optimization_barrier((*values, *others)))[: len(values)]


def dense(tokens, cotangent, routes, combine, w_in, w_out, v_in):
    experts = lax.axis_size("expert")
    tok_dev, model_dim = tokens.shape
    half = w_in.shape[2]
    wide = model_dim + LANES
    inside = pl.BlockSpec(memory_space=pltpu.VMEM)
    own = pl.pallas_call(
        functools.partial(pack_kernel, experts=experts),
        in_specs=[inside] * 4,
        out_specs=inside,
        out_shape=jax.ShapeDtypeStruct((2 * tok_dev, wide), jnp.bfloat16),
        compiler_params=pltpu.CompilerParams(vmem_limit_bytes=2 * 2**20),
    )(tokens, cotangent, routes.T, combine.T)

    lane = jnp.arange(LANES, dtype=jnp.int32)[None, :]
    expert = lax.axis_index("expert")
    pick = ((lane % experts == expert) & (lane < 3 * experts)).astype(jnp.bfloat16)
    pick = jnp.broadcast_to(pick, (16, LANES))
    is_inner = inner(expert)
    shards = (
        w_in.reshape(2 * half, model_dim),
        v_in.reshape(2 * half, model_dim),
        w_out.reshape(half, model_dim),
    )

    def call(kernel, stack, theirs, more, outs, scratch, limit):
        rows = stack.shape[0]
        operands = (stack, theirs, pick, *shards, *more)
        held = [
            ((rows, model_dim), jnp.bfloat16),
            ((2 * half, rows), jnp.bfloat16),
            ((rows, model_dim), jnp.bfloat16),
            ((rows, LANES), jnp.bfloat16),
        ]
        if outs is None:
            outs, held = held[:2], held[2:]
            out_specs = [inside] * 2
        else:
            out_specs = [inside if outs[1] else pl.BlockSpec(memory_space=pl.ANY)]
            outs = [((2 * half, model_dim), jnp.float32)]
        return pl.pallas_call(
            functools.partial(kernel, tok_dev=tok_dev),
            in_specs=[inside] * len(operands),
            out_specs=out_specs,
            out_shape=[jax.ShapeDtypeStruct(*o) for o in outs],
            scratch_shapes=[pltpu.VMEM(*h) for h in held] + scratch,
            compiler_params=pltpu.CompilerParams(vmem_limit_bytes=limit * 2**20),
            cost_estimate=pl.CostEstimate(
                flops=2 * rows * model_dim * 7 * half,
                bytes_accessed=12 * 2**20,
                transcendentals=rows * half,
            ),
        )(*operands)

    flag = is_inner.astype(jnp.int32)[None]
    block = 2 * tok_dev

    def stack(inputs, *layouts):
        def size(part):
            return part[0][2] if isinstance(part[0], tuple) else part[2]

        return pl.pallas_call(
            functools.partial(stack_kernel, count=len(inputs), layouts=layouts),
            in_specs=[pl.BlockSpec(memory_space=pltpu.SMEM)] + [inside] * len(inputs),
            out_specs=[inside] * len(layouts),
            out_shape=[
                jax.ShapeDtypeStruct((sum(map(size, parts)), wide), jnp.bfloat16)
                for parts in layouts
            ],
            compiler_params=pltpu.CompilerParams(vmem_limit_bytes=2 * 2**20),
        )(flag, *inputs)

    def rows_of(n, first=0, count=1):
        return (n, first * block, count * block)

    order = (Z_NEAR ^ Z_FAR, X ^ Y, X, Y, Z_NEAR)
    first = tied([swap(own, m) for m in order])
    middle, across, beside_x, beside_y, near = first

    through, outward, pair = stack(
        [near, middle, across],
        [rows_of(0), rows_of(2)],
        [rows_of(1), rows_of(2)],
        [rows_of(0), rows_of(1)],
    )
    through = swap(through, Z_NEAR ^ Z_FAR, inner)
    outward = swap(outward, Z_NEAR)
    pair_x, pair_y = swap(pair, X), swap(pair, Y)
    (stack_a,) = stack([own, beside_x, beside_y, across], [rows_of(n) for n in range(4)])
    early = call(first_kernel, stack_a, swap(stack_a, CORE), (), None, [], 6)
    outward, through, pair_x, pair_y, *early = tied([outward, through, pair_x, pair_y, *early])

    far, beyond, relayed = stack(
        [through, outward, middle],
        [(rows_of(0), rows_of(1))],
        [(rows_of(0), rows_of(2))],
        [rows_of(0, 1)],
    )
    third = [swap(beyond, X ^ Y), swap(far, X), swap(far, Y), swap(relayed, Z_NEAR, inner)]
    (stack_b,) = stack(
        [pair, pair_x, pair_y, outward, far],
        [rows_of(0, 0, 2), rows_of(1, 0, 2), rows_of(2, 0, 2), rows_of(3, 1), rows_of(4)],
    )
    (total,) = call(second_kernel, stack_b, swap(stack_b, CORE), early, (0, True), [], 11)
    *third, total = tied([*third, total])

    (stack_c,) = stack(
        [*third, through],
        [rows_of(0), rows_of(1), rows_of(2), (rows_of(4, 1), rows_of(3))],
    )
    scratch = [
        pltpu.VMEM((2 * half, model_dim), jnp.float32),
        pltpu.SemaphoreType.DMA((model_dim // COLUMNS,)),
    ]
    (out,) = call(last_kernel, stack_c, swap(stack_c, CORE), (total,), (0, False), scratch, 11)
    return out.reshape(1, 2, half, model_dim)


def local(tokens, cotangent, routes, combine, w_in, w_out, v_in):
    experts = lax.axis_size("expert") * w_in.shape[0]
    tok_dev, top_k = routes.shape
    sizes = (lax.axis_size("dp"), lax.axis_size("expert"))
    if sizes == (2, 16) and w_in.shape[0] == 1 and 2 * tok_dev * top_k // experts >= tok_dev:
        return dense(tokens, cotangent, routes, combine, w_in, w_out, v_in)
    return dispatched(tokens, cotangent, routes, combine, w_in, w_out, v_in)


def solution(mesh):
    in_specs = (
        P(("dp", "expert"), None),
        P(("dp", "expert"), None),
        P(("dp", "expert"), None),
        P(("dp", "expert"), None),
        P("expert", None, "dp", None),
        P("expert", "dp", None),
        P("expert", None, "dp", None),
    )
    out_specs = P("expert", None, "dp", None)
    return jax.shard_map(local, mesh=mesh, in_specs=in_specs, out_specs=out_specs, check_vma=False)
```

```python
import functools

import jax
import jax.numpy as jnp
from jax import lax
from jax.experimental import pallas as pl
from jax.experimental.pallas import tpu as pltpu
from jax.sharding import PartitionSpec as P

NT = (((1,), (1,)), ((), ()))
NN = (((1,), (0,)), ((), ()))


def expert_terms(slot_rows, slot_grads, w_pair, v_pair, w_down):
    hidden_width = w_pair.shape[1]
    model_dim = w_pair.shape[2]
    stacked = jnp.concatenate([w_pair, v_pair], axis=0).reshape(4 * hidden_width, model_dim)
    projected = lax.dot_general(slot_rows, stacked, NT, preferred_element_type=jnp.float32)
    pre_gate = projected[:, :hidden_width]
    pre_up = projected[:, hidden_width : 2 * hidden_width]
    tan_gate = projected[:, 2 * hidden_width : 3 * hidden_width]
    tan_up = projected[:, 3 * hidden_width :]
    back_grad = lax.dot_general(slot_grads, w_down, NT, preferred_element_type=jnp.float32)
    gate_dir, up_dir = directions(pre_gate, pre_up, tan_gate, tan_up, back_grad)
    gate_term = lax.dot_general(
        gate_dir, slot_rows, (((0,), (0,)), ((), ())), preferred_element_type=jnp.float32
    )
    up_term = lax.dot_general(
        up_dir, slot_rows, (((0,), (0,)), ((), ())), preferred_element_type=jnp.float32
    )
    return jnp.stack([gate_term, up_term], axis=0)


def directions(pre_gate, pre_up, tan_gate, tan_up, back_grad):
    gate_sig = jax.nn.sigmoid(pre_gate)
    first_deriv = gate_sig * (1.0 + pre_gate * (1.0 - gate_sig))
    second_deriv = gate_sig * (1.0 - gate_sig) * (2.0 + pre_gate * (1.0 - 2.0 * gate_sig))
    gate_dir = back_grad * (tan_up * first_deriv + pre_up * second_deriv * tan_gate)
    up_dir = back_grad * first_deriv * tan_gate
    return gate_dir.astype(jnp.bfloat16), up_dir.astype(jnp.bfloat16)


def dispatched(tokens, cotangent, routes, combine, w_in, w_out, v_in):
    n_expert = lax.axis_size("expert")
    exp_dev = w_in.shape[0]
    experts = n_expert * exp_dev
    tok_dev, top_k = routes.shape
    model_dim = tokens.shape[1]
    capacity = 2 * tok_dev * top_k // experts
    pair_count = tok_dev * top_k
    slot_count = n_expert * capacity
    flat_routes = routes.reshape(pair_count)
    onehot = (flat_routes[:, None] == jnp.arange(experts, dtype=jnp.int32)[None, :]).astype(
        jnp.int32
    )
    earlier = jnp.cumsum(onehot, axis=0) - onehot
    slot_rank = jnp.sum(earlier * onehot, axis=1)
    position = flat_routes * capacity + slot_rank
    slot_table = jnp.full((experts * capacity,), pair_count, jnp.int32)
    slot_table = slot_table.at[position].set(jnp.arange(pair_count, dtype=jnp.int32))
    token_index = slot_table // top_k
    padded_tokens = jnp.concatenate([tokens, jnp.zeros((1, model_dim), jnp.bfloat16)], axis=0)
    scaled = (combine[:, :, None] * cotangent[:, None, :].astype(jnp.float32)).astype(jnp.bfloat16)
    padded_scaled = jnp.concatenate(
        [scaled.reshape(pair_count, model_dim), jnp.zeros((1, model_dim), jnp.bfloat16)], axis=0
    )
    send_rows = padded_tokens[token_index].reshape(n_expert, exp_dev * capacity, model_dim)
    send_grads = padded_scaled[slot_table].reshape(n_expert, exp_dev * capacity, model_dim)
    recv_rows = lax.all_to_all(send_rows, "expert", split_axis=0, concat_axis=0, tiled=True)
    recv_grads = lax.all_to_all(send_grads, "expert", split_axis=0, concat_axis=0, tiled=True)

    def regroup(received):
        shaped = received.reshape(n_expert, exp_dev, capacity, model_dim)
        return jnp.transpose(shaped, (1, 0, 2, 3)).reshape(exp_dev, slot_count, model_dim)

    local_rows = regroup(recv_rows)
    local_grads = regroup(recv_grads)
    batched_terms = jax.vmap(expert_terms)
    pair_piece, probe_piece, down_piece = lax.all_gather(
        (w_in, v_in, w_out[:, None]), "dp", axis=2, tiled=True
    )
    partials = batched_terms(local_rows, local_grads, pair_piece, probe_piece, down_piece[:, 0])
    return lax.psum_scatter(
        partials.astype(jnp.bfloat16), "dp", scatter_dimension=2, tiled=True
    ).astype(jnp.float32)


CORE, X, Y = 1, 2, 16
Z_NEAR, Z_FAR = 4, 8
LANES = 128


def pack_kernel(
    tok_hbm, cot_hbm, route_hbm, comb_hbm, out_ref, route_ref, comb_ref, sems, *, experts
):
    tok_dev, model_dim = tok_hbm.shape
    tok_at = out_ref.at[pl.ds(0, tok_dev), pl.ds(0, model_dim)]
    cot_at = out_ref.at[pl.ds(tok_dev, tok_dev), pl.ds(0, model_dim)]
    moves = ((route_hbm, route_ref), (comb_hbm, comb_ref), (tok_hbm, tok_at), (cot_hbm, cot_at))
    copies = [pltpu.make_async_copy(*m, sems.at[n]) for n, m in enumerate(moves)]
    for copy in copies:
        copy.start()
    copies[0].wait()
    copies[1].wait()
    line = lax.broadcasted_iota(jnp.int32, (LANES, tok_dev), 0)
    weight = jnp.zeros((LANES, tok_dev), jnp.float32)
    for k in range(route_ref.shape[0]):
        named = route_ref[k : k + 1, :] == line % experts
        weight = jnp.where(named, comb_ref[k : k + 1, :], weight)
    high = weight.astype(jnp.bfloat16).astype(jnp.float32)
    middle = (weight - high).astype(jnp.bfloat16).astype(jnp.float32)
    low = weight - high - middle
    part = line // experts
    zero = jnp.zeros_like(weight)
    value = jnp.where(part == 0, high, jnp.where(part == 1, middle, jnp.where(part == 2, low, zero)))
    row = lax.broadcasted_iota(jnp.int32, (tok_dev, tok_dev), 0)
    column = lax.broadcasted_iota(jnp.int32, (tok_dev, tok_dev), 1)
    same = (row == column).astype(jnp.float32).astype(jnp.bfloat16)
    turned = lax.dot_general(
        same, value.astype(jnp.bfloat16), NT, preferred_element_type=jnp.float32
    )
    out_ref[0:tok_dev, model_dim:] = turned.astype(jnp.bfloat16)
    out_ref[tok_dev:, model_dim:] = jnp.zeros((tok_dev, LANES), jnp.bfloat16)
    copies[2].wait()
    copies[3].wait()


def stack_kernel(flag_ref, *refs, count, layouts):
    for out_ref, parts in zip(refs[count:], layouts):
        row = 0
        for part in parts:
            at = pl.ds(row, part[0][2] if isinstance(part[0], tuple) else part[2])
            if isinstance(part[0], tuple):
                for taken, (n, first, rows) in zip((1, 0), part):

                    @pl.when(flag_ref[0] == taken)
                    def _(n=n, first=first, rows=rows, at=at, out_ref=out_ref):
                        out_ref[at, :] = refs[n][first : first + rows]

            else:
                n, first, rows = part
                out_ref[at, :] = refs[n][first : first + rows]
            row += at.size


def unpack(pieces, x_ref, c_ref, wt_ref, tok_dev):
    model_dim = x_ref.shape[1]
    row = 0
    for piece in pieces:
        for first in range(0, piece.shape[0], 2 * tok_dev):
            at = pl.ds(row, tok_dev)
            x_ref[at, :] = piece[first : first + tok_dev, 0:model_dim]
            wt_ref[at, :] = piece[first : first + tok_dev, model_dim:]
            c_ref[at, :] = piece[first + tok_dev : first + 2 * tok_dev, 0:model_dim]
            row += tok_dev


def unit_dirs(weight, w_ref, v_ref, wo_ref, x_ref, c_ref, dir_ref):
    half = wo_ref.shape[0]
    both = jnp.concatenate([w_ref[...], v_ref[...]], axis=0)
    seen = lax.dot_general(both, x_ref[...], NT, preferred_element_type=jnp.float32)
    back = lax.dot_general(wo_ref[...], c_ref[...], NT, preferred_element_type=jnp.float32)
    parts = [seen[n * half : (n + 1) * half] for n in range(4)]
    gate_dir, up_dir = directions(*parts, back * weight)
    dir_ref[0:half, :] = gate_dir
    dir_ref[half:, :] = up_dir


def rows_to_dirs(stacks, pick_ref, shards, x_ref, c_ref, wt_ref, dir_ref, tok_dev):
    unpack(stacks, x_ref, c_ref, wt_ref, tok_dev)
    weight = lax.dot_general(pick_ref[...], wt_ref[...], NT, preferred_element_type=jnp.float32)
    unit_dirs(weight[0:1], *shards, x_ref, c_ref, dir_ref)


def first_kernel(mine, theirs, pick_ref, w, v, wo, x_ref, dir_ref, c_ref, wt_ref, *, tok_dev):
    rows_to_dirs((mine, theirs), pick_ref, (w, v, wo), x_ref, c_ref, wt_ref, dir_ref, tok_dev)


COLUMNS = 512


def second_kernel(
    mine, theirs, pick_ref, w, v, wo, early_x, early_dir, sum_ref, x_ref, dir_ref, c_ref, wt_ref,
    *, tok_dev
):
    rows_to_dirs((mine, theirs), pick_ref, (w, v, wo), x_ref, c_ref, wt_ref, dir_ref, tok_dev)
    dirs = jnp.concatenate([early_dir[...], dir_ref[...]], axis=1)
    for n in range(sum_ref.shape[1] // COLUMNS):
        at = pl.ds(n * COLUMNS, COLUMNS)
        rows = jnp.concatenate([early_x[:, at], x_ref[:, at]], axis=0)
        sum_ref[:, at] = lax.dot_general(dirs, rows, NN, preferred_element_type=jnp.float32)


def last_kernel(
    mine, theirs, pick_ref, w, v, wo, add_ref, out_ref, x_ref, dir_ref, c_ref, wt_ref, sum_ref, sems,
    *, tok_dev
):
    rows_to_dirs((mine, theirs), pick_ref, (w, v, wo), x_ref, c_ref, wt_ref, dir_ref, tok_dev)
    copies = []
    for n in range(out_ref.shape[1] // COLUMNS):
        at = pl.ds(n * COLUMNS, COLUMNS)
        total = lax.dot_general(
            dir_ref[...], x_ref[:, at], NN, preferred_element_type=jnp.float32
        )
        sum_ref[:, at] = total + add_ref[:, at]
        copy = pltpu.make_async_copy(sum_ref.at[:, at], out_ref.at[:, at], sems.at[n])
        copy.start()
        copies.append(copy)
    for copy in copies:
        copy.wait()


def swap(value, mask, sender=None):
    axes = ("dp", "expert")
    count = lax.axis_size("dp") * lax.axis_size("expert")
    pairs = [(i, i ^ mask) for i in range(count) if sender is None or sender(i)]
    return lax.ppermute(value, axes, pairs)


def inner(place):
    return (place & Z_NEAR) // Z_NEAR != (place & Z_FAR) // Z_FAR


def after(value, *others):
    return lax.optimization_barrier((value, *others))[0]


def tied(values, *others):
    return list(lax.optimization_barrier((*values, *others)))[: len(values)]


def dense(tokens, cotangent, routes, combine, w_in, w_out, v_in):
    experts = lax.axis_size("expert")
    tok_dev, model_dim = tokens.shape
    half = w_in.shape[2]
    wide = model_dim + LANES
    inside = pl.BlockSpec(memory_space=pltpu.VMEM)
    own = pl.pallas_call(
        functools.partial(pack_kernel, experts=experts),
        in_specs=[pl.BlockSpec(memory_space=pl.ANY)] * 4,
        out_specs=inside,
        out_shape=jax.ShapeDtypeStruct((2 * tok_dev, wide), jnp.bfloat16),
        scratch_shapes=[
            pltpu.VMEM(routes.shape[::-1], jnp.int32),
            pltpu.VMEM(combine.shape[::-1], jnp.float32),
            pltpu.SemaphoreType.DMA((4,)),
        ],
        compiler_params=pltpu.CompilerParams(vmem_limit_bytes=63_190_000),
    )(tokens, cotangent, routes.T, combine.T)

    lane = jnp.arange(LANES, dtype=jnp.int32)[None, :]
    expert = lax.axis_index("expert")
    pick = ((lane % experts == expert) & (lane < 3 * experts)).astype(jnp.bfloat16)
    pick = jnp.broadcast_to(pick, (16, LANES))
    is_inner = inner(expert)
    shards = (
        w_in.reshape(2 * half, model_dim),
        v_in.reshape(2 * half, model_dim),
        w_out.reshape(half, model_dim),
    )

    def call(kernel, stack, theirs, more, outs, scratch, limit):
        rows = stack.shape[0]
        operands = (stack, theirs, pick, *shards, *more)
        held = [
            ((rows, model_dim), jnp.bfloat16),
            ((2 * half, rows), jnp.bfloat16),
            ((rows, model_dim), jnp.bfloat16),
            ((rows, LANES), jnp.bfloat16),
        ]
        if outs is None:
            outs, held = held[:2], held[2:]
            out_specs = [inside] * 2
        else:
            out_specs = [inside if outs[1] else pl.BlockSpec(memory_space=pl.ANY)]
            outs = [((2 * half, model_dim), jnp.float32)]
        return pl.pallas_call(
            functools.partial(kernel, tok_dev=tok_dev),
            in_specs=[inside] * len(operands),
            out_specs=out_specs,
            out_shape=[jax.ShapeDtypeStruct(*o) for o in outs],
            scratch_shapes=[pltpu.VMEM(*h) for h in held] + scratch,
            compiler_params=pltpu.CompilerParams(vmem_limit_bytes=limit * 2**20),
            cost_estimate=pl.CostEstimate(
                flops=2 * rows * model_dim * 7 * half,
                bytes_accessed=12 * 2**20,
                transcendentals=rows * half,
            ),
        )(*operands)

    flag = is_inner.astype(jnp.int32)[None]
    block = 2 * tok_dev

    def stack(inputs, *layouts):
        def size(part):
            return part[0][2] if isinstance(part[0], tuple) else part[2]

        return pl.pallas_call(
            functools.partial(stack_kernel, count=len(inputs), layouts=layouts),
            in_specs=[pl.BlockSpec(memory_space=pltpu.SMEM)] + [inside] * len(inputs),
            out_specs=[inside] * len(layouts),
            out_shape=[
                jax.ShapeDtypeStruct((sum(map(size, parts)), wide), jnp.bfloat16)
                for parts in layouts
            ],
            compiler_params=pltpu.CompilerParams(vmem_limit_bytes=2 * 2**20),
        )(flag, *inputs)

    def rows_of(n, first=0, count=1):
        return (n, first * block, count * block)

    order = (Z_NEAR ^ Z_FAR, X ^ Y, X, Y, Z_NEAR)
    middle, across, beside_x, beside_y, near = (swap(own, m) for m in order)

    through, outward, pair = stack(
        [near, middle, across],
        [rows_of(0), rows_of(2)],
        [rows_of(1), rows_of(2)],
        [rows_of(0), rows_of(1)],
    )
    through = swap(through, Z_NEAR ^ Z_FAR, inner)
    outward = swap(outward, Z_NEAR)
    pair_x, pair_y = swap(pair, X), swap(after(pair, beside_x, beside_y), Y)
    (stack_a,) = stack([after(own, outward), beside_x, beside_y, across], [rows_of(n) for n in range(4)])
    early = call(first_kernel, stack_a, swap(stack_a, CORE), (), None, [], 6)

    far, beyond, relayed = stack(
        [through, outward, middle],
        [(rows_of(0), rows_of(1))],
        [(rows_of(0), rows_of(2))],
        [rows_of(0, 1)],
    )
    third = [swap(beyond, X ^ Y), swap(far, X), swap(far, Y), swap(relayed, Z_NEAR, inner)]
    (stack_b,) = stack(
        [pair, pair_x, pair_y, outward, far],
        [rows_of(0, 0, 2), rows_of(1, 0, 2), rows_of(2, 0, 2), rows_of(3, 1), rows_of(4)],
    )
    (total,) = call(second_kernel, stack_b, swap(stack_b, CORE), early, (0, True), [], 11)
    *third, total = tied([*third, total])

    (stack_c,) = stack(
        [*third, through],
        [rows_of(0), rows_of(1), rows_of(2), (rows_of(4, 1), rows_of(3))],
    )
    scratch = [
        pltpu.VMEM((2 * half, model_dim), jnp.float32),
        pltpu.SemaphoreType.DMA((model_dim // COLUMNS,)),
    ]
    (out,) = call(last_kernel, stack_c, swap(stack_c, CORE), (total,), (0, False), scratch, 11)
    return out.reshape(1, 2, half, model_dim)


def local(tokens, cotangent, routes, combine, w_in, w_out, v_in):
    experts = lax.axis_size("expert") * w_in.shape[0]
    tok_dev, top_k = routes.shape
    sizes = (lax.axis_size("dp"), lax.axis_size("expert"))
    if sizes == (2, 16) and w_in.shape[0] == 1 and 2 * tok_dev * top_k // experts >= tok_dev:
        return dense(tokens, cotangent, routes, combine, w_in, w_out, v_in)
    return dispatched(tokens, cotangent, routes, combine, w_in, w_out, v_in)


def solution(mesh):
    in_specs = (
        P(("dp", "expert"), None),
        P(("dp", "expert"), None),
        P(("dp", "expert"), None),
        P(("dp", "expert"), None),
        P("expert", None, "dp", None),
        P("expert", "dp", None),
        P("expert", None, "dp", None),
    )
    out_specs = P("expert", None, "dp", None)
    return jax.shard_map(local, mesh=mesh, in_specs=in_specs, out_specs=out_specs, check_vma=False)
```

```python
import functools

import jax
import jax.numpy as jnp
from jax import lax
from jax.experimental import pallas as pl
from jax.experimental.pallas import tpu as pltpu
from jax.sharding import PartitionSpec as P

NT = (((1,), (1,)), ((), ()))
NN = (((1,), (0,)), ((), ()))


def expert_terms(slot_rows, slot_grads, w_pair, v_pair, w_down):
    hidden_width = w_pair.shape[1]
    model_dim = w_pair.shape[2]
    stacked = jnp.concatenate([w_pair, v_pair], axis=0).reshape(4 * hidden_width, model_dim)
    projected = lax.dot_general(slot_rows, stacked, NT, preferred_element_type=jnp.float32)
    pre_gate = projected[:, :hidden_width]
    pre_up = projected[:, hidden_width : 2 * hidden_width]
    tan_gate = projected[:, 2 * hidden_width : 3 * hidden_width]
    tan_up = projected[:, 3 * hidden_width :]
    back_grad = lax.dot_general(slot_grads, w_down, NT, preferred_element_type=jnp.float32)
    gate_dir, up_dir = directions(pre_gate, pre_up, tan_gate, tan_up, back_grad)
    gate_term = lax.dot_general(
        gate_dir, slot_rows, (((0,), (0,)), ((), ())), preferred_element_type=jnp.float32
    )
    up_term = lax.dot_general(
        up_dir, slot_rows, (((0,), (0,)), ((), ())), preferred_element_type=jnp.float32
    )
    return jnp.stack([gate_term, up_term], axis=0)


def directions(pre_gate, pre_up, tan_gate, tan_up, back_grad):
    gate_sig = jax.nn.sigmoid(pre_gate)
    first_deriv = gate_sig * (1.0 + pre_gate * (1.0 - gate_sig))
    second_deriv = gate_sig * (1.0 - gate_sig) * (2.0 + pre_gate * (1.0 - 2.0 * gate_sig))
    gate_dir = back_grad * (tan_up * first_deriv + pre_up * second_deriv * tan_gate)
    up_dir = back_grad * first_deriv * tan_gate
    return gate_dir.astype(jnp.bfloat16), up_dir.astype(jnp.bfloat16)


def dispatched(tokens, cotangent, routes, combine, w_in, w_out, v_in):
    n_expert = lax.axis_size("expert")
    exp_dev = w_in.shape[0]
    experts = n_expert * exp_dev
    tok_dev, top_k = routes.shape
    model_dim = tokens.shape[1]
    capacity = 2 * tok_dev * top_k // experts
    pair_count = tok_dev * top_k
    slot_count = n_expert * capacity
    flat_routes = routes.reshape(pair_count)
    onehot = (flat_routes[:, None] == jnp.arange(experts, dtype=jnp.int32)[None, :]).astype(
        jnp.int32
    )
    earlier = jnp.cumsum(onehot, axis=0) - onehot
    slot_rank = jnp.sum(earlier * onehot, axis=1)
    position = flat_routes * capacity + slot_rank
    slot_table = jnp.full((experts * capacity,), pair_count, jnp.int32)
    slot_table = slot_table.at[position].set(jnp.arange(pair_count, dtype=jnp.int32))
    token_index = slot_table // top_k
    padded_tokens = jnp.concatenate([tokens, jnp.zeros((1, model_dim), jnp.bfloat16)], axis=0)
    scaled = (combine[:, :, None] * cotangent[:, None, :].astype(jnp.float32)).astype(jnp.bfloat16)
    padded_scaled = jnp.concatenate(
        [scaled.reshape(pair_count, model_dim), jnp.zeros((1, model_dim), jnp.bfloat16)], axis=0
    )
    send_rows = padded_tokens[token_index].reshape(n_expert, exp_dev * capacity, model_dim)
    send_grads = padded_scaled[slot_table].reshape(n_expert, exp_dev * capacity, model_dim)
    recv_rows = lax.all_to_all(send_rows, "expert", split_axis=0, concat_axis=0, tiled=True)
    recv_grads = lax.all_to_all(send_grads, "expert", split_axis=0, concat_axis=0, tiled=True)

    def regroup(received):
        shaped = received.reshape(n_expert, exp_dev, capacity, model_dim)
        return jnp.transpose(shaped, (1, 0, 2, 3)).reshape(exp_dev, slot_count, model_dim)

    local_rows = regroup(recv_rows)
    local_grads = regroup(recv_grads)
    batched_terms = jax.vmap(expert_terms)
    pair_piece, probe_piece, down_piece = lax.all_gather(
        (w_in, v_in, w_out[:, None]), "dp", axis=2, tiled=True
    )
    partials = batched_terms(local_rows, local_grads, pair_piece, probe_piece, down_piece[:, 0])
    return lax.psum_scatter(
        partials.astype(jnp.bfloat16), "dp", scatter_dimension=2, tiled=True
    ).astype(jnp.float32)


CORE, X, Y = 1, 2, 16
Z_NEAR, Z_FAR = 4, 8
LANES = 128


def pack_kernel(
    tok_hbm, cot_hbm, route_hbm, comb_hbm, out_ref, route_ref, comb_ref, sems, *, experts
):
    tok_dev, model_dim = tok_hbm.shape
    tok_at = out_ref.at[pl.ds(0, tok_dev), pl.ds(0, model_dim)]
    cot_at = out_ref.at[pl.ds(tok_dev, tok_dev), pl.ds(0, model_dim)]
    moves = ((route_hbm, route_ref), (comb_hbm, comb_ref), (tok_hbm, tok_at), (cot_hbm, cot_at))
    copies = [pltpu.make_async_copy(*m, sems.at[n]) for n, m in enumerate(moves)]
    for copy in copies:
        copy.start()
    copies[0].wait()
    copies[1].wait()
    line = lax.broadcasted_iota(jnp.int32, (LANES, tok_dev), 0)
    weight = jnp.zeros((LANES, tok_dev), jnp.float32)
    for k in range(route_ref.shape[0]):
        named = route_ref[k : k + 1, :] == line % experts
        weight = jnp.where(named, comb_ref[k : k + 1, :], weight)
    high = weight.astype(jnp.bfloat16).astype(jnp.float32)
    middle = (weight - high).astype(jnp.bfloat16).astype(jnp.float32)
    low = weight - high - middle
    part = line // experts
    zero = jnp.zeros_like(weight)
    value = jnp.where(part == 0, high, jnp.where(part == 1, middle, jnp.where(part == 2, low, zero)))
    row = lax.broadcasted_iota(jnp.int32, (tok_dev, tok_dev), 0)
    column = lax.broadcasted_iota(jnp.int32, (tok_dev, tok_dev), 1)
    same = (row == column).astype(jnp.float32).astype(jnp.bfloat16)
    turned = lax.dot_general(
        same, value.astype(jnp.bfloat16), NT, preferred_element_type=jnp.float32
    )
    out_ref[0:tok_dev, model_dim:] = turned.astype(jnp.bfloat16)
    out_ref[tok_dev:, model_dim:] = jnp.zeros((tok_dev, LANES), jnp.bfloat16)
    copies[2].wait()
    copies[3].wait()


def stack_kernel(flag_ref, *refs, count, layouts):
    for out_ref, parts in zip(refs[count:], layouts):
        row = 0
        for part in parts:
            at = pl.ds(row, part[0][2] if isinstance(part[0], tuple) else part[2])
            if isinstance(part[0], tuple):
                for taken, (n, first, rows) in zip((1, 0), part):

                    @pl.when(flag_ref[0] == taken)
                    def _(n=n, first=first, rows=rows, at=at, out_ref=out_ref):
                        out_ref[at, :] = refs[n][first : first + rows]

            else:
                n, first, rows = part
                out_ref[at, :] = refs[n][first : first + rows]
            row += at.size


def unpack(pieces, x_ref, c_ref, wt_ref, tok_dev):
    model_dim = x_ref.shape[1]
    for row, (piece, first) in enumerate(pieces):
        at = pl.ds(row * tok_dev, tok_dev)
        x_ref[at, :] = piece[first : first + tok_dev, 0:model_dim]
        wt_ref[at, :] = piece[first : first + tok_dev, model_dim:]
        c_ref[at, :] = piece[first + tok_dev : first + 2 * tok_dev, 0:model_dim]


COLUMNS = 512
ROWS = 256


def rows_to_dirs(stacks, pick_ref, shards, x_ref, c_ref, wt_ref, dir_ref, tok_dev):
    w_ref, v_ref, wo_ref = shards
    half = wo_ref.shape[0]
    pieces = [(s, first) for s in stacks for first in range(0, s.shape[0], 2 * tok_dev)]
    for start in range(0, x_ref.shape[0], ROWS):
        part = pieces[start // tok_dev : (start + ROWS) // tok_dev]
        x_at = x_ref.at[pl.ds(start, ROWS)]
        unpack(part, x_at, c_ref, wt_ref, tok_dev)
        weight = lax.dot_general(
            pick_ref[...], wt_ref[...], NT, preferred_element_type=jnp.float32
        )
        both = jnp.concatenate([w_ref[...], v_ref[...]], axis=0)
        seen = lax.dot_general(both, x_at[...], NT, preferred_element_type=jnp.float32)
        back = lax.dot_general(wo_ref[...], c_ref[...], NT, preferred_element_type=jnp.float32)
        parts = [seen[n * half : (n + 1) * half] for n in range(4)]
        gate_dir, up_dir = directions(*parts, back * weight[0:1])
        dir_ref[0:half, start : start + ROWS] = gate_dir
        dir_ref[half:, start : start + ROWS] = up_dir


def early_kernel(
    mine, theirs, pick_ref, w, v, wo, sum_ref, x_ref, dir_ref, c_ref, wt_ref, *, tok_dev
):
    rows_to_dirs((mine, theirs), pick_ref, (w, v, wo), x_ref, c_ref, wt_ref, dir_ref, tok_dev)
    for n in range(sum_ref.shape[1] // COLUMNS):
        at = pl.ds(n * COLUMNS, COLUMNS)
        sum_ref[:, at] = lax.dot_general(
            dir_ref[...], x_ref[:, at], NN, preferred_element_type=jnp.float32
        )


def last_kernel(
    mine, theirs, pick_ref, w, v, wo, add_ref, out_ref, x_ref, dir_ref, c_ref, wt_ref, sum_ref, sems,
    *, tok_dev
):
    rows_to_dirs((mine, theirs), pick_ref, (w, v, wo), x_ref, c_ref, wt_ref, dir_ref, tok_dev)
    copies = []
    for n in range(out_ref.shape[1] // COLUMNS):
        at = pl.ds(n * COLUMNS, COLUMNS)
        total = lax.dot_general(
            dir_ref[...], x_ref[:, at], NN, preferred_element_type=jnp.float32
        )
        sum_ref[:, at] = total + add_ref[:, at]
        copy = pltpu.make_async_copy(sum_ref.at[:, at], out_ref.at[:, at], sems.at[n])
        copy.start()
        copies.append(copy)
    for copy in copies:
        copy.wait()


def swap(value, mask, sender=None):
    axes = ("dp", "expert")
    count = lax.axis_size("dp") * lax.axis_size("expert")
    pairs = [(i, i ^ mask) for i in range(count) if sender is None or sender(i)]
    return lax.ppermute(value, axes, pairs)


def inner(place):
    return (place & Z_NEAR) // Z_NEAR != (place & Z_FAR) // Z_FAR


def after(value, *others):
    return lax.optimization_barrier((value, *others))[0]


def tied(values, *others):
    return list(lax.optimization_barrier((*values, *others)))[: len(values)]


def dense(tokens, cotangent, routes, combine, w_in, w_out, v_in):
    experts = lax.axis_size("expert")
    tok_dev, model_dim = tokens.shape
    half = w_in.shape[2]
    wide = model_dim + LANES
    inside = pl.BlockSpec(memory_space=pltpu.VMEM)
    own = pl.pallas_call(
        functools.partial(pack_kernel, experts=experts),
        in_specs=[pl.BlockSpec(memory_space=pl.ANY)] * 4,
        out_specs=inside,
        out_shape=jax.ShapeDtypeStruct((2 * tok_dev, wide), jnp.bfloat16),
        scratch_shapes=[
            pltpu.VMEM(routes.shape[::-1], jnp.int32),
            pltpu.VMEM(combine.shape[::-1], jnp.float32),
            pltpu.SemaphoreType.DMA((4,)),
        ],
        compiler_params=pltpu.CompilerParams(vmem_limit_bytes=63_120_000),
    )(tokens, cotangent, routes.T, combine.T)

    lane = jnp.arange(LANES, dtype=jnp.int32)[None, :]
    expert = lax.axis_index("expert")
    pick = ((lane % experts == expert) & (lane < 3 * experts)).astype(jnp.bfloat16)
    pick = jnp.broadcast_to(pick, (16, LANES))
    is_inner = inner(expert)
    shards = (
        w_in.reshape(2 * half, model_dim),
        v_in.reshape(2 * half, model_dim),
        w_out.reshape(half, model_dim),
    )

    def call(kernel, stack, theirs, more, out_spec, scratch, limit):
        rows = stack.shape[0]
        operands = (stack, theirs, pick, *shards, *more)
        return pl.pallas_call(
            functools.partial(kernel, tok_dev=tok_dev),
            in_specs=[inside] * len(operands),
            out_specs=out_spec,
            out_shape=jax.ShapeDtypeStruct((2 * half, model_dim), jnp.float32),
            scratch_shapes=[
                pltpu.VMEM((rows, model_dim), jnp.bfloat16),
                pltpu.VMEM((2 * half, rows), jnp.bfloat16),
                pltpu.VMEM((ROWS, model_dim), jnp.bfloat16),
                pltpu.VMEM((ROWS, LANES), jnp.bfloat16),
            ]
            + scratch,
            compiler_params=pltpu.CompilerParams(vmem_limit_bytes=limit * 2**20),
            cost_estimate=pl.CostEstimate(
                flops=2 * rows * model_dim * 7 * half,
                bytes_accessed=12 * 2**20,
                transcendentals=rows * half,
            ),
        )(*operands)

    flag = is_inner.astype(jnp.int32)[None]
    block = 2 * tok_dev

    def stack(inputs, *layouts):
        def size(part):
            return part[0][2] if isinstance(part[0], tuple) else part[2]

        return pl.pallas_call(
            functools.partial(stack_kernel, count=len(inputs), layouts=layouts),
            in_specs=[pl.BlockSpec(memory_space=pltpu.SMEM)] + [inside] * len(inputs),
            out_specs=[inside] * len(layouts),
            out_shape=[
                jax.ShapeDtypeStruct((sum(map(size, parts)), wide), jnp.bfloat16)
                for parts in layouts
            ],
            compiler_params=pltpu.CompilerParams(vmem_limit_bytes=2 * 2**20),
        )(flag, *inputs)

    def rows_of(n, first=0, count=1):
        return (n, first * block, count * block)

    order = (Z_NEAR ^ Z_FAR, X ^ Y, X, Y, Z_NEAR)
    middle, across, beside_x, beside_y, near = (swap(own, m) for m in order)

    (pair,) = stack([near, middle], [rows_of(0), rows_of(1)])
    pair_x, pair_y = swap(pair, X), swap(after(pair, beside_x, beside_y), Y)
    through = swap(near, Z_NEAR ^ Z_FAR, inner)
    outward = swap(middle, Z_NEAR, inner)
    near_across = swap(after(across, pair), Z_NEAR)
    through_across = swap(after(across, pair), Z_NEAR ^ Z_FAR, inner)

    far, beyond = stack(
        [through, outward, middle],
        [(rows_of(0), rows_of(1))],
        [(rows_of(0), rows_of(2))],
    )
    third = [swap(beyond, X ^ Y), swap(far, X), swap(far, Y)]
    third += [swap(through_across, Z_NEAR, inner)]
    (stack_a,) = stack(
        [own, beside_x, beside_y, across, pair, pair_x, pair_y, far, near_across],
        [rows_of(n) for n in range(4)]
        + [rows_of(n, 0, 2) for n in range(4, 7)]
        + [rows_of(7), rows_of(8)],
    )
    total = call(early_kernel, stack_a, swap(stack_a, CORE), (), inside, [], 14)
    *third, total = tied([*third, total])

    (stack_b,) = stack(
        [*third, through_across],
        [rows_of(0), rows_of(1), rows_of(2), (rows_of(4), rows_of(3))],
    )
    scratch = [
        pltpu.VMEM((2 * half, model_dim), jnp.float32),
        pltpu.SemaphoreType.DMA((model_dim // COLUMNS,)),
    ]
    outside = pl.BlockSpec(memory_space=pl.ANY)
    out = call(last_kernel, stack_b, swap(stack_b, CORE), (total,), outside, scratch, 11)
    return out.reshape(1, 2, half, model_dim)


def local(tokens, cotangent, routes, combine, w_in, w_out, v_in):
    experts = lax.axis_size("expert") * w_in.shape[0]
    tok_dev, top_k = routes.shape
    sizes = (lax.axis_size("dp"), lax.axis_size("expert"))
    if sizes == (2, 16) and w_in.shape[0] == 1 and 2 * tok_dev * top_k // experts >= tok_dev:
        return dense(tokens, cotangent, routes, combine, w_in, w_out, v_in)
    return dispatched(tokens, cotangent, routes, combine, w_in, w_out, v_in)


def solution(mesh):
    in_specs = (
        P(("dp", "expert"), None),
        P(("dp", "expert"), None),
        P(("dp", "expert"), None),
        P(("dp", "expert"), None),
        P("expert", None, "dp", None),
        P("expert", "dp", None),
        P("expert", None, "dp", None),
    )
    out_specs = P("expert", None, "dp", None)
    return jax.shard_map(local, mesh=mesh, in_specs=in_specs, out_specs=out_specs, check_vma=False)
```

```python
import functools

import jax
import jax.numpy as jnp
from jax import lax
from jax.experimental import pallas as pl
from jax.experimental.pallas import tpu as pltpu
from jax.sharding import PartitionSpec as P

NT = (((1,), (1,)), ((), ()))
NN = (((1,), (0,)), ((), ()))


def expert_terms(slot_rows, slot_grads, w_pair, v_pair, w_down):
    hidden_width = w_pair.shape[1]
    model_dim = w_pair.shape[2]
    stacked = jnp.concatenate([w_pair, v_pair], axis=0).reshape(4 * hidden_width, model_dim)
    projected = lax.dot_general(slot_rows, stacked, NT, preferred_element_type=jnp.float32)
    pre_gate = projected[:, :hidden_width]
    pre_up = projected[:, hidden_width : 2 * hidden_width]
    tan_gate = projected[:, 2 * hidden_width : 3 * hidden_width]
    tan_up = projected[:, 3 * hidden_width :]
    back_grad = lax.dot_general(slot_grads, w_down, NT, preferred_element_type=jnp.float32)
    gate_dir, up_dir = directions(pre_gate, pre_up, tan_gate, tan_up, back_grad)
    gate_term = lax.dot_general(
        gate_dir, slot_rows, (((0,), (0,)), ((), ())), preferred_element_type=jnp.float32
    )
    up_term = lax.dot_general(
        up_dir, slot_rows, (((0,), (0,)), ((), ())), preferred_element_type=jnp.float32
    )
    return jnp.stack([gate_term, up_term], axis=0)


def directions(pre_gate, pre_up, tan_gate, tan_up, back_grad):
    gate_sig = jax.nn.sigmoid(pre_gate)
    first_deriv = gate_sig * (1.0 + pre_gate * (1.0 - gate_sig))
    second_deriv = gate_sig * (1.0 - gate_sig) * (2.0 + pre_gate * (1.0 - 2.0 * gate_sig))
    gate_dir = back_grad * (tan_up * first_deriv + pre_up * second_deriv * tan_gate)
    up_dir = back_grad * first_deriv * tan_gate
    return gate_dir.astype(jnp.bfloat16), up_dir.astype(jnp.bfloat16)


def dispatched(tokens, cotangent, routes, combine, w_in, w_out, v_in):
    n_expert = lax.axis_size("expert")
    exp_dev = w_in.shape[0]
    experts = n_expert * exp_dev
    tok_dev, top_k = routes.shape
    model_dim = tokens.shape[1]
    capacity = 2 * tok_dev * top_k // experts
    pair_count = tok_dev * top_k
    slot_count = n_expert * capacity
    flat_routes = routes.reshape(pair_count)
    onehot = (flat_routes[:, None] == jnp.arange(experts, dtype=jnp.int32)[None, :]).astype(
        jnp.int32
    )
    earlier = jnp.cumsum(onehot, axis=0) - onehot
    slot_rank = jnp.sum(earlier * onehot, axis=1)
    position = flat_routes * capacity + slot_rank
    slot_table = jnp.full((experts * capacity,), pair_count, jnp.int32)
    slot_table = slot_table.at[position].set(jnp.arange(pair_count, dtype=jnp.int32))
    token_index = slot_table // top_k
    padded_tokens = jnp.concatenate([tokens, jnp.zeros((1, model_dim), jnp.bfloat16)], axis=0)
    scaled = (combine[:, :, None] * cotangent[:, None, :].astype(jnp.float32)).astype(jnp.bfloat16)
    padded_scaled = jnp.concatenate(
        [scaled.reshape(pair_count, model_dim), jnp.zeros((1, model_dim), jnp.bfloat16)], axis=0
    )
    send_rows = padded_tokens[token_index].reshape(n_expert, exp_dev * capacity, model_dim)
    send_grads = padded_scaled[slot_table].reshape(n_expert, exp_dev * capacity, model_dim)
    recv_rows = lax.all_to_all(send_rows, "expert", split_axis=0, concat_axis=0, tiled=True)
    recv_grads = lax.all_to_all(send_grads, "expert", split_axis=0, concat_axis=0, tiled=True)

    def regroup(received):
        shaped = received.reshape(n_expert, exp_dev, capacity, model_dim)
        return jnp.transpose(shaped, (1, 0, 2, 3)).reshape(exp_dev, slot_count, model_dim)

    local_rows = regroup(recv_rows)
    local_grads = regroup(recv_grads)
    batched_terms = jax.vmap(expert_terms)
    pair_piece, probe_piece, down_piece = lax.all_gather(
        (w_in, v_in, w_out[:, None]), "dp", axis=2, tiled=True
    )
    partials = batched_terms(local_rows, local_grads, pair_piece, probe_piece, down_piece[:, 0])
    return lax.psum_scatter(
        partials.astype(jnp.bfloat16), "dp", scatter_dimension=2, tiled=True
    ).astype(jnp.float32)


CORE, X, Y = 1, 2, 16
Z_NEAR, Z_FAR = 4, 8
LANES = 128


def pack_kernel(
    tok_hbm, cot_hbm, route_hbm, comb_hbm, out_ref, route_ref, comb_ref, sems, *, experts
):
    tok_dev, model_dim = tok_hbm.shape
    tok_at = out_ref.at[pl.ds(0, tok_dev), pl.ds(0, model_dim)]
    cot_at = out_ref.at[pl.ds(tok_dev, tok_dev), pl.ds(0, model_dim)]
    moves = ((route_hbm, route_ref), (comb_hbm, comb_ref), (tok_hbm, tok_at), (cot_hbm, cot_at))
    copies = [pltpu.make_async_copy(*m, sems.at[n]) for n, m in enumerate(moves)]
    for copy in copies:
        copy.start()
    copies[0].wait()
    copies[1].wait()
    line = lax.broadcasted_iota(jnp.int32, (LANES, tok_dev), 0)
    weight = jnp.zeros((LANES, tok_dev), jnp.float32)
    for k in range(route_ref.shape[0]):
        named = route_ref[k : k + 1, :] == line % experts
        weight = jnp.where(named, comb_ref[k : k + 1, :], weight)
    high = weight.astype(jnp.bfloat16).astype(jnp.float32)
    middle = (weight - high).astype(jnp.bfloat16).astype(jnp.float32)
    low = weight - high - middle
    part = line // experts
    zero = jnp.zeros_like(weight)
    value = jnp.where(part == 0, high, jnp.where(part == 1, middle, jnp.where(part == 2, low, zero)))
    row = lax.broadcasted_iota(jnp.int32, (tok_dev, tok_dev), 0)
    column = lax.broadcasted_iota(jnp.int32, (tok_dev, tok_dev), 1)
    same = (row == column).astype(jnp.float32).astype(jnp.bfloat16)
    turned = lax.dot_general(
        same, value.astype(jnp.bfloat16), NT, preferred_element_type=jnp.float32
    )
    out_ref[0:tok_dev, model_dim:] = turned.astype(jnp.bfloat16)
    out_ref[tok_dev:, model_dim:] = jnp.zeros((tok_dev, LANES), jnp.bfloat16)
    copies[2].wait()
    copies[3].wait()


def stack_kernel(flag_ref, *refs, count, layouts):
    for out_ref, parts in zip(refs[count:], layouts):
        row = 0
        for part in parts:
            at = pl.ds(row, part[0][2] if isinstance(part[0], tuple) else part[2])
            if isinstance(part[0], tuple):
                for taken, (n, first, rows) in zip((1, 0), part):

                    @pl.when(flag_ref[0] == taken)
                    def _(n=n, first=first, rows=rows, at=at, out_ref=out_ref):
                        out_ref[at, :] = refs[n][first : first + rows]

            else:
                n, first, rows = part
                out_ref[at, :] = refs[n][first : first + rows]
            row += at.size


def unpack(pieces, x_ref, c_ref, wt_ref, tok_dev):
    model_dim = x_ref.shape[1]
    for row, (piece, first) in enumerate(pieces):
        at = pl.ds(row * tok_dev, tok_dev)
        x_ref[at, :] = piece[first : first + tok_dev, 0:model_dim]
        wt_ref[at, :] = piece[first : first + tok_dev, model_dim:]
        c_ref[at, :] = piece[first + tok_dev : first + 2 * tok_dev, 0:model_dim]


COLUMNS = 512
ROWS = 256


def rows_to_dirs(stacks, pick_ref, shards, x_ref, c_ref, wt_ref, dir_ref, tok_dev):
    w_ref, v_ref, wo_ref = shards
    half = wo_ref.shape[0]
    pieces = [(s, first) for s in stacks for first in range(0, s.shape[0], 2 * tok_dev)]
    for start in range(0, x_ref.shape[0], ROWS):
        part = pieces[start // tok_dev : (start + ROWS) // tok_dev]
        x_at = x_ref.at[pl.ds(start, ROWS)]
        unpack(part, x_at, c_ref, wt_ref, tok_dev)
        weight = lax.dot_general(
            pick_ref[...], wt_ref[...], NT, preferred_element_type=jnp.float32
        )
        both = jnp.concatenate([w_ref[...], v_ref[...]], axis=0)
        seen = lax.dot_general(both, x_at[...], NT, preferred_element_type=jnp.float32)
        back = lax.dot_general(wo_ref[...], c_ref[...], NT, preferred_element_type=jnp.float32)
        parts = [seen[n * half : (n + 1) * half] for n in range(4)]
        gate_dir, up_dir = directions(*parts, back * weight[0:1])
        dir_ref[0:half, start : start + ROWS] = gate_dir
        dir_ref[half:, start : start + ROWS] = up_dir


def early_kernel(
    mine, theirs, pick_ref, w, v, wo, sum_ref, x_ref, dir_ref, c_ref, wt_ref, *, tok_dev
):
    rows_to_dirs((mine, theirs), pick_ref, (w, v, wo), x_ref, c_ref, wt_ref, dir_ref, tok_dev)
    for n in range(sum_ref.shape[1] // COLUMNS):
        at = pl.ds(n * COLUMNS, COLUMNS)
        sum_ref[:, at] = lax.dot_general(
            dir_ref[...], x_ref[:, at], NN, preferred_element_type=jnp.float32
        )


def last_kernel(
    mine, theirs, pick_ref, w, v, wo, add_ref, out_ref, x_ref, dir_ref, c_ref, wt_ref, sum_ref, sems,
    *, tok_dev
):
    rows_to_dirs((mine, theirs), pick_ref, (w, v, wo), x_ref, c_ref, wt_ref, dir_ref, tok_dev)
    copies = []
    for n in range(out_ref.shape[1] // COLUMNS):
        at = pl.ds(n * COLUMNS, COLUMNS)
        total = lax.dot_general(
            dir_ref[...], x_ref[:, at], NN, preferred_element_type=jnp.float32
        )
        sum_ref[:, at] = total + add_ref[:, at]
        copy = pltpu.make_async_copy(sum_ref.at[:, at], out_ref.at[:, at], sems.at[n])
        copy.start()
        copies.append(copy)
    for copy in copies:
        copy.wait()


def swap(value, mask, sender=None):
    axes = ("dp", "expert")
    count = lax.axis_size("dp") * lax.axis_size("expert")
    pairs = [(i, i ^ mask) for i in range(count) if sender is None or sender(i)]
    return lax.ppermute(value, axes, pairs)


def inner(place):
    return (place & Z_NEAR) // Z_NEAR != (place & Z_FAR) // Z_FAR


def after(value, *others):
    return lax.optimization_barrier((value, *others))[0]


def tied(values, *others):
    return list(lax.optimization_barrier((*values, *others)))[: len(values)]


def dense(tokens, cotangent, routes, combine, w_in, w_out, v_in):
    experts = lax.axis_size("expert")
    tok_dev, model_dim = tokens.shape
    half = w_in.shape[2]
    wide = model_dim + LANES
    inside = pl.BlockSpec(memory_space=pltpu.VMEM)
    own = pl.pallas_call(
        functools.partial(pack_kernel, experts=experts),
        in_specs=[pl.BlockSpec(memory_space=pl.ANY)] * 4,
        out_specs=inside,
        out_shape=jax.ShapeDtypeStruct((2 * tok_dev, wide), jnp.bfloat16),
        scratch_shapes=[
            pltpu.VMEM(routes.shape[::-1], jnp.int32),
            pltpu.VMEM(combine.shape[::-1], jnp.float32),
            pltpu.SemaphoreType.DMA((4,)),
        ],
        compiler_params=pltpu.CompilerParams(vmem_limit_bytes=63_120_000),
    )(tokens, cotangent, routes.T, combine.T)

    lane = jnp.arange(LANES, dtype=jnp.int32)[None, :]
    expert = lax.axis_index("expert")
    pick = ((lane % experts == expert) & (lane < 3 * experts)).astype(jnp.bfloat16)
    pick = jnp.broadcast_to(pick, (16, LANES))
    is_inner = inner(expert)
    shards = (
        w_in.reshape(2 * half, model_dim),
        v_in.reshape(2 * half, model_dim),
        w_out.reshape(half, model_dim),
    )

    def call(kernel, stack, theirs, more, out_spec, scratch, limit):
        rows = stack.shape[0]
        operands = (stack, theirs, pick, *shards, *more)
        return pl.pallas_call(
            functools.partial(kernel, tok_dev=tok_dev),
            in_specs=[inside] * len(operands),
            out_specs=out_spec,
            out_shape=jax.ShapeDtypeStruct((2 * half, model_dim), jnp.float32),
            scratch_shapes=[
                pltpu.VMEM((rows, model_dim), jnp.bfloat16),
                pltpu.VMEM((2 * half, rows), jnp.bfloat16),
                pltpu.VMEM((ROWS, model_dim), jnp.bfloat16),
                pltpu.VMEM((ROWS, LANES), jnp.bfloat16),
            ]
            + scratch,
            compiler_params=pltpu.CompilerParams(vmem_limit_bytes=limit * 2**20),
            cost_estimate=pl.CostEstimate(
                flops=2 * rows * model_dim * 7 * half,
                bytes_accessed=12 * 2**20,
                transcendentals=rows * half,
            ),
        )(*operands)

    flag = is_inner.astype(jnp.int32)[None]
    block = 2 * tok_dev

    def stack(inputs, *layouts):
        def size(part):
            return part[0][2] if isinstance(part[0], tuple) else part[2]

        return pl.pallas_call(
            functools.partial(stack_kernel, count=len(inputs), layouts=layouts),
            in_specs=[pl.BlockSpec(memory_space=pltpu.SMEM)] + [inside] * len(inputs),
            out_specs=[inside] * len(layouts),
            out_shape=[
                jax.ShapeDtypeStruct((sum(map(size, parts)), wide), jnp.bfloat16)
                for parts in layouts
            ],
            compiler_params=pltpu.CompilerParams(vmem_limit_bytes=2 * 2**20),
        )(flag, *inputs)

    def rows_of(n, first=0, count=1):
        return (n, first * block, count * block)

    order = (Z_NEAR ^ Z_FAR, X ^ Y, X, Y, Z_NEAR)
    middle, across, beside_x, beside_y, near = (swap(own, m) for m in order)

    through, outward, pair = stack(
        [near, middle, across],
        [rows_of(0), rows_of(2)],
        [rows_of(1), rows_of(2)],
        [rows_of(0), rows_of(1)],
    )
    through = swap(through, Z_NEAR ^ Z_FAR, inner)
    outward = swap(outward, Z_NEAR)
    pair_x, pair_y = swap(pair, X), swap(after(pair, beside_x, beside_y), Y)

    (held,) = stack([after(own, pair)], [rows_of(0)])
    through, held = tied([through, held])

    beyond, far, relayed = stack(
        [through, outward, middle],
        [(rows_of(0), rows_of(2))],
        [(rows_of(0), rows_of(1))],
        [rows_of(0, 1)],
    )
    third = [swap(beyond, X ^ Y), swap(far, X), swap(far, Y), swap(relayed, Z_NEAR, inner)]
    (stack_a,) = stack(
        [held, beside_x, beside_y, across, pair, pair_x, pair_y, far, outward],
        [rows_of(n) for n in range(4)]
        + [rows_of(n, 0, 2) for n in range(4, 7)]
        + [rows_of(7), rows_of(8, 1)],
    )
    total = call(early_kernel, stack_a, swap(stack_a, CORE), (), inside, [], 14)
    *third, total = tied([*third, total])

    (stack_b,) = stack(
        [*third, through],
        [rows_of(0), rows_of(1), rows_of(2), (rows_of(4, 1), rows_of(3))],
    )
    scratch = [
        pltpu.VMEM((2 * half, model_dim), jnp.float32),
        pltpu.SemaphoreType.DMA((model_dim // COLUMNS,)),
    ]
    outside = pl.BlockSpec(memory_space=pl.ANY)
    out = call(last_kernel, stack_b, swap(stack_b, CORE), (total,), outside, scratch, 11)
    return out.reshape(1, 2, half, model_dim)


def local(tokens, cotangent, routes, combine, w_in, w_out, v_in):
    experts = lax.axis_size("expert") * w_in.shape[0]
    tok_dev, top_k = routes.shape
    sizes = (lax.axis_size("dp"), lax.axis_size("expert"))
    if sizes == (2, 16) and w_in.shape[0] == 1 and 2 * tok_dev * top_k // experts >= tok_dev:
        return dense(tokens, cotangent, routes, combine, w_in, w_out, v_in)
    return dispatched(tokens, cotangent, routes, combine, w_in, w_out, v_in)


def solution(mesh):
    in_specs = (
        P(("dp", "expert"), None),
        P(("dp", "expert"), None),
        P(("dp", "expert"), None),
        P(("dp", "expert"), None),
        P("expert", None, "dp", None),
        P("expert", "dp", None),
        P("expert", None, "dp", None),
    )
    out_specs = P("expert", None, "dp", None)
    return jax.shard_map(local, mesh=mesh, in_specs=in_specs, out_specs=out_specs, check_vma=False)
```

```python
import functools

import jax
import jax.numpy as jnp
from jax import lax
from jax.experimental import pallas as pl
from jax.experimental.pallas import tpu as pltpu
from jax.sharding import PartitionSpec as P

NT = (((1,), (1,)), ((), ()))
NN = (((1,), (0,)), ((), ()))


def expert_terms(slot_rows, slot_grads, w_pair, v_pair, w_down):
    hidden_width = w_pair.shape[1]
    model_dim = w_pair.shape[2]
    stacked = jnp.concatenate([w_pair, v_pair], axis=0).reshape(4 * hidden_width, model_dim)
    projected = lax.dot_general(slot_rows, stacked, NT, preferred_element_type=jnp.float32)
    pre_gate = projected[:, :hidden_width]
    pre_up = projected[:, hidden_width : 2 * hidden_width]
    tan_gate = projected[:, 2 * hidden_width : 3 * hidden_width]
    tan_up = projected[:, 3 * hidden_width :]
    back_grad = lax.dot_general(slot_grads, w_down, NT, preferred_element_type=jnp.float32)
    gate_dir, up_dir = directions(pre_gate, pre_up, tan_gate, tan_up, back_grad)
    gate_term = lax.dot_general(
        gate_dir, slot_rows, (((0,), (0,)), ((), ())), preferred_element_type=jnp.float32
    )
    up_term = lax.dot_general(
        up_dir, slot_rows, (((0,), (0,)), ((), ())), preferred_element_type=jnp.float32
    )
    return jnp.stack([gate_term, up_term], axis=0)


def directions(pre_gate, pre_up, tan_gate, tan_up, back_grad):
    gate_sig = jax.nn.sigmoid(pre_gate)
    first_deriv = gate_sig * (1.0 + pre_gate * (1.0 - gate_sig))
    second_deriv = gate_sig * (1.0 - gate_sig) * (2.0 + pre_gate * (1.0 - 2.0 * gate_sig))
    gate_dir = back_grad * (tan_up * first_deriv + pre_up * second_deriv * tan_gate)
    up_dir = back_grad * first_deriv * tan_gate
    return gate_dir.astype(jnp.bfloat16), up_dir.astype(jnp.bfloat16)


def dispatched(tokens, cotangent, routes, combine, w_in, w_out, v_in):
    n_expert = lax.axis_size("expert")
    exp_dev = w_in.shape[0]
    experts = n_expert * exp_dev
    tok_dev, top_k = routes.shape
    model_dim = tokens.shape[1]
    capacity = 2 * tok_dev * top_k // experts
    pair_count = tok_dev * top_k
    slot_count = n_expert * capacity
    flat_routes = routes.reshape(pair_count)
    onehot = (flat_routes[:, None] == jnp.arange(experts, dtype=jnp.int32)[None, :]).astype(
        jnp.int32
    )
    earlier = jnp.cumsum(onehot, axis=0) - onehot
    slot_rank = jnp.sum(earlier * onehot, axis=1)
    position = flat_routes * capacity + slot_rank
    slot_table = jnp.full((experts * capacity,), pair_count, jnp.int32)
    slot_table = slot_table.at[position].set(jnp.arange(pair_count, dtype=jnp.int32))
    token_index = slot_table // top_k
    padded_tokens = jnp.concatenate([tokens, jnp.zeros((1, model_dim), jnp.bfloat16)], axis=0)
    scaled = (combine[:, :, None] * cotangent[:, None, :].astype(jnp.float32)).astype(jnp.bfloat16)
    padded_scaled = jnp.concatenate(
        [scaled.reshape(pair_count, model_dim), jnp.zeros((1, model_dim), jnp.bfloat16)], axis=0
    )
    send_rows = padded_tokens[token_index].reshape(n_expert, exp_dev * capacity, model_dim)
    send_grads = padded_scaled[slot_table].reshape(n_expert, exp_dev * capacity, model_dim)
    recv_rows = lax.all_to_all(send_rows, "expert", split_axis=0, concat_axis=0, tiled=True)
    recv_grads = lax.all_to_all(send_grads, "expert", split_axis=0, concat_axis=0, tiled=True)

    def regroup(received):
        shaped = received.reshape(n_expert, exp_dev, capacity, model_dim)
        return jnp.transpose(shaped, (1, 0, 2, 3)).reshape(exp_dev, slot_count, model_dim)

    local_rows = regroup(recv_rows)
    local_grads = regroup(recv_grads)
    batched_terms = jax.vmap(expert_terms)
    pair_piece, probe_piece, down_piece = lax.all_gather(
        (w_in, v_in, w_out[:, None]), "dp", axis=2, tiled=True
    )
    partials = batched_terms(local_rows, local_grads, pair_piece, probe_piece, down_piece[:, 0])
    return lax.psum_scatter(
        partials.astype(jnp.bfloat16), "dp", scatter_dimension=2, tiled=True
    ).astype(jnp.float32)


CORE, X, Y = 1, 2, 16
Z_NEAR, Z_FAR = 4, 8
LANES = 128


def pack_kernel(
    tok_hbm, cot_hbm, route_hbm, comb_hbm, out_ref, route_ref, comb_ref, sems, *, experts
):
    tok_dev, model_dim = tok_hbm.shape
    tok_at = out_ref.at[pl.ds(0, tok_dev), pl.ds(0, model_dim)]
    cot_at = out_ref.at[pl.ds(tok_dev, tok_dev), pl.ds(0, model_dim)]
    moves = ((route_hbm, route_ref), (comb_hbm, comb_ref), (tok_hbm, tok_at), (cot_hbm, cot_at))
    copies = [pltpu.make_async_copy(*m, sems.at[n]) for n, m in enumerate(moves)]
    for copy in copies:
        copy.start()
    copies[0].wait()
    copies[1].wait()
    line = lax.broadcasted_iota(jnp.int32, (LANES, tok_dev), 0)
    weight = jnp.zeros((LANES, tok_dev), jnp.float32)
    for k in range(route_ref.shape[0]):
        named = route_ref[k : k + 1, :] == line % experts
        weight = jnp.where(named, comb_ref[k : k + 1, :], weight)
    high = weight.astype(jnp.bfloat16).astype(jnp.float32)
    middle = (weight - high).astype(jnp.bfloat16).astype(jnp.float32)
    low = weight - high - middle
    part = line // experts
    zero = jnp.zeros_like(weight)
    value = jnp.where(part == 0, high, jnp.where(part == 1, middle, jnp.where(part == 2, low, zero)))
    row = lax.broadcasted_iota(jnp.int32, (tok_dev, tok_dev), 0)
    column = lax.broadcasted_iota(jnp.int32, (tok_dev, tok_dev), 1)
    same = (row == column).astype(jnp.float32).astype(jnp.bfloat16)
    turned = lax.dot_general(
        same, value.astype(jnp.bfloat16), NT, preferred_element_type=jnp.float32
    )
    out_ref[0:tok_dev, model_dim:] = turned.astype(jnp.bfloat16)
    out_ref[tok_dev:, model_dim:] = jnp.zeros((tok_dev, LANES), jnp.bfloat16)
    copies[2].wait()
    copies[3].wait()


def stack_kernel(flag_ref, *refs, count, layouts):
    for out_ref, parts in zip(refs[count:], layouts):
        row = 0
        for part in parts:
            at = pl.ds(row, part[0][2] if isinstance(part[0], tuple) else part[2])
            if isinstance(part[0], tuple):
                for taken, (n, first, rows) in zip((1, 0), part):

                    @pl.when(flag_ref[0] == taken)
                    def _(n=n, first=first, rows=rows, at=at, out_ref=out_ref):
                        out_ref[at, :] = refs[n][first : first + rows]

            else:
                n, first, rows = part
                out_ref[at, :] = refs[n][first : first + rows]
            row += at.size


def unpack(pieces, x_ref, c_ref, wt_ref, tok_dev):
    model_dim = x_ref.shape[1]
    for row, (piece, first) in enumerate(pieces):
        at = pl.ds(row * tok_dev, tok_dev)
        x_ref[at, :] = piece[first : first + tok_dev, 0:model_dim]
        wt_ref[at, :] = piece[first : first + tok_dev, model_dim:]
        c_ref[at, :] = piece[first + tok_dev : first + 2 * tok_dev, 0:model_dim]


COLUMNS = 512
ROWS = 256


def sum_kernel(*refs, stacks, adds, leaves, tok_dev):
    pieces = []
    for stack, skipped in zip(refs, stacks):
        pieces += [(stack, n) for n in range(skipped, stack.shape[0], 2 * tok_dev)]
    pick_ref, w_ref, v_ref, wo_ref, *refs = refs[len(stacks) :]
    if adds:
        add_ref, *refs = refs
    if leaves:
        out_ref, x_ref, dir_ref, c_ref, wt_ref, sum_ref, sems = refs
    else:
        sum_ref, x_ref, dir_ref, c_ref, wt_ref = refs
    half = wo_ref.shape[0]
    rows = x_ref.shape[0]
    for start in range(0, rows, c_ref.shape[0]):
        step = min(c_ref.shape[0], rows - start)
        part = pieces[start // tok_dev : (start + step) // tok_dev]
        x_at = x_ref.at[pl.ds(start, step)]
        unpack(part, x_at, c_ref, wt_ref, tok_dev)
        weight = lax.dot_general(
            pick_ref[...], wt_ref[0:step], NT, preferred_element_type=jnp.float32
        )
        both = jnp.concatenate([w_ref[...], v_ref[...]], axis=0)
        seen = lax.dot_general(both, x_at[...], NT, preferred_element_type=jnp.float32)
        back = lax.dot_general(
            wo_ref[...], c_ref[0:step], NT, preferred_element_type=jnp.float32
        )
        parts = [seen[n * half : (n + 1) * half] for n in range(4)]
        gate_dir, up_dir = directions(*parts, back * weight[0:1])
        dir_ref[0:half, start : start + step] = gate_dir
        dir_ref[half:, start : start + step] = up_dir
    copies = []
    for n in range(sum_ref.shape[1] // COLUMNS):
        at = pl.ds(n * COLUMNS, COLUMNS)
        term = lax.dot_general(
            dir_ref[...], x_ref[:, at], NN, preferred_element_type=jnp.float32
        )
        sum_ref[:, at] = term + add_ref[:, at] if adds else term
        if leaves:
            copy = pltpu.make_async_copy(sum_ref.at[:, at], out_ref.at[:, at], sems.at[n])
            copy.start()
            copies.append(copy)
    for copy in copies:
        copy.wait()


def swap(value, mask, sender=None):
    axes = ("dp", "expert")
    count = lax.axis_size("dp") * lax.axis_size("expert")
    pairs = [(i, i ^ mask) for i in range(count) if sender is None or sender(i)]
    return lax.ppermute(value, axes, pairs)


def inner(place):
    return (place & Z_NEAR) // Z_NEAR != (place & Z_FAR) // Z_FAR


def after(value, *others):
    return lax.optimization_barrier((value, *others))[0]


def tied(values, *others):
    return list(lax.optimization_barrier((*values, *others)))[: len(values)]


def dense(tokens, cotangent, routes, combine, w_in, w_out, v_in):
    experts = lax.axis_size("expert")
    tok_dev, model_dim = tokens.shape
    half = w_in.shape[2]
    wide = model_dim + LANES
    inside = pl.BlockSpec(memory_space=pltpu.VMEM)
    own = pl.pallas_call(
        functools.partial(pack_kernel, experts=experts),
        in_specs=[pl.BlockSpec(memory_space=pl.ANY)] * 4,
        out_specs=inside,
        out_shape=jax.ShapeDtypeStruct((2 * tok_dev, wide), jnp.bfloat16),
        scratch_shapes=[
            pltpu.VMEM(routes.shape[::-1], jnp.int32),
            pltpu.VMEM(combine.shape[::-1], jnp.float32),
            pltpu.SemaphoreType.DMA((4,)),
        ],
        compiler_params=pltpu.CompilerParams(vmem_limit_bytes=63_120_000),
    )(tokens, cotangent, routes.T, combine.T)

    lane = jnp.arange(LANES, dtype=jnp.int32)[None, :]
    expert = lax.axis_index("expert")
    pick = ((lane % experts == expert) & (lane < 3 * experts)).astype(jnp.bfloat16)
    pick = jnp.broadcast_to(pick, (16, LANES))
    is_inner = inner(expert)
    shards = (
        w_in.reshape(2 * half, model_dim),
        v_in.reshape(2 * half, model_dim),
        w_out.reshape(half, model_dim),
    )

    def add_terms(stacks, total, limit, leaves=False, skipped=0):
        skips = [skipped] + [0] * (len(stacks) - 1)
        rows = (sum(stack.shape[0] for stack in stacks) - skipped) // 2
        step = min(rows, ROWS)
        adds = [] if total is None else [total]
        operands = (*stacks, pick, *shards, *adds)
        scratch = [
            pltpu.VMEM((rows, model_dim), jnp.bfloat16),
            pltpu.VMEM((2 * half, rows), jnp.bfloat16),
            pltpu.VMEM((step, model_dim), jnp.bfloat16),
            pltpu.VMEM((step, LANES), jnp.bfloat16),
        ]
        if leaves:
            scratch += [
                pltpu.VMEM((2 * half, model_dim), jnp.float32),
                pltpu.SemaphoreType.DMA((model_dim // COLUMNS,)),
            ]
        return pl.pallas_call(
            functools.partial(
                sum_kernel, stacks=skips, adds=len(adds), leaves=leaves, tok_dev=tok_dev
            ),
            in_specs=[inside] * len(operands),
            out_specs=pl.BlockSpec(memory_space=pl.ANY) if leaves else inside,
            out_shape=jax.ShapeDtypeStruct((2 * half, model_dim), jnp.float32),
            scratch_shapes=scratch,
            compiler_params=pltpu.CompilerParams(vmem_limit_bytes=limit * 2**20),
            cost_estimate=pl.CostEstimate(
                flops=2 * rows * model_dim * 7 * half,
                bytes_accessed=12 * 2**20,
                transcendentals=rows * half,
            ),
        )(*operands)

    flag = is_inner.astype(jnp.int32)[None]
    block = 2 * tok_dev

    def stack(inputs, *layouts):
        def size(part):
            return part[0][2] if isinstance(part[0], tuple) else part[2]

        return pl.pallas_call(
            functools.partial(stack_kernel, count=len(inputs), layouts=layouts),
            in_specs=[pl.BlockSpec(memory_space=pltpu.SMEM)] + [inside] * len(inputs),
            out_specs=[inside] * len(layouts),
            out_shape=[
                jax.ShapeDtypeStruct((sum(map(size, parts)), wide), jnp.bfloat16)
                for parts in layouts
            ],
            compiler_params=pltpu.CompilerParams(vmem_limit_bytes=2 * 2**20),
        )(flag, *inputs)

    def rows_of(n, first=0, count=1):
        return (n, first * block, count * block)

    order = (Z_NEAR ^ Z_FAR, X ^ Y, X, Y, Z_NEAR)
    middle, across, beside_x, beside_y, near = (swap(own, m) for m in order)

    (held,) = stack([own], [rows_of(0)])
    middle, held = tied([middle, held])
    through, outward, pair = stack(
        [near, middle, across],
        [rows_of(0), rows_of(2)],
        [rows_of(1), rows_of(2)],
        [rows_of(0), rows_of(1)],
    )
    through = swap(through, Z_NEAR ^ Z_FAR, inner)
    outward = swap(outward, Z_NEAR)
    pair_x, pair_y = swap(pair, X), swap(after(pair, beside_x, beside_y), Y)

    total = add_terms([held, beside_x, beside_y, across], None, 8)
    through, total = tied([through, total])

    beyond, far_x, far_y, far, relayed = stack(
        [through, outward, middle],
        [(rows_of(0), rows_of(2))],
        *[[(rows_of(0), rows_of(1))]] * 3,
        [rows_of(0, 1)],
    )
    third = [swap(beyond, X ^ Y), swap(far_x, X), swap(far_y, Y), swap(relayed, Z_NEAR, inner)]
    (stack_b,) = stack(
        [held, beside_x, beside_y, across, pair, pair_x, pair_y, far, outward],
        [rows_of(n) for n in range(4)]
        + [rows_of(n, 0, 2) for n in range(4, 7)]
        + [rows_of(7), rows_of(8, 1)],
    )
    total = add_terms([stack_b, swap(stack_b, CORE)], total, 14, skipped=4 * block)
    *third, total = tied([*third, total])

    (stack_c,) = stack(
        [*third, through],
        [rows_of(0), rows_of(1), rows_of(2), (rows_of(4, 1), rows_of(3))],
    )
    theirs = swap(stack_c, CORE)
    total = add_terms([stack_c], total, 8)
    out = add_terms([theirs], total, 11, leaves=True)
    return out.reshape(1, 2, half, model_dim)


def local(tokens, cotangent, routes, combine, w_in, w_out, v_in):
    experts = lax.axis_size("expert") * w_in.shape[0]
    tok_dev, top_k = routes.shape
    sizes = (lax.axis_size("dp"), lax.axis_size("expert"))
    if sizes == (2, 16) and w_in.shape[0] == 1 and 2 * tok_dev * top_k // experts >= tok_dev:
        return dense(tokens, cotangent, routes, combine, w_in, w_out, v_in)
    return dispatched(tokens, cotangent, routes, combine, w_in, w_out, v_in)


def solution(mesh):
    in_specs = (
        P(("dp", "expert"), None),
        P(("dp", "expert"), None),
        P(("dp", "expert"), None),
        P(("dp", "expert"), None),
        P("expert", None, "dp", None),
        P("expert", "dp", None),
        P("expert", None, "dp", None),
    )
    out_specs = P("expert", None, "dp", None)
    return jax.shard_map(local, mesh=mesh, in_specs=in_specs, out_specs=out_specs, check_vma=False)
```

```python
import functools

import jax
import jax.numpy as jnp
from jax import lax
from jax.experimental import pallas as pl
from jax.experimental.pallas import tpu as pltpu
from jax.sharding import PartitionSpec as P

NT = (((1,), (1,)), ((), ()))
NN = (((1,), (0,)), ((), ()))


def expert_terms(slot_rows, slot_grads, w_pair, v_pair, w_down):
    hidden_width = w_pair.shape[1]
    model_dim = w_pair.shape[2]
    stacked = jnp.concatenate([w_pair, v_pair], axis=0).reshape(4 * hidden_width, model_dim)
    projected = lax.dot_general(slot_rows, stacked, NT, preferred_element_type=jnp.float32)
    pre_gate = projected[:, :hidden_width]
    pre_up = projected[:, hidden_width : 2 * hidden_width]
    tan_gate = projected[:, 2 * hidden_width : 3 * hidden_width]
    tan_up = projected[:, 3 * hidden_width :]
    back_grad = lax.dot_general(slot_grads, w_down, NT, preferred_element_type=jnp.float32)
    gate_dir, up_dir = directions(pre_gate, pre_up, tan_gate, tan_up, back_grad)
    gate_term = lax.dot_general(
        gate_dir, slot_rows, (((0,), (0,)), ((), ())), preferred_element_type=jnp.float32
    )
    up_term = lax.dot_general(
        up_dir, slot_rows, (((0,), (0,)), ((), ())), preferred_element_type=jnp.float32
    )
    return jnp.stack([gate_term, up_term], axis=0)


def directions(pre_gate, pre_up, tan_gate, tan_up, back_grad):
    gate_sig = jax.nn.sigmoid(pre_gate)
    first_deriv = gate_sig * (1.0 + pre_gate * (1.0 - gate_sig))
    second_deriv = gate_sig * (1.0 - gate_sig) * (2.0 + pre_gate * (1.0 - 2.0 * gate_sig))
    gate_dir = back_grad * (tan_up * first_deriv + pre_up * second_deriv * tan_gate)
    up_dir = back_grad * first_deriv * tan_gate
    return gate_dir.astype(jnp.bfloat16), up_dir.astype(jnp.bfloat16)


def dispatched(tokens, cotangent, routes, combine, w_in, w_out, v_in):
    n_expert = lax.axis_size("expert")
    exp_dev = w_in.shape[0]
    experts = n_expert * exp_dev
    tok_dev, top_k = routes.shape
    model_dim = tokens.shape[1]
    capacity = 2 * tok_dev * top_k // experts
    pair_count = tok_dev * top_k
    slot_count = n_expert * capacity
    flat_routes = routes.reshape(pair_count)
    onehot = (flat_routes[:, None] == jnp.arange(experts, dtype=jnp.int32)[None, :]).astype(
        jnp.int32
    )
    earlier = jnp.cumsum(onehot, axis=0) - onehot
    slot_rank = jnp.sum(earlier * onehot, axis=1)
    position = flat_routes * capacity + slot_rank
    slot_table = jnp.full((experts * capacity,), pair_count, jnp.int32)
    slot_table = slot_table.at[position].set(jnp.arange(pair_count, dtype=jnp.int32))
    token_index = slot_table // top_k
    padded_tokens = jnp.concatenate([tokens, jnp.zeros((1, model_dim), jnp.bfloat16)], axis=0)
    scaled = (combine[:, :, None] * cotangent[:, None, :].astype(jnp.float32)).astype(jnp.bfloat16)
    padded_scaled = jnp.concatenate(
        [scaled.reshape(pair_count, model_dim), jnp.zeros((1, model_dim), jnp.bfloat16)], axis=0
    )
    send_rows = padded_tokens[token_index].reshape(n_expert, exp_dev * capacity, model_dim)
    send_grads = padded_scaled[slot_table].reshape(n_expert, exp_dev * capacity, model_dim)
    recv_rows = lax.all_to_all(send_rows, "expert", split_axis=0, concat_axis=0, tiled=True)
    recv_grads = lax.all_to_all(send_grads, "expert", split_axis=0, concat_axis=0, tiled=True)

    def regroup(received):
        shaped = received.reshape(n_expert, exp_dev, capacity, model_dim)
        return jnp.transpose(shaped, (1, 0, 2, 3)).reshape(exp_dev, slot_count, model_dim)

    local_rows = regroup(recv_rows)
    local_grads = regroup(recv_grads)
    batched_terms = jax.vmap(expert_terms)
    pair_piece, probe_piece, down_piece = lax.all_gather(
        (w_in, v_in, w_out[:, None]), "dp", axis=2, tiled=True
    )
    partials = batched_terms(local_rows, local_grads, pair_piece, probe_piece, down_piece[:, 0])
    return lax.psum_scatter(
        partials.astype(jnp.bfloat16), "dp", scatter_dimension=2, tiled=True
    ).astype(jnp.float32)


CORE, X, Y = 1, 2, 16
Z_NEAR, Z_FAR = 4, 8
LANES = 128


def pack_kernel(
    tok_hbm, cot_hbm, route_hbm, comb_hbm, out_ref, route_ref, comb_ref, sems, *, experts
):
    tok_dev, model_dim = tok_hbm.shape
    tok_at = out_ref.at[pl.ds(0, tok_dev), pl.ds(0, model_dim)]
    cot_at = out_ref.at[pl.ds(tok_dev, tok_dev), pl.ds(0, model_dim)]
    moves = ((route_hbm, route_ref), (comb_hbm, comb_ref), (tok_hbm, tok_at), (cot_hbm, cot_at))
    copies = [pltpu.make_async_copy(*m, sems.at[n]) for n, m in enumerate(moves)]
    for copy in copies:
        copy.start()
    copies[0].wait()
    copies[1].wait()
    line = lax.broadcasted_iota(jnp.int32, (LANES, tok_dev), 0)
    weight = jnp.zeros((LANES, tok_dev), jnp.float32)
    for k in range(route_ref.shape[0]):
        named = route_ref[k : k + 1, :] == line % experts
        weight = jnp.where(named, comb_ref[k : k + 1, :], weight)
    high = weight.astype(jnp.bfloat16).astype(jnp.float32)
    middle = (weight - high).astype(jnp.bfloat16).astype(jnp.float32)
    low = weight - high - middle
    part = line // experts
    zero = jnp.zeros_like(weight)
    value = jnp.where(part == 0, high, jnp.where(part == 1, middle, jnp.where(part == 2, low, zero)))
    row = lax.broadcasted_iota(jnp.int32, (tok_dev, tok_dev), 0)
    column = lax.broadcasted_iota(jnp.int32, (tok_dev, tok_dev), 1)
    same = (row == column).astype(jnp.float32).astype(jnp.bfloat16)
    turned = lax.dot_general(
        same, value.astype(jnp.bfloat16), NT, preferred_element_type=jnp.float32
    )
    out_ref[0:tok_dev, model_dim:] = turned.astype(jnp.bfloat16)
    out_ref[tok_dev:, model_dim:] = jnp.zeros((tok_dev, LANES), jnp.bfloat16)
    copies[2].wait()
    copies[3].wait()


def stack_kernel(flag_ref, *refs, count, layouts):
    for out_ref, parts in zip(refs[count:], layouts):
        row = 0
        for part in parts:
            at = pl.ds(row, part[0][2] if isinstance(part[0], tuple) else part[2])
            if isinstance(part[0], tuple):
                for taken, (n, first, rows) in zip((1, 0), part):

                    @pl.when(flag_ref[0] == taken)
                    def _(n=n, first=first, rows=rows, at=at, out_ref=out_ref):
                        out_ref[at, :] = refs[n][first : first + rows]

            else:
                n, first, rows = part
                out_ref[at, :] = refs[n][first : first + rows]
            row += at.size


def unpack(pieces, x_ref, c_ref, wt_ref, tok_dev):
    model_dim = x_ref.shape[1]
    for row, (piece, first) in enumerate(pieces):
        at = pl.ds(row * tok_dev, tok_dev)
        x_ref[at, :] = piece[first : first + tok_dev, 0:model_dim]
        wt_ref[at, :] = piece[first : first + tok_dev, model_dim:]
        c_ref[at, :] = piece[first + tok_dev : first + 2 * tok_dev, 0:model_dim]


COLUMNS = 512
ROWS = 256


def rows_to_dirs(stacks, pick_ref, shards, x_ref, c_ref, wt_ref, dir_ref, tok_dev):
    w_ref, v_ref, wo_ref = shards
    half = wo_ref.shape[0]
    pieces = [(s, first) for s in stacks for first in range(0, s.shape[0], 2 * tok_dev)]
    for start in range(0, x_ref.shape[0], ROWS):
        part = pieces[start // tok_dev : (start + ROWS) // tok_dev]
        x_at = x_ref.at[pl.ds(start, ROWS)]
        unpack(part, x_at, c_ref, wt_ref, tok_dev)
        weight = lax.dot_general(
            pick_ref[...], wt_ref[...], NT, preferred_element_type=jnp.float32
        )
        both = jnp.concatenate([w_ref[...], v_ref[...]], axis=0)
        seen = lax.dot_general(both, x_at[...], NT, preferred_element_type=jnp.float32)
        back = lax.dot_general(wo_ref[...], c_ref[...], NT, preferred_element_type=jnp.float32)
        parts = [seen[n * half : (n + 1) * half] for n in range(4)]
        gate_dir, up_dir = directions(*parts, back * weight[0:1])
        dir_ref[0:half, start : start + ROWS] = gate_dir
        dir_ref[half:, start : start + ROWS] = up_dir


def early_kernel(
    mine, theirs, pick_ref, w, v, wo, sum_ref, x_ref, dir_ref, c_ref, wt_ref, *, tok_dev
):
    rows_to_dirs((mine, theirs), pick_ref, (w, v, wo), x_ref, c_ref, wt_ref, dir_ref, tok_dev)
    for n in range(sum_ref.shape[1] // COLUMNS):
        at = pl.ds(n * COLUMNS, COLUMNS)
        sum_ref[:, at] = lax.dot_general(
            dir_ref[...], x_ref[:, at], NN, preferred_element_type=jnp.float32
        )


def last_kernel(
    mine, theirs, pick_ref, w, v, wo, add_ref, out_ref, x_ref, dir_ref, c_ref, wt_ref, sum_ref, sems,
    *, tok_dev
):
    rows_to_dirs((mine, theirs), pick_ref, (w, v, wo), x_ref, c_ref, wt_ref, dir_ref, tok_dev)
    copies = []
    for n in range(out_ref.shape[1] // COLUMNS):
        at = pl.ds(n * COLUMNS, COLUMNS)
        total = lax.dot_general(
            dir_ref[...], x_ref[:, at], NN, preferred_element_type=jnp.float32
        )
        sum_ref[:, at] = total + add_ref[:, at]
        copy = pltpu.make_async_copy(sum_ref.at[:, at], out_ref.at[:, at], sems.at[n])
        copy.start()
        copies.append(copy)
    for copy in copies:
        copy.wait()


def swap(value, mask, sender=None):
    axes = ("dp", "expert")
    count = lax.axis_size("dp") * lax.axis_size("expert")
    pairs = [(i, i ^ mask) for i in range(count) if sender is None or sender(i)]
    return lax.ppermute(value, axes, pairs)


def inner(place):
    return (place & Z_NEAR) // Z_NEAR != (place & Z_FAR) // Z_FAR


def after(value, *others):
    return lax.optimization_barrier((value, *others))[0]


def tied(values, *others):
    return list(lax.optimization_barrier((*values, *others)))[: len(values)]


def dense(tokens, cotangent, routes, combine, w_in, w_out, v_in):
    experts = lax.axis_size("expert")
    tok_dev, model_dim = tokens.shape
    half = w_in.shape[2]
    wide = model_dim + LANES
    inside = pl.BlockSpec(memory_space=pltpu.VMEM)
    own = pl.pallas_call(
        functools.partial(pack_kernel, experts=experts),
        in_specs=[pl.BlockSpec(memory_space=pl.ANY)] * 4,
        out_specs=inside,
        out_shape=jax.ShapeDtypeStruct((2 * tok_dev, wide), jnp.bfloat16),
        scratch_shapes=[
            pltpu.VMEM(routes.shape[::-1], jnp.int32),
            pltpu.VMEM(combine.shape[::-1], jnp.float32),
            pltpu.SemaphoreType.DMA((4,)),
        ],
        compiler_params=pltpu.CompilerParams(vmem_limit_bytes=63_120_000),
    )(tokens, cotangent, routes.T, combine.T)

    lane = jnp.arange(LANES, dtype=jnp.int32)[None, :]
    expert = lax.axis_index("expert")
    pick = ((lane % experts == expert) & (lane < 3 * experts)).astype(jnp.bfloat16)
    pick = jnp.broadcast_to(pick, (16, LANES))
    is_inner = inner(expert)
    shards = (
        w_in.reshape(2 * half, model_dim),
        v_in.reshape(2 * half, model_dim),
        w_out.reshape(half, model_dim),
    )

    def call(kernel, stack, theirs, more, out_spec, scratch, limit):
        rows = stack.shape[0]
        operands = (stack, theirs, pick, *shards, *more)
        return pl.pallas_call(
            functools.partial(kernel, tok_dev=tok_dev),
            in_specs=[inside] * len(operands),
            out_specs=out_spec,
            out_shape=jax.ShapeDtypeStruct((2 * half, model_dim), jnp.float32),
            scratch_shapes=[
                pltpu.VMEM((rows, model_dim), jnp.bfloat16),
                pltpu.VMEM((2 * half, rows), jnp.bfloat16),
                pltpu.VMEM((ROWS, model_dim), jnp.bfloat16),
                pltpu.VMEM((ROWS, LANES), jnp.bfloat16),
            ]
            + scratch,
            compiler_params=pltpu.CompilerParams(vmem_limit_bytes=limit * 2**20),
            cost_estimate=pl.CostEstimate(
                flops=2 * rows * model_dim * 7 * half,
                bytes_accessed=12 * 2**20,
                transcendentals=rows * half,
            ),
        )(*operands)

    flag = is_inner.astype(jnp.int32)[None]
    block = 2 * tok_dev

    def stack(inputs, *layouts):
        def size(part):
            return part[0][2] if isinstance(part[0], tuple) else part[2]

        return pl.pallas_call(
            functools.partial(stack_kernel, count=len(inputs), layouts=layouts),
            in_specs=[pl.BlockSpec(memory_space=pltpu.SMEM)] + [inside] * len(inputs),
            out_specs=[inside] * len(layouts),
            out_shape=[
                jax.ShapeDtypeStruct((sum(map(size, parts)), wide), jnp.bfloat16)
                for parts in layouts
            ],
            compiler_params=pltpu.CompilerParams(vmem_limit_bytes=2 * 2**20),
        )(flag, *inputs)

    def rows_of(n, first=0, count=1):
        return (n, first * block, count * block)

    order = (Z_NEAR ^ Z_FAR, X ^ Y, X, Y, Z_NEAR)
    middle, across, beside_x, beside_y, near = tied([swap(own, m) for m in order])

    ready = stack(
        [near, middle, across],
        *[[rows_of(0), rows_of(1)]] * 3,
        [rows_of(0), rows_of(2)],
        [rows_of(1), rows_of(2)],
    )
    pair, pair_x, pair_y, through, outward = ready
    pair_x, pair_y = swap(pair_x, X), swap(pair_y, Y)
    through = swap(through, Z_NEAR ^ Z_FAR, inner)
    outward = swap(outward, Z_NEAR)

    (held,) = stack([after(own, near)], [rows_of(0)])
    pair_x, pair_y, through, outward, held = tied([pair_x, pair_y, through, outward, held])

    beyond, far_x, far_y, far, relayed = stack(
        [through, outward, middle],
        [(rows_of(0), rows_of(2))],
        *[[(rows_of(0), rows_of(1))]] * 3,
        [rows_of(0, 1)],
    )
    third = [swap(beyond, X ^ Y), swap(far_x, X), swap(far_y, Y), swap(relayed, Z_NEAR, inner)]
    (stack_a,) = stack(
        [held, beside_x, beside_y, across, pair, pair_x, pair_y, far, outward],
        [rows_of(n) for n in range(4)]
        + [rows_of(n, 0, 2) for n in range(4, 7)]
        + [rows_of(7), rows_of(8, 1)],
    )
    total = call(early_kernel, stack_a, swap(stack_a, CORE), (), inside, [], 14)
    *third, total = tied([*third, total])

    (stack_b,) = stack(
        [*third, through],
        [rows_of(0), rows_of(1), rows_of(2), (rows_of(4, 1), rows_of(3))],
    )
    scratch = [
        pltpu.VMEM((2 * half, model_dim), jnp.float32),
        pltpu.SemaphoreType.DMA((model_dim // COLUMNS,)),
    ]
    outside = pl.BlockSpec(memory_space=pl.ANY)
    out = call(last_kernel, stack_b, swap(stack_b, CORE), (total,), outside, scratch, 11)
    return out.reshape(1, 2, half, model_dim)


def local(tokens, cotangent, routes, combine, w_in, w_out, v_in):
    experts = lax.axis_size("expert") * w_in.shape[0]
    tok_dev, top_k = routes.shape
    sizes = (lax.axis_size("dp"), lax.axis_size("expert"))
    if sizes == (2, 16) and w_in.shape[0] == 1 and 2 * tok_dev * top_k // experts >= tok_dev:
        return dense(tokens, cotangent, routes, combine, w_in, w_out, v_in)
    return dispatched(tokens, cotangent, routes, combine, w_in, w_out, v_in)


def solution(mesh):
    in_specs = (
        P(("dp", "expert"), None),
        P(("dp", "expert"), None),
        P(("dp", "expert"), None),
        P(("dp", "expert"), None),
        P("expert", None, "dp", None),
        P("expert", "dp", None),
        P("expert", None, "dp", None),
    )
    out_specs = P("expert", None, "dp", None)
    return jax.shard_map(local, mesh=mesh, in_specs=in_specs, out_specs=out_specs, check_vma=False)
```

```python
import functools

import jax
import jax.numpy as jnp
from jax import lax
from jax.experimental import pallas as pl
from jax.experimental.pallas import tpu as pltpu
from jax.sharding import PartitionSpec as P

NT = (((1,), (1,)), ((), ()))
NN = (((1,), (0,)), ((), ()))


def expert_terms(slot_rows, slot_grads, w_pair, v_pair, w_down):
    hidden_width = w_pair.shape[1]
    model_dim = w_pair.shape[2]
    stacked = jnp.concatenate([w_pair, v_pair], axis=0).reshape(4 * hidden_width, model_dim)
    projected = lax.dot_general(slot_rows, stacked, NT, preferred_element_type=jnp.float32)
    pre_gate = projected[:, :hidden_width]
    pre_up = projected[:, hidden_width : 2 * hidden_width]
    tan_gate = projected[:, 2 * hidden_width : 3 * hidden_width]
    tan_up = projected[:, 3 * hidden_width :]
    back_grad = lax.dot_general(slot_grads, w_down, NT, preferred_element_type=jnp.float32)
    gate_dir, up_dir = directions(pre_gate, pre_up, tan_gate, tan_up, back_grad)
    gate_term = lax.dot_general(
        gate_dir, slot_rows, (((0,), (0,)), ((), ())), preferred_element_type=jnp.float32
    )
    up_term = lax.dot_general(
        up_dir, slot_rows, (((0,), (0,)), ((), ())), preferred_element_type=jnp.float32
    )
    return jnp.stack([gate_term, up_term], axis=0)


def directions(pre_gate, pre_up, tan_gate, tan_up, back_grad):
    gate_sig = jax.nn.sigmoid(pre_gate)
    first_deriv = gate_sig * (1.0 + pre_gate * (1.0 - gate_sig))
    second_deriv = gate_sig * (1.0 - gate_sig) * (2.0 + pre_gate * (1.0 - 2.0 * gate_sig))
    gate_dir = back_grad * (tan_up * first_deriv + pre_up * second_deriv * tan_gate)
    up_dir = back_grad * first_deriv * tan_gate
    return gate_dir.astype(jnp.bfloat16), up_dir.astype(jnp.bfloat16)


def dispatched(tokens, cotangent, routes, combine, w_in, w_out, v_in):
    n_expert = lax.axis_size("expert")
    exp_dev = w_in.shape[0]
    experts = n_expert * exp_dev
    tok_dev, top_k = routes.shape
    model_dim = tokens.shape[1]
    capacity = 2 * tok_dev * top_k // experts
    pair_count = tok_dev * top_k
    slot_count = n_expert * capacity
    flat_routes = routes.reshape(pair_count)
    onehot = (flat_routes[:, None] == jnp.arange(experts, dtype=jnp.int32)[None, :]).astype(
        jnp.int32
    )
    earlier = jnp.cumsum(onehot, axis=0) - onehot
    slot_rank = jnp.sum(earlier * onehot, axis=1)
    position = flat_routes * capacity + slot_rank
    slot_table = jnp.full((experts * capacity,), pair_count, jnp.int32)
    slot_table = slot_table.at[position].set(jnp.arange(pair_count, dtype=jnp.int32))
    token_index = slot_table // top_k
    padded_tokens = jnp.concatenate([tokens, jnp.zeros((1, model_dim), jnp.bfloat16)], axis=0)
    scaled = (combine[:, :, None] * cotangent[:, None, :].astype(jnp.float32)).astype(jnp.bfloat16)
    padded_scaled = jnp.concatenate(
        [scaled.reshape(pair_count, model_dim), jnp.zeros((1, model_dim), jnp.bfloat16)], axis=0
    )
    send_rows = padded_tokens[token_index].reshape(n_expert, exp_dev * capacity, model_dim)
    send_grads = padded_scaled[slot_table].reshape(n_expert, exp_dev * capacity, model_dim)
    recv_rows = lax.all_to_all(send_rows, "expert", split_axis=0, concat_axis=0, tiled=True)
    recv_grads = lax.all_to_all(send_grads, "expert", split_axis=0, concat_axis=0, tiled=True)

    def regroup(received):
        shaped = received.reshape(n_expert, exp_dev, capacity, model_dim)
        return jnp.transpose(shaped, (1, 0, 2, 3)).reshape(exp_dev, slot_count, model_dim)

    local_rows = regroup(recv_rows)
    local_grads = regroup(recv_grads)
    batched_terms = jax.vmap(expert_terms)
    pair_piece, probe_piece, down_piece = lax.all_gather(
        (w_in, v_in, w_out[:, None]), "dp", axis=2, tiled=True
    )
    partials = batched_terms(local_rows, local_grads, pair_piece, probe_piece, down_piece[:, 0])
    return lax.psum_scatter(
        partials.astype(jnp.bfloat16), "dp", scatter_dimension=2, tiled=True
    ).astype(jnp.float32)


CORE, X, Y = 1, 2, 16
Z_NEAR, Z_FAR = 4, 8
LANES = 128


def pack_kernel(
    tok_hbm, cot_hbm, route_hbm, comb_hbm, out_ref, route_ref, comb_ref, sems, *, experts
):
    tok_dev, model_dim = tok_hbm.shape
    tok_at = out_ref.at[pl.ds(0, tok_dev), pl.ds(0, model_dim)]
    cot_at = out_ref.at[pl.ds(tok_dev, tok_dev), pl.ds(0, model_dim)]
    moves = ((route_hbm, route_ref), (comb_hbm, comb_ref), (tok_hbm, tok_at), (cot_hbm, cot_at))
    copies = [pltpu.make_async_copy(*m, sems.at[n]) for n, m in enumerate(moves)]
    for copy in copies:
        copy.start()
    copies[0].wait()
    copies[1].wait()
    line = lax.broadcasted_iota(jnp.int32, (LANES, tok_dev), 0)
    weight = jnp.zeros((LANES, tok_dev), jnp.float32)
    for k in range(route_ref.shape[0]):
        named = route_ref[k : k + 1, :] == line % experts
        weight = jnp.where(named, comb_ref[k : k + 1, :], weight)
    high = weight.astype(jnp.bfloat16).astype(jnp.float32)
    middle = (weight - high).astype(jnp.bfloat16).astype(jnp.float32)
    low = weight - high - middle
    part = line // experts
    zero = jnp.zeros_like(weight)
    value = jnp.where(part == 0, high, jnp.where(part == 1, middle, jnp.where(part == 2, low, zero)))
    row = lax.broadcasted_iota(jnp.int32, (tok_dev, tok_dev), 0)
    column = lax.broadcasted_iota(jnp.int32, (tok_dev, tok_dev), 1)
    same = (row == column).astype(jnp.float32).astype(jnp.bfloat16)
    turned = lax.dot_general(
        same, value.astype(jnp.bfloat16), NT, preferred_element_type=jnp.float32
    )
    out_ref[0:tok_dev, model_dim:] = turned.astype(jnp.bfloat16)
    out_ref[tok_dev:, model_dim:] = jnp.zeros((tok_dev, LANES), jnp.bfloat16)
    copies[2].wait()
    copies[3].wait()


def stack_kernel(flag_ref, *refs, count, layouts):
    for out_ref, parts in zip(refs[count:], layouts):
        row = 0
        for part in parts:
            at = pl.ds(row, part[0][2] if isinstance(part[0], tuple) else part[2])
            if isinstance(part[0], tuple):
                for taken, (n, first, rows) in zip((1, 0), part):

                    @pl.when(flag_ref[0] == taken)
                    def _(n=n, first=first, rows=rows, at=at, out_ref=out_ref):
                        out_ref[at, :] = refs[n][first : first + rows]

            else:
                n, first, rows = part
                out_ref[at, :] = refs[n][first : first + rows]
            row += at.size


def unpack(pieces, x_ref, c_ref, wt_ref, tok_dev):
    model_dim = x_ref.shape[1]
    for row, (piece, first) in enumerate(pieces):
        at = pl.ds(row * tok_dev, tok_dev)
        x_ref[at, :] = piece[first : first + tok_dev, 0:model_dim]
        wt_ref[at, :] = piece[first : first + tok_dev, model_dim:]
        c_ref[at, :] = piece[first + tok_dev : first + 2 * tok_dev, 0:model_dim]


COLUMNS = 512
ROWS = 256


def rows_to_dirs(stacks, pick_ref, shards, x_ref, c_ref, wt_ref, dir_ref, tok_dev):
    w_ref, v_ref, wo_ref = shards
    half = wo_ref.shape[0]
    pieces = [(s, first) for s in stacks for first in range(0, s.shape[0], 2 * tok_dev)]
    for start in range(0, x_ref.shape[0], ROWS):
        part = pieces[start // tok_dev : (start + ROWS) // tok_dev]
        x_at = x_ref.at[pl.ds(start, ROWS)]
        unpack(part, x_at, c_ref, wt_ref, tok_dev)
        weight = lax.dot_general(
            pick_ref[...], wt_ref[...], NT, preferred_element_type=jnp.float32
        )
        both = jnp.concatenate([w_ref[...], v_ref[...]], axis=0)
        seen = lax.dot_general(both, x_at[...], NT, preferred_element_type=jnp.float32)
        back = lax.dot_general(wo_ref[...], c_ref[...], NT, preferred_element_type=jnp.float32)
        parts = [seen[n * half : (n + 1) * half] for n in range(4)]
        gate_dir, up_dir = directions(*parts, back * weight[0:1])
        dir_ref[0:half, start : start + ROWS] = gate_dir
        dir_ref[half:, start : start + ROWS] = up_dir


def early_kernel(
    mine, theirs, pick_ref, w, v, wo, sum_ref, x_ref, dir_ref, c_ref, wt_ref, *, tok_dev
):
    rows_to_dirs((mine, theirs), pick_ref, (w, v, wo), x_ref, c_ref, wt_ref, dir_ref, tok_dev)
    for n in range(sum_ref.shape[1] // COLUMNS):
        at = pl.ds(n * COLUMNS, COLUMNS)
        sum_ref[:, at] = lax.dot_general(
            dir_ref[...], x_ref[:, at], NN, preferred_element_type=jnp.float32
        )


def last_kernel(
    mine, theirs, pick_ref, w, v, wo, add_ref, out_ref, x_ref, dir_ref, c_ref, wt_ref, sum_ref, sems,
    *, tok_dev
):
    rows_to_dirs((mine, theirs), pick_ref, (w, v, wo), x_ref, c_ref, wt_ref, dir_ref, tok_dev)
    copies = []
    for n in range(out_ref.shape[1] // COLUMNS):
        at = pl.ds(n * COLUMNS, COLUMNS)
        total = lax.dot_general(
            dir_ref[...], x_ref[:, at], NN, preferred_element_type=jnp.float32
        )
        sum_ref[:, at] = total + add_ref[:, at]
        copy = pltpu.make_async_copy(sum_ref.at[:, at], out_ref.at[:, at], sems.at[n])
        copy.start()
        copies.append(copy)
    for copy in copies:
        copy.wait()


def swap(value, mask, sender=None):
    axes = ("dp", "expert")
    count = lax.axis_size("dp") * lax.axis_size("expert")
    pairs = [(i, i ^ mask) for i in range(count) if sender is None or sender(i)]
    return lax.ppermute(value, axes, pairs)


def inner(place):
    return (place & Z_NEAR) // Z_NEAR != (place & Z_FAR) // Z_FAR


def after(value, *others):
    return lax.optimization_barrier((value, *others))[0]


def tied(values, *others):
    return list(lax.optimization_barrier((*values, *others)))[: len(values)]


def dense(tokens, cotangent, routes, combine, w_in, w_out, v_in):
    experts = lax.axis_size("expert")
    tok_dev, model_dim = tokens.shape
    half = w_in.shape[2]
    wide = model_dim + LANES
    inside = pl.BlockSpec(memory_space=pltpu.VMEM)
    own = pl.pallas_call(
        functools.partial(pack_kernel, experts=experts),
        in_specs=[pl.BlockSpec(memory_space=pl.ANY)] * 4,
        out_specs=inside,
        out_shape=jax.ShapeDtypeStruct((2 * tok_dev, wide), jnp.bfloat16),
        scratch_shapes=[
            pltpu.VMEM(routes.shape[::-1], jnp.int32),
            pltpu.VMEM(combine.shape[::-1], jnp.float32),
            pltpu.SemaphoreType.DMA((4,)),
        ],
        compiler_params=pltpu.CompilerParams(vmem_limit_bytes=63_120_000),
    )(tokens, cotangent, routes.T, combine.T)

    lane = jnp.arange(LANES, dtype=jnp.int32)[None, :]
    expert = lax.axis_index("expert")
    pick = ((lane % experts == expert) & (lane < 3 * experts)).astype(jnp.bfloat16)
    pick = jnp.broadcast_to(pick, (16, LANES))
    is_inner = inner(expert)
    shards = (
        w_in.reshape(2 * half, model_dim),
        v_in.reshape(2 * half, model_dim),
        w_out.reshape(half, model_dim),
    )

    def call(kernel, stack, theirs, more, out_spec, scratch, limit):
        rows = stack.shape[0]
        operands = (stack, theirs, pick, *shards, *more)
        return pl.pallas_call(
            functools.partial(kernel, tok_dev=tok_dev),
            in_specs=[inside] * len(operands),
            out_specs=out_spec,
            out_shape=jax.ShapeDtypeStruct((2 * half, model_dim), jnp.float32),
            scratch_shapes=[
                pltpu.VMEM((rows, model_dim), jnp.bfloat16),
                pltpu.VMEM((2 * half, rows), jnp.bfloat16),
                pltpu.VMEM((ROWS, model_dim), jnp.bfloat16),
                pltpu.VMEM((ROWS, LANES), jnp.bfloat16),
            ]
            + scratch,
            compiler_params=pltpu.CompilerParams(vmem_limit_bytes=limit * 2**20),
            cost_estimate=pl.CostEstimate(
                flops=2 * rows * model_dim * 7 * half,
                bytes_accessed=12 * 2**20,
                transcendentals=rows * half,
            ),
        )(*operands)

    flag = is_inner.astype(jnp.int32)[None]
    block = 2 * tok_dev

    def stack(inputs, *layouts):
        def size(part):
            return part[0][2] if isinstance(part[0], tuple) else part[2]

        return pl.pallas_call(
            functools.partial(stack_kernel, count=len(inputs), layouts=layouts),
            in_specs=[pl.BlockSpec(memory_space=pltpu.SMEM)] + [inside] * len(inputs),
            out_specs=[inside] * len(layouts),
            out_shape=[
                jax.ShapeDtypeStruct((sum(map(size, parts)), wide), jnp.bfloat16)
                for parts in layouts
            ],
            compiler_params=pltpu.CompilerParams(vmem_limit_bytes=2 * 2**20),
        )(flag, *inputs)

    def rows_of(n, first=0, count=1):
        return (n, first * block, count * block)

    order = (Z_NEAR, Y, X, X ^ Y, Z_NEAR ^ Z_FAR)
    near, beside_y, beside_x, across, middle = tied([swap(own, m) for m in order])

    ready = stack(
        [near, middle, across],
        *[[rows_of(0), rows_of(1)]] * 3,
        [rows_of(0), rows_of(2)],
        [rows_of(1), rows_of(2)],
    )
    pair, pair_x, pair_y, through, outward = ready
    pair_x, pair_y = swap(pair_x, X), swap(pair_y, Y)
    through = swap(through, Z_NEAR ^ Z_FAR, inner)
    outward = swap(outward, Z_NEAR)

    (held,) = stack([after(own, near)], [rows_of(0)])
    pair_x, pair_y, through, outward, held = tied([pair_x, pair_y, through, outward, held])

    beyond, far_x, far_y, far, relayed = stack(
        [through, outward, middle],
        [(rows_of(0), rows_of(2))],
        *[[(rows_of(0), rows_of(1))]] * 3,
        [rows_of(0, 1)],
    )
    third = [swap(beyond, X ^ Y), swap(far_x, X), swap(far_y, Y), swap(relayed, Z_NEAR, inner)]
    (stack_a,) = stack(
        [held, beside_x, beside_y, across, pair, pair_x, pair_y, far, outward],
        [rows_of(n) for n in range(4)]
        + [rows_of(n, 0, 2) for n in range(4, 7)]
        + [rows_of(7), rows_of(8, 1)],
    )
    total = call(early_kernel, stack_a, swap(stack_a, CORE), (), inside, [], 14)
    *third, total = tied([*third, total])

    (stack_b,) = stack(
        [*third, through],
        [rows_of(0), rows_of(1), rows_of(2), (rows_of(4, 1), rows_of(3))],
    )
    scratch = [
        pltpu.VMEM((2 * half, model_dim), jnp.float32),
        pltpu.SemaphoreType.DMA((model_dim // COLUMNS,)),
    ]
    outside = pl.BlockSpec(memory_space=pl.ANY)
    out = call(last_kernel, stack_b, swap(stack_b, CORE), (total,), outside, scratch, 11)
    return out.reshape(1, 2, half, model_dim)


def local(tokens, cotangent, routes, combine, w_in, w_out, v_in):
    experts = lax.axis_size("expert") * w_in.shape[0]
    tok_dev, top_k = routes.shape
    sizes = (lax.axis_size("dp"), lax.axis_size("expert"))
    if sizes == (2, 16) and w_in.shape[0] == 1 and 2 * tok_dev * top_k // experts >= tok_dev:
        return dense(tokens, cotangent, routes, combine, w_in, w_out, v_in)
    return dispatched(tokens, cotangent, routes, combine, w_in, w_out, v_in)


def solution(mesh):
    in_specs = (
        P(("dp", "expert"), None),
        P(("dp", "expert"), None),
        P(("dp", "expert"), None),
        P(("dp", "expert"), None),
        P("expert", None, "dp", None),
        P("expert", "dp", None),
        P("expert", None, "dp", None),
    )
    out_specs = P("expert", None, "dp", None)
    return jax.shard_map(local, mesh=mesh, in_specs=in_specs, out_specs=out_specs, check_vma=False)
```

```python
import functools

import jax
import jax.numpy as jnp
from jax import lax
from jax.experimental import pallas as pl
from jax.experimental.pallas import tpu as pltpu
from jax.sharding import PartitionSpec as P

NT = (((1,), (1,)), ((), ()))
NN = (((1,), (0,)), ((), ()))


def expert_terms(slot_rows, slot_grads, w_pair, v_pair, w_down):
    hidden_width = w_pair.shape[1]
    model_dim = w_pair.shape[2]
    stacked = jnp.concatenate([w_pair, v_pair], axis=0).reshape(4 * hidden_width, model_dim)
    projected = lax.dot_general(slot_rows, stacked, NT, preferred_element_type=jnp.float32)
    pre_gate = projected[:, :hidden_width]
    pre_up = projected[:, hidden_width : 2 * hidden_width]
    tan_gate = projected[:, 2 * hidden_width : 3 * hidden_width]
    tan_up = projected[:, 3 * hidden_width :]
    back_grad = lax.dot_general(slot_grads, w_down, NT, preferred_element_type=jnp.float32)
    gate_dir, up_dir = directions(pre_gate, pre_up, tan_gate, tan_up, back_grad)
    gate_term = lax.dot_general(
        gate_dir, slot_rows, (((0,), (0,)), ((), ())), preferred_element_type=jnp.float32
    )
    up_term = lax.dot_general(
        up_dir, slot_rows, (((0,), (0,)), ((), ())), preferred_element_type=jnp.float32
    )
    return jnp.stack([gate_term, up_term], axis=0)


def directions(pre_gate, pre_up, tan_gate, tan_up, back_grad):
    gate_sig = jax.nn.sigmoid(pre_gate)
    first_deriv = gate_sig * (1.0 + pre_gate * (1.0 - gate_sig))
    second_deriv = gate_sig * (1.0 - gate_sig) * (2.0 + pre_gate * (1.0 - 2.0 * gate_sig))
    gate_dir = back_grad * (tan_up * first_deriv + pre_up * second_deriv * tan_gate)
    up_dir = back_grad * first_deriv * tan_gate
    return gate_dir.astype(jnp.bfloat16), up_dir.astype(jnp.bfloat16)


def dispatched(tokens, cotangent, routes, combine, w_in, w_out, v_in):
    n_expert = lax.axis_size("expert")
    exp_dev = w_in.shape[0]
    experts = n_expert * exp_dev
    tok_dev, top_k = routes.shape
    model_dim = tokens.shape[1]
    capacity = 2 * tok_dev * top_k // experts
    pair_count = tok_dev * top_k
    slot_count = n_expert * capacity
    flat_routes = routes.reshape(pair_count)
    onehot = (flat_routes[:, None] == jnp.arange(experts, dtype=jnp.int32)[None, :]).astype(
        jnp.int32
    )
    earlier = jnp.cumsum(onehot, axis=0) - onehot
    slot_rank = jnp.sum(earlier * onehot, axis=1)
    position = flat_routes * capacity + slot_rank
    slot_table = jnp.full((experts * capacity,), pair_count, jnp.int32)
    slot_table = slot_table.at[position].set(jnp.arange(pair_count, dtype=jnp.int32))
    token_index = slot_table // top_k
    padded_tokens = jnp.concatenate([tokens, jnp.zeros((1, model_dim), jnp.bfloat16)], axis=0)
    scaled = (combine[:, :, None] * cotangent[:, None, :].astype(jnp.float32)).astype(jnp.bfloat16)
    padded_scaled = jnp.concatenate(
        [scaled.reshape(pair_count, model_dim), jnp.zeros((1, model_dim), jnp.bfloat16)], axis=0
    )
    send_rows = padded_tokens[token_index].reshape(n_expert, exp_dev * capacity, model_dim)
    send_grads = padded_scaled[slot_table].reshape(n_expert, exp_dev * capacity, model_dim)
    recv_rows = lax.all_to_all(send_rows, "expert", split_axis=0, concat_axis=0, tiled=True)
    recv_grads = lax.all_to_all(send_grads, "expert", split_axis=0, concat_axis=0, tiled=True)

    def regroup(received):
        shaped = received.reshape(n_expert, exp_dev, capacity, model_dim)
        return jnp.transpose(shaped, (1, 0, 2, 3)).reshape(exp_dev, slot_count, model_dim)

    local_rows = regroup(recv_rows)
    local_grads = regroup(recv_grads)
    batched_terms = jax.vmap(expert_terms)
    pair_piece, probe_piece, down_piece = lax.all_gather(
        (w_in, v_in, w_out[:, None]), "dp", axis=2, tiled=True
    )
    partials = batched_terms(local_rows, local_grads, pair_piece, probe_piece, down_piece[:, 0])
    return lax.psum_scatter(
        partials.astype(jnp.bfloat16), "dp", scatter_dimension=2, tiled=True
    ).astype(jnp.float32)


CORE, X, Y = 1, 2, 16
Z_NEAR, Z_FAR = 4, 8
LANES = 128


def pack_kernel(
    tok_hbm, cot_hbm, route_hbm, comb_hbm, out_ref, route_ref, comb_ref, sems, *, experts
):
    tok_dev, model_dim = tok_hbm.shape
    tok_at = out_ref.at[pl.ds(0, tok_dev), pl.ds(0, model_dim)]
    cot_at = out_ref.at[pl.ds(tok_dev, tok_dev), pl.ds(0, model_dim)]
    moves = ((route_hbm, route_ref), (comb_hbm, comb_ref), (tok_hbm, tok_at), (cot_hbm, cot_at))
    copies = [pltpu.make_async_copy(*m, sems.at[n]) for n, m in enumerate(moves)]
    for copy in copies:
        copy.start()
    copies[0].wait()
    copies[1].wait()
    line = lax.broadcasted_iota(jnp.int32, (LANES, tok_dev), 0)
    weight = jnp.zeros((LANES, tok_dev), jnp.float32)
    for k in range(route_ref.shape[0]):
        named = route_ref[k : k + 1, :] == line % experts
        weight = jnp.where(named, comb_ref[k : k + 1, :], weight)
    high = weight.astype(jnp.bfloat16).astype(jnp.float32)
    middle = (weight - high).astype(jnp.bfloat16).astype(jnp.float32)
    low = weight - high - middle
    part = line // experts
    zero = jnp.zeros_like(weight)
    value = jnp.where(part == 0, high, jnp.where(part == 1, middle, jnp.where(part == 2, low, zero)))
    row = lax.broadcasted_iota(jnp.int32, (tok_dev, tok_dev), 0)
    column = lax.broadcasted_iota(jnp.int32, (tok_dev, tok_dev), 1)
    same = (row == column).astype(jnp.float32).astype(jnp.bfloat16)
    turned = lax.dot_general(
        same, value.astype(jnp.bfloat16), NT, preferred_element_type=jnp.float32
    )
    out_ref[0:tok_dev, model_dim:] = turned.astype(jnp.bfloat16)
    out_ref[tok_dev:, model_dim:] = jnp.zeros((tok_dev, LANES), jnp.bfloat16)
    copies[2].wait()
    copies[3].wait()


def stack_kernel(flag_ref, *refs, count, layouts):
    for out_ref, parts in zip(refs[count:], layouts):
        row = 0
        for part in parts:
            at = pl.ds(row, part[0][2] if isinstance(part[0], tuple) else part[2])
            if isinstance(part[0], tuple):
                for taken, (n, first, rows) in zip((1, 0), part):

                    @pl.when(flag_ref[0] == taken)
                    def _(n=n, first=first, rows=rows, at=at, out_ref=out_ref):
                        out_ref[at, :] = refs[n][first : first + rows]

            else:
                n, first, rows = part
                out_ref[at, :] = refs[n][first : first + rows]
            row += at.size


def unpack(pieces, x_ref, c_ref, wt_ref, tok_dev):
    model_dim = x_ref.shape[1]
    for row, (piece, first) in enumerate(pieces):
        at = pl.ds(row * tok_dev, tok_dev)
        x_ref[at, :] = piece[first : first + tok_dev, 0:model_dim]
        wt_ref[at, :] = piece[first : first + tok_dev, model_dim:]
        c_ref[at, :] = piece[first + tok_dev : first + 2 * tok_dev, 0:model_dim]


COLUMNS = 512
ROWS = 256


def rows_to_dirs(stacks, pick_ref, shards, x_ref, c_ref, wt_ref, dir_ref, tok_dev):
    w_ref, v_ref, wo_ref = shards
    half = wo_ref.shape[0]
    pieces = [(s, first) for s in stacks for first in range(0, s.shape[0], 2 * tok_dev)]
    for start in range(0, x_ref.shape[0], ROWS):
        part = pieces[start // tok_dev : (start + ROWS) // tok_dev]
        x_at = x_ref.at[pl.ds(start, ROWS)]
        unpack(part, x_at, c_ref, wt_ref, tok_dev)
        weight = lax.dot_general(
            pick_ref[...], wt_ref[...], NT, preferred_element_type=jnp.float32
        )
        both = jnp.concatenate([w_ref[...], v_ref[...]], axis=0)
        seen = lax.dot_general(both, x_at[...], NT, preferred_element_type=jnp.float32)
        back = lax.dot_general(wo_ref[...], c_ref[...], NT, preferred_element_type=jnp.float32)
        parts = [seen[n * half : (n + 1) * half] for n in range(4)]
        gate_dir, up_dir = directions(*parts, back * weight[0:1])
        dir_ref[0:half, start : start + ROWS] = gate_dir
        dir_ref[half:, start : start + ROWS] = up_dir


def early_kernel(
    mine, theirs, pick_ref, w, v, wo, sum_ref, x_ref, dir_ref, c_ref, wt_ref, *, tok_dev
):
    rows_to_dirs((mine, theirs), pick_ref, (w, v, wo), x_ref, c_ref, wt_ref, dir_ref, tok_dev)
    for n in range(sum_ref.shape[1] // COLUMNS):
        at = pl.ds(n * COLUMNS, COLUMNS)
        sum_ref[:, at] = lax.dot_general(
            dir_ref[...], x_ref[:, at], NN, preferred_element_type=jnp.float32
        )


def last_kernel(
    mine, theirs, pick_ref, w, v, wo, add_ref, out_ref, x_ref, dir_ref, c_ref, wt_ref, sum_ref, sems,
    *, tok_dev
):
    rows_to_dirs((mine, theirs), pick_ref, (w, v, wo), x_ref, c_ref, wt_ref, dir_ref, tok_dev)
    copies = []
    for n in range(out_ref.shape[1] // COLUMNS):
        at = pl.ds(n * COLUMNS, COLUMNS)
        total = lax.dot_general(
            dir_ref[...], x_ref[:, at], NN, preferred_element_type=jnp.float32
        )
        sum_ref[:, at] = total + add_ref[:, at]
        copy = pltpu.make_async_copy(sum_ref.at[:, at], out_ref.at[:, at], sems.at[n])
        copy.start()
        copies.append(copy)
    for copy in copies:
        copy.wait()


def swap(value, mask, sender=None):
    axes = ("dp", "expert")
    count = lax.axis_size("dp") * lax.axis_size("expert")
    pairs = [(i, i ^ mask) for i in range(count) if sender is None or sender(i)]
    return lax.ppermute(value, axes, pairs)


def inner(place):
    return (place & Z_NEAR) // Z_NEAR != (place & Z_FAR) // Z_FAR


def after(value, *others):
    return lax.optimization_barrier((value, *others))[0]


def tied(values, *others):
    return list(lax.optimization_barrier((*values, *others)))[: len(values)]


def dense(tokens, cotangent, routes, combine, w_in, w_out, v_in):
    experts = lax.axis_size("expert")
    tok_dev, model_dim = tokens.shape
    half = w_in.shape[2]
    wide = model_dim + LANES
    inside = pl.BlockSpec(memory_space=pltpu.VMEM)
    own = pl.pallas_call(
        functools.partial(pack_kernel, experts=experts),
        in_specs=[pl.BlockSpec(memory_space=pl.ANY)] * 4,
        out_specs=inside,
        out_shape=jax.ShapeDtypeStruct((2 * tok_dev, wide), jnp.bfloat16),
        scratch_shapes=[
            pltpu.VMEM(routes.shape[::-1], jnp.int32),
            pltpu.VMEM(combine.shape[::-1], jnp.float32),
            pltpu.SemaphoreType.DMA((4,)),
        ],
        compiler_params=pltpu.CompilerParams(vmem_limit_bytes=63_120_000),
    )(tokens, cotangent, routes.T, combine.T)

    lane = jnp.arange(LANES, dtype=jnp.int32)[None, :]
    expert = lax.axis_index("expert")
    pick = ((lane % experts == expert) & (lane < 3 * experts)).astype(jnp.bfloat16)
    pick = jnp.broadcast_to(pick, (16, LANES))
    is_inner = inner(expert)
    shards = (
        w_in.reshape(2 * half, model_dim),
        v_in.reshape(2 * half, model_dim),
        w_out.reshape(half, model_dim),
    )

    def call(kernel, stack, theirs, more, out_spec, scratch, limit):
        rows = stack.shape[0]
        operands = (stack, theirs, pick, *shards, *more)
        return pl.pallas_call(
            functools.partial(kernel, tok_dev=tok_dev),
            in_specs=[inside] * len(operands),
            out_specs=out_spec,
            out_shape=jax.ShapeDtypeStruct((2 * half, model_dim), jnp.float32),
            scratch_shapes=[
                pltpu.VMEM((rows, model_dim), jnp.bfloat16),
                pltpu.VMEM((2 * half, rows), jnp.bfloat16),
                pltpu.VMEM((ROWS, model_dim), jnp.bfloat16),
                pltpu.VMEM((ROWS, LANES), jnp.bfloat16),
            ]
            + scratch,
            compiler_params=pltpu.CompilerParams(vmem_limit_bytes=limit * 2**20),
            cost_estimate=pl.CostEstimate(
                flops=2 * rows * model_dim * 7 * half,
                bytes_accessed=12 * 2**20,
                transcendentals=rows * half,
            ),
        )(*operands)

    flag = is_inner.astype(jnp.int32)[None]
    block = 2 * tok_dev

    def stack(inputs, *layouts):
        def size(part):
            return part[0][2] if isinstance(part[0], tuple) else part[2]

        return pl.pallas_call(
            functools.partial(stack_kernel, count=len(inputs), layouts=layouts),
            in_specs=[pl.BlockSpec(memory_space=pltpu.SMEM)] + [inside] * len(inputs),
            out_specs=[inside] * len(layouts),
            out_shape=[
                jax.ShapeDtypeStruct((sum(map(size, parts)), wide), jnp.bfloat16)
                for parts in layouts
            ],
            compiler_params=pltpu.CompilerParams(vmem_limit_bytes=2 * 2**20),
        )(flag, *inputs)

    def rows_of(n, first=0, count=1):
        return (n, first * block, count * block)

    order = (Z_NEAR ^ Z_FAR, X ^ Y, X, Y, Z_NEAR)
    middle, across, beside_x, beside_y, near = (swap(own, m) for m in order)

    through, outward, pair = stack(
        [near, middle, across],
        [rows_of(0), rows_of(2)],
        [rows_of(1), rows_of(2)],
        [rows_of(0), rows_of(1)],
    )
    through = swap(through, Z_NEAR ^ Z_FAR, inner)
    outward = swap(outward, Z_NEAR)
    pair_x, pair_y = swap(pair, X), swap(after(pair, beside_x, beside_y), Y)

    (held,) = stack([after(own, pair)], [rows_of(0)])
    through, held = tied([through, held])

    beyond, far_x, far_y, far, relayed = stack(
        [through, outward, middle],
        [(rows_of(0), rows_of(2))],
        *[[(rows_of(0), rows_of(1))]] * 3,
        [rows_of(0, 1)],
    )
    third = [swap(beyond, X ^ Y), swap(far_x, X), swap(far_y, Y), swap(relayed, Z_NEAR, inner)]
    (stack_a,) = stack(
        [held, beside_x, beside_y, across, pair, pair_x, pair_y, far, outward],
        [rows_of(n) for n in range(4)]
        + [rows_of(n, 0, 2) for n in range(4, 7)]
        + [rows_of(7), rows_of(8, 1)],
    )
    total = call(early_kernel, stack_a, swap(stack_a, CORE), (), inside, [], 14)
    *third, total = tied([*third, total])

    (stack_b,) = stack(
        [*third, through],
        [rows_of(0), rows_of(1), rows_of(2), (rows_of(4, 1), rows_of(3))],
    )
    scratch = [
        pltpu.VMEM((2 * half, model_dim), jnp.float32),
        pltpu.SemaphoreType.DMA((model_dim // COLUMNS,)),
    ]
    outside = pl.BlockSpec(memory_space=pl.ANY)
    out = call(last_kernel, stack_b, swap(stack_b, CORE), (total,), outside, scratch, 11)
    return out.reshape(1, 2, half, model_dim)


def local(tokens, cotangent, routes, combine, w_in, w_out, v_in):
    experts = lax.axis_size("expert") * w_in.shape[0]
    tok_dev, top_k = routes.shape
    sizes = (lax.axis_size("dp"), lax.axis_size("expert"))
    if sizes == (2, 16) and w_in.shape[0] == 1 and 2 * tok_dev * top_k // experts >= tok_dev:
        return dense(tokens, cotangent, routes, combine, w_in, w_out, v_in)
    return dispatched(tokens, cotangent, routes, combine, w_in, w_out, v_in)


def solution(mesh):
    in_specs = (
        P(("dp", "expert"), None),
        P(("dp", "expert"), None),
        P(("dp", "expert"), None),
        P(("dp", "expert"), None),
        P("expert", None, "dp", None),
        P("expert", "dp", None),
        P("expert", None, "dp", None),
    )
    out_specs = P("expert", None, "dp", None)
    return jax.shard_map(local, mesh=mesh, in_specs=in_specs, out_specs=out_specs, check_vma=False)
```

```python
import functools

import jax
import jax.numpy as jnp
from jax import lax
from jax.experimental import pallas as pl
from jax.experimental.pallas import tpu as pltpu
from jax.sharding import PartitionSpec as P

NT = (((1,), (1,)), ((), ()))
NN = (((1,), (0,)), ((), ()))


def expert_terms(slot_rows, slot_grads, w_pair, v_pair, w_down):
    hidden_width = w_pair.shape[1]
    model_dim = w_pair.shape[2]
    stacked = jnp.concatenate([w_pair, v_pair], axis=0).reshape(4 * hidden_width, model_dim)
    projected = lax.dot_general(slot_rows, stacked, NT, preferred_element_type=jnp.float32)
    pre_gate = projected[:, :hidden_width]
    pre_up = projected[:, hidden_width : 2 * hidden_width]
    tan_gate = projected[:, 2 * hidden_width : 3 * hidden_width]
    tan_up = projected[:, 3 * hidden_width :]
    back_grad = lax.dot_general(slot_grads, w_down, NT, preferred_element_type=jnp.float32)
    gate_dir, up_dir = directions(pre_gate, pre_up, tan_gate, tan_up, back_grad)
    gate_term = lax.dot_general(
        gate_dir, slot_rows, (((0,), (0,)), ((), ())), preferred_element_type=jnp.float32
    )
    up_term = lax.dot_general(
        up_dir, slot_rows, (((0,), (0,)), ((), ())), preferred_element_type=jnp.float32
    )
    return jnp.stack([gate_term, up_term], axis=0)


def directions(pre_gate, pre_up, tan_gate, tan_up, back_grad):
    gate_sig = jax.nn.sigmoid(pre_gate)
    first_deriv = gate_sig * (1.0 + pre_gate * (1.0 - gate_sig))
    second_deriv = gate_sig * (1.0 - gate_sig) * (2.0 + pre_gate * (1.0 - 2.0 * gate_sig))
    gate_dir = back_grad * (tan_up * first_deriv + pre_up * second_deriv * tan_gate)
    up_dir = back_grad * first_deriv * tan_gate
    return gate_dir.astype(jnp.bfloat16), up_dir.astype(jnp.bfloat16)


def dispatched(tokens, cotangent, routes, combine, w_in, w_out, v_in):
    n_expert = lax.axis_size("expert")
    exp_dev = w_in.shape[0]
    experts = n_expert * exp_dev
    tok_dev, top_k = routes.shape
    model_dim = tokens.shape[1]
    capacity = 2 * tok_dev * top_k // experts
    pair_count = tok_dev * top_k
    slot_count = n_expert * capacity
    flat_routes = routes.reshape(pair_count)
    onehot = (flat_routes[:, None] == jnp.arange(experts, dtype=jnp.int32)[None, :]).astype(
        jnp.int32
    )
    earlier = jnp.cumsum(onehot, axis=0) - onehot
    slot_rank = jnp.sum(earlier * onehot, axis=1)
    position = flat_routes * capacity + slot_rank
    slot_table = jnp.full((experts * capacity,), pair_count, jnp.int32)
    slot_table = slot_table.at[position].set(jnp.arange(pair_count, dtype=jnp.int32))
    token_index = slot_table // top_k
    padded_tokens = jnp.concatenate([tokens, jnp.zeros((1, model_dim), jnp.bfloat16)], axis=0)
    scaled = (combine[:, :, None] * cotangent[:, None, :].astype(jnp.float32)).astype(jnp.bfloat16)
    padded_scaled = jnp.concatenate(
        [scaled.reshape(pair_count, model_dim), jnp.zeros((1, model_dim), jnp.bfloat16)], axis=0
    )
    send_rows = padded_tokens[token_index].reshape(n_expert, exp_dev * capacity, model_dim)
    send_grads = padded_scaled[slot_table].reshape(n_expert, exp_dev * capacity, model_dim)
    recv_rows = lax.all_to_all(send_rows, "expert", split_axis=0, concat_axis=0, tiled=True)
    recv_grads = lax.all_to_all(send_grads, "expert", split_axis=0, concat_axis=0, tiled=True)

    def regroup(received):
        shaped = received.reshape(n_expert, exp_dev, capacity, model_dim)
        return jnp.transpose(shaped, (1, 0, 2, 3)).reshape(exp_dev, slot_count, model_dim)

    local_rows = regroup(recv_rows)
    local_grads = regroup(recv_grads)
    batched_terms = jax.vmap(expert_terms)
    pair_piece, probe_piece, down_piece = lax.all_gather(
        (w_in, v_in, w_out[:, None]), "dp", axis=2, tiled=True
    )
    partials = batched_terms(local_rows, local_grads, pair_piece, probe_piece, down_piece[:, 0])
    return lax.psum_scatter(
        partials.astype(jnp.bfloat16), "dp", scatter_dimension=2, tiled=True
    ).astype(jnp.float32)


CORE, X, Y = 1, 2, 16
Z_NEAR, Z_FAR = 4, 8
LANES = 128


def pack_kernel(
    tok_hbm, cot_hbm, route_hbm, comb_hbm, out_ref, route_ref, comb_ref, sems, *, experts
):
    tok_dev, model_dim = tok_hbm.shape
    tok_at = out_ref.at[pl.ds(0, tok_dev), pl.ds(0, model_dim)]
    cot_at = out_ref.at[pl.ds(tok_dev, tok_dev), pl.ds(0, model_dim)]
    moves = ((route_hbm, route_ref), (comb_hbm, comb_ref), (tok_hbm, tok_at), (cot_hbm, cot_at))
    copies = [pltpu.make_async_copy(*m, sems.at[n]) for n, m in enumerate(moves)]
    for copy in copies:
        copy.start()
    copies[0].wait()
    copies[1].wait()
    line = lax.broadcasted_iota(jnp.int32, (LANES, tok_dev), 0)
    weight = jnp.zeros((LANES, tok_dev), jnp.float32)
    for k in range(route_ref.shape[0]):
        named = route_ref[k : k + 1, :] == line % experts
        weight = jnp.where(named, comb_ref[k : k + 1, :], weight)
    high = weight.astype(jnp.bfloat16).astype(jnp.float32)
    middle = (weight - high).astype(jnp.bfloat16).astype(jnp.float32)
    low = weight - high - middle
    part = line // experts
    zero = jnp.zeros_like(weight)
    value = jnp.where(part == 0, high, jnp.where(part == 1, middle, jnp.where(part == 2, low, zero)))
    row = lax.broadcasted_iota(jnp.int32, (tok_dev, tok_dev), 0)
    column = lax.broadcasted_iota(jnp.int32, (tok_dev, tok_dev), 1)
    same = (row == column).astype(jnp.float32).astype(jnp.bfloat16)
    turned = lax.dot_general(
        same, value.astype(jnp.bfloat16), NT, preferred_element_type=jnp.float32
    )
    out_ref[0:tok_dev, model_dim:] = turned.astype(jnp.bfloat16)
    out_ref[tok_dev:, model_dim:] = jnp.zeros((tok_dev, LANES), jnp.bfloat16)
    copies[2].wait()
    copies[3].wait()


def stack_kernel(flag_ref, *refs, count, layouts):
    for out_ref, parts in zip(refs[count:], layouts):
        row = 0
        for part in parts:
            at = pl.ds(row, part[0][2] if isinstance(part[0], tuple) else part[2])
            if isinstance(part[0], tuple):
                for taken, (n, first, rows) in zip((1, 0), part):

                    @pl.when(flag_ref[0] == taken)
                    def _(n=n, first=first, rows=rows, at=at, out_ref=out_ref):
                        out_ref[at, :] = refs[n][first : first + rows]

            else:
                n, first, rows = part
                out_ref[at, :] = refs[n][first : first + rows]
            row += at.size


def unpack(pieces, x_ref, c_ref, wt_ref, tok_dev):
    model_dim = x_ref.shape[1]
    for row, (piece, first) in enumerate(pieces):
        at = pl.ds(row * tok_dev, tok_dev)
        x_ref[at, :] = piece[first : first + tok_dev, 0:model_dim]
        wt_ref[at, :] = piece[first : first + tok_dev, model_dim:]
        c_ref[at, :] = piece[first + tok_dev : first + 2 * tok_dev, 0:model_dim]


COLUMNS = 256
ROWS = 256


def rows_to_dirs(stacks, pick_ref, shards, x_ref, c_ref, wt_ref, dir_ref, tok_dev):
    w_ref, v_ref, wo_ref = shards
    half = wo_ref.shape[0]
    pieces = [(s, first) for s in stacks for first in range(0, s.shape[0], 2 * tok_dev)]
    for start in range(0, x_ref.shape[0], ROWS):
        part = pieces[start // tok_dev : (start + ROWS) // tok_dev]
        x_at = x_ref.at[pl.ds(start, ROWS)]
        unpack(part, x_at, c_ref, wt_ref, tok_dev)
        weight = lax.dot_general(
            pick_ref[...], wt_ref[...], NT, preferred_element_type=jnp.float32
        )
        both = jnp.concatenate([w_ref[...], v_ref[...]], axis=0)
        seen = lax.dot_general(both, x_at[...], NT, preferred_element_type=jnp.float32)
        back = lax.dot_general(wo_ref[...], c_ref[...], NT, preferred_element_type=jnp.float32)
        parts = [seen[n * half : (n + 1) * half] for n in range(4)]
        gate_dir, up_dir = directions(*parts, back * weight[0:1])
        dir_ref[0:half, start : start + ROWS] = gate_dir
        dir_ref[half:, start : start + ROWS] = up_dir


def early_kernel(
    mine, theirs, pick_ref, w, v, wo, sum_ref, x_ref, dir_ref, c_ref, wt_ref, *, tok_dev
):
    rows_to_dirs((mine, theirs), pick_ref, (w, v, wo), x_ref, c_ref, wt_ref, dir_ref, tok_dev)
    for n in range(sum_ref.shape[1] // COLUMNS):
        at = pl.ds(n * COLUMNS, COLUMNS)
        sum_ref[:, at] = lax.dot_general(
            dir_ref[...], x_ref[:, at], NN, preferred_element_type=jnp.float32
        )


def last_kernel(
    mine, theirs, pick_ref, w, v, wo, add_ref, out_ref, x_ref, dir_ref, c_ref, wt_ref, sum_ref, sems,
    *, tok_dev
):
    rows_to_dirs((mine, theirs), pick_ref, (w, v, wo), x_ref, c_ref, wt_ref, dir_ref, tok_dev)
    copies = []
    for n in range(out_ref.shape[1] // COLUMNS):
        at = pl.ds(n * COLUMNS, COLUMNS)
        total = lax.dot_general(
            dir_ref[...], x_ref[:, at], NN, preferred_element_type=jnp.float32
        )
        sum_ref[:, at] = total + add_ref[:, at]
        copy = pltpu.make_async_copy(sum_ref.at[:, at], out_ref.at[:, at], sems.at[n])
        copy.start()
        copies.append(copy)
    for copy in copies:
        copy.wait()


def swap(value, mask, sender=None):
    axes = ("dp", "expert")
    count = lax.axis_size("dp") * lax.axis_size("expert")
    pairs = [(i, i ^ mask) for i in range(count) if sender is None or sender(i)]
    return lax.ppermute(value, axes, pairs)


def inner(place):
    return (place & Z_NEAR) // Z_NEAR != (place & Z_FAR) // Z_FAR


def after(value, *others):
    return lax.optimization_barrier((value, *others))[0]


def tied(values, *others):
    return list(lax.optimization_barrier((*values, *others)))[: len(values)]


def dense(tokens, cotangent, routes, combine, w_in, w_out, v_in):
    experts = lax.axis_size("expert")
    tok_dev, model_dim = tokens.shape
    half = w_in.shape[2]
    wide = model_dim + LANES
    inside = pl.BlockSpec(memory_space=pltpu.VMEM)
    own = pl.pallas_call(
        functools.partial(pack_kernel, experts=experts),
        in_specs=[pl.BlockSpec(memory_space=pl.ANY)] * 4,
        out_specs=inside,
        out_shape=jax.ShapeDtypeStruct((2 * tok_dev, wide), jnp.bfloat16),
        scratch_shapes=[
            pltpu.VMEM(routes.shape[::-1], jnp.int32),
            pltpu.VMEM(combine.shape[::-1], jnp.float32),
            pltpu.SemaphoreType.DMA((4,)),
        ],
        compiler_params=pltpu.CompilerParams(vmem_limit_bytes=63_120_000),
    )(tokens, cotangent, routes.T, combine.T)

    lane = jnp.arange(LANES, dtype=jnp.int32)[None, :]
    expert = lax.axis_index("expert")
    pick = ((lane % experts == expert) & (lane < 3 * experts)).astype(jnp.bfloat16)
    pick = jnp.broadcast_to(pick, (16, LANES))
    is_inner = inner(expert)
    shards = (
        w_in.reshape(2 * half, model_dim),
        v_in.reshape(2 * half, model_dim),
        w_out.reshape(half, model_dim),
    )

    def call(kernel, stack, theirs, more, out_spec, scratch, limit):
        rows = stack.shape[0]
        operands = (stack, theirs, pick, *shards, *more)
        return pl.pallas_call(
            functools.partial(kernel, tok_dev=tok_dev),
            in_specs=[inside] * len(operands),
            out_specs=out_spec,
            out_shape=jax.ShapeDtypeStruct((2 * half, model_dim), jnp.float32),
            scratch_shapes=[
                pltpu.VMEM((rows, model_dim), jnp.bfloat16),
                pltpu.VMEM((2 * half, rows), jnp.bfloat16),
                pltpu.VMEM((ROWS, model_dim), jnp.bfloat16),
                pltpu.VMEM((ROWS, LANES), jnp.bfloat16),
            ]
            + scratch,
            compiler_params=pltpu.CompilerParams(vmem_limit_bytes=limit * 2**20),
            cost_estimate=pl.CostEstimate(
                flops=2 * rows * model_dim * 7 * half,
                bytes_accessed=12 * 2**20,
                transcendentals=rows * half,
            ),
        )(*operands)

    flag = is_inner.astype(jnp.int32)[None]
    block = 2 * tok_dev

    def stack(inputs, *layouts):
        def size(part):
            return part[0][2] if isinstance(part[0], tuple) else part[2]

        return pl.pallas_call(
            functools.partial(stack_kernel, count=len(inputs), layouts=layouts),
            in_specs=[pl.BlockSpec(memory_space=pltpu.SMEM)] + [inside] * len(inputs),
            out_specs=[inside] * len(layouts),
            out_shape=[
                jax.ShapeDtypeStruct((sum(map(size, parts)), wide), jnp.bfloat16)
                for parts in layouts
            ],
            compiler_params=pltpu.CompilerParams(vmem_limit_bytes=2 * 2**20),
        )(flag, *inputs)

    def rows_of(n, first=0, count=1):
        return (n, first * block, count * block)

    order = (Z_NEAR ^ Z_FAR, X ^ Y, X, Y, Z_NEAR)
    middle, across, beside_x, beside_y, near = (swap(own, m) for m in order)

    through, outward, pair = stack(
        [near, middle, across],
        [rows_of(0), rows_of(2)],
        [rows_of(1), rows_of(2)],
        [rows_of(0), rows_of(1)],
    )
    through = swap(through, Z_NEAR ^ Z_FAR, inner)
    outward = swap(outward, Z_NEAR)
    pair_x, pair_y = swap(pair, X), swap(after(pair, beside_x, beside_y), Y)

    (held,) = stack([after(own, pair)], [rows_of(0)])
    through, held = tied([through, held])

    beyond, far, relayed = stack(
        [through, outward, middle],
        [(rows_of(0), rows_of(2))],
        [(rows_of(0), rows_of(1))],
        [rows_of(0, 1)],
    )
    third = [swap(beyond, X ^ Y), swap(far, X), swap(far, Y), swap(relayed, Z_NEAR, inner)]
    (stack_a,) = stack(
        [held, beside_x, beside_y, across, pair, pair_x, pair_y, far, outward],
        [rows_of(n) for n in range(4)]
        + [rows_of(n, 0, 2) for n in range(4, 7)]
        + [rows_of(7), rows_of(8, 1)],
    )
    total = call(early_kernel, stack_a, swap(stack_a, CORE), (), inside, [], 14)
    *third, total = tied([*third, total])

    (stack_b,) = stack(
        [*third, through],
        [rows_of(0), rows_of(1), rows_of(2), (rows_of(4, 1), rows_of(3))],
    )
    scratch = [
        pltpu.VMEM((2 * half, model_dim), jnp.float32),
        pltpu.SemaphoreType.DMA((model_dim // COLUMNS,)),
    ]
    outside = pl.BlockSpec(memory_space=pl.ANY)
    out = call(last_kernel, stack_b, swap(stack_b, CORE), (total,), outside, scratch, 11)
    return out.reshape(1, 2, half, model_dim)


def local(tokens, cotangent, routes, combine, w_in, w_out, v_in):
    experts = lax.axis_size("expert") * w_in.shape[0]
    tok_dev, top_k = routes.shape
    sizes = (lax.axis_size("dp"), lax.axis_size("expert"))
    if sizes == (2, 16) and w_in.shape[0] == 1 and 2 * tok_dev * top_k // experts >= tok_dev:
        return dense(tokens, cotangent, routes, combine, w_in, w_out, v_in)
    return dispatched(tokens, cotangent, routes, combine, w_in, w_out, v_in)


def solution(mesh):
    in_specs = (
        P(("dp", "expert"), None),
        P(("dp", "expert"), None),
        P(("dp", "expert"), None),
        P(("dp", "expert"), None),
        P("expert", None, "dp", None),
        P("expert", "dp", None),
        P("expert", None, "dp", None),
    )
    out_specs = P("expert", None, "dp", None)
    return jax.shard_map(local, mesh=mesh, in_specs=in_specs, out_specs=out_specs, check_vma=False)
```
